32 devices in a mesh: left: 4 (over z), right: 4 (over y, x), occ: 2 (over core).
Axes of the slice: x: 2, y: 2, z: 4, core: 2. Of those that a mesh axis runs over, the one named last changes fastest.
Arguments:
- chol: bfloat16 [16, 1024, 2048], P('right', 'occ', 'left'), may hold values from -0.125 to 0.125
- amps: bfloat16 [4, 4, 1024, 512], P('left', None, 'occ', 'right'), may hold values from -1.5 to 1.5
- listed: int32 [4, 4, 4, 4], replicated, may hold values 0 or 1
Outputs:
- residual: float32 [4, 4, 1024, 512], P('left', None, 'occ', 'right')
The draws below stay inside these ranges and needn't reach their ends.
All inputs are finite; a program needn't handle non-finite values.
Results may differ from the reference program's by a relative error of at most 0.0029.
Values may be sent and summed in bfloat16 or wider, within the bound.
No kernel may reach another device: no remote copies, remote signals or barrier semaphores. Data moves between devices by JAX's collectives and lax.ppermute only.
A program may use at most 192 MiB of HBM per device.

```python
import jax
import jax.numpy as jnp
from jax import lax

TV = 32
NTV = 4
NQ = 2048
NOP = 512
PAIR = 1024
NPT = 16


def place_ends(values, stream_key, smallest, top_value):
    longest = values.shape.index(max(values.shape))
    spots = []
    for shift in (0, 1):
        where = [jax.random.randint(jax.random.fold_in(stream_key, axis), (), 0, length) for axis, length in enumerate(values.shape)]
        where[longest] = (where[longest] + shift) % values.shape[longest]
        spots.append(tuple(where))
    return values.at[spots[0]].set(smallest).at[spots[1]].set(top_value)


def block_levels(rng, shape, shards, smallest, top_value):
    gain = 1.0
    for dim, shards_of in shards:
        heights = jax.random.uniform(jax.random.fold_in(jax.random.fold_in(rng, 6), dim), (shards_of,), jnp.float32, smallest / len(shards), top_value / len(shards))
        gain = gain * jnp.repeat(jnp.exp(heights), shape[dim] // shards_of).reshape((-1,) + (1,) * (len(shape) - 1 - dim))
    return gain


def noise(key, extent, deviation, most, pieces=(), kind=jnp.bfloat16):
    gain = block_levels(key, extent, pieces, -0.22, 0.18) if pieces else 1.0
    values = jax.random.normal(key, extent, jnp.float32) * deviation * gain
    return jnp.minimum(jnp.maximum(values, -most), most).astype(kind)


def setup_inputs(seed: int = 0) -> dict:
    key_list = jax.random.split(jax.random.key(seed), 4)
    chol = noise(key_list[0], (NPT, PAIR, NQ), NQ ** -0.5, 0.125, ((0, 4), (1, 2), (2, 4)))
    amps = noise(key_list[1], (NTV, NTV, PAIR, NOP), 0.25, 1.5, ((0, 4), (2, 2), (3, 4)))
    listed = place_ends((jax.random.randint(key_list[2], (NTV, NTV, NTV, NTV), 0, 4) < 3).astype(jnp.int32), jax.random.fold_in(key_list[2], 1), 0, 1)
    return {"chol": chol, "amps": amps, "listed": listed}


def reference(chol, amps, listed):
    tiles = chol.astype(jnp.float32).reshape(NTV, NTV, PAIR, NQ)
    amp_full = amps.astype(jnp.float32)
    live_all = listed.astype(jnp.float32)

    def one_block(block_index):
        a_tile = block_index // NTV
        b_tile = block_index % NTV

        def add_task(running, task_index):
            c_tile = task_index // NTV
            d_tile = task_index % NTV
            left_tile = tiles[a_tile, c_tile]
            right_tile = tiles[b_tile, d_tile]
            inner = jnp.dot(left_tile, right_tile.T, precision=lax.Precision.HIGHEST)
            inner = lax.optimization_barrier(inner.astype(jnp.bfloat16)).astype(jnp.float32)
            swapped = inner.reshape(TV, TV, TV, TV).transpose(0, 2, 1, 3).reshape(PAIR, PAIR)
            term = jnp.dot(swapped, amp_full[c_tile, d_tile], precision=lax.Precision.HIGHEST)
            return running + live_all[a_tile, c_tile, b_tile, d_tile] * term, None

        running, _ = lax.scan(add_task, jnp.zeros((PAIR, NOP), jnp.float32), jnp.arange(NTV * NTV).astype(jnp.int32))
        return running

    blocks = lax.map(one_block, jnp.arange(NTV * NTV).astype(jnp.int32))
    return blocks.reshape(NTV, NTV, PAIR, NOP)
```

```python
import functools

import jax
import jax.numpy as jnp
from jax import lax
from jax.experimental import pallas as pl
from jax.experimental.pallas import tpu as pltpu
from jax.sharding import PartitionSpec as P

TV = 32
NTV = 4
NOP = 512
PAIR = 1024
GROUPS = 4


def ladder_kernel(steps, half_ref, live_ref, *refs):
    lefts = [refs[s * NTV:(s + 1) * NTV] for s in range(steps)]
    rights = [refs[steps * NTV + 2 * s: steps * NTV + 2 * s + 2] for s in range(steps)]
    amp_ref, out_ref, ready = refs[steps * (NTV + 2):]
    d_tile = pl.program_id(0)
    rows, depth = lefts[0][0].shape
    a_count = rows // TV
    c_part = TV // GROUPS
    group_rows = rows // GROUPS
    wide = 2 * GROUPS * TV
    half_b = rows // (GROUPS * TV)
    lane_group = lax.broadcasted_iota(jnp.int32, (NTV * group_rows, wide), 1) // TV % GROUPS
    for half in range(2):
        first_b = (half_ref[0] if half == 0 else 1 - half_ref[0]) * half_b

        def column_block(p, _):
            products = []
            for j in range(GROUPS):
                total = None
                for s in range(steps):
                    left = jnp.concatenate(
                        [lefts[s][k][j * group_rows:(j + 1) * group_rows, :] for k in range(NTV)], axis=0
                    )
                    right_ref = rights[s][half]
                    right = jnp.concatenate(
                        [
                            right_ref[0, pl.ds(pl.multiple_of(p * wide + (g // GROUPS * GROUPS + (g + j) % GROUPS) * TV, TV), TV), :]
                            for g in range(2 * GROUPS)
                        ],
                        axis=0,
                    )
                    term = lax.dot_general(
                        left, right, (((1,), (1,)), ((), ())), preferred_element_type=jnp.float32
                    )
                    total = term if total is None else total + term
                products.append(total.astype(jnp.bfloat16))
            for k in range(GROUPS):
                mixed = products[k]
                for g in range(1, GROUPS):
                    mixed = jnp.where(lane_group == g, products[(k - g) % GROUPS], mixed)
                mixed = mixed.reshape(NTV, c_part, a_count, wide)
                for b in range(2):
                    for c in range(c_part):
                        ready[k, :, first_b + 2 * p + b, :, c * GROUPS * TV:(c + 1) * GROUPS * TV] = mixed[
                            :, c, :, b * GROUPS * TV:(b + 1) * GROUPS * TV
                        ]
            return 0

        lax.fori_loop(0, half_b // 2, column_block, 0)

    for k in range(GROUPS):
        amp = jnp.concatenate(
            [
                amp_ref[0, pl.ds((((k - g) % GROUPS) * c_part + c) * TV, TV), :]
                for c in range(c_part)
                for g in range(GROUPS)
            ],
            axis=0,
        )
        block_rows = 2 * half_b * a_count
        terms = jnp.dot(
            ready[k].reshape(NTV * block_rows, TV * TV), amp, preferred_element_type=jnp.float32
        ).reshape(NTV, block_rows, amp.shape[1])
        for t in range(NTV):
            term = terms[t] * live_ref[t, d_tile].astype(jnp.float32)

            @pl.when(d_tile == 0)
            def _():
                out_ref[t, k] = term

            @pl.when(d_tile != 0)
            def _():
                out_ref[t, k] += term


def ladder(half, live, lefts, rights, amps):
    steps = len(lefts)
    rows, depth = lefts[0][0].shape
    columns = amps.shape[2]
    a_count = rows // TV
    b_blocks = TV // GROUPS
    left_spec = pl.BlockSpec((rows, depth), lambda d: (0, 0), pipeline_mode=pl.Buffered(1))
    right_spec = pl.BlockSpec((1, rows, depth), lambda d: (d, 0, 0))
    result = (NTV, GROUPS, b_blocks * a_count, columns)
    flops = 2 * NTV * NTV * rows * 2 * rows * (steps * depth + columns)
    return pl.pallas_call(
        functools.partial(ladder_kernel, steps),
        grid=(NTV,),
        in_specs=[pl.BlockSpec(memory_space=pltpu.SMEM)] * 2
        + [left_spec] * (steps * NTV)
        + [right_spec] * (2 * steps)
        + [pl.BlockSpec((1, 2 * rows, columns), lambda d: (d, 0, 0))],
        out_specs=pl.BlockSpec(result, lambda d: (0, 0, 0, 0)),
        out_shape=jax.ShapeDtypeStruct(result, jnp.float32),
        scratch_shapes=[pltpu.VMEM((GROUPS, NTV, b_blocks, a_count, TV * TV), jnp.bfloat16)],
        compiler_params=pltpu.CompilerParams(vmem_limit_bytes=56 * 2**20),
        cost_estimate=pl.CostEstimate(flops=flops, bytes_accessed=32 * 2**20, transcendentals=0),
    )(half, live, *[x for step in lefts for x in step], *[x for step in rights for x in step], amps)


def partner(value, axis, size, flip):
    return lax.ppermute(value, axis, [(i, i ^ flip) for i in range(size)])


def shift(value, axis, size, step):
    return lax.ppermute(value, axis, [(i, (i + step) % size) for i in range(size)])


def on_square(chol, amps, listed):
    row_count, depth = chol.shape[1:]
    columns = amps.shape[3]
    a_count = row_count // TV
    left_index = lax.axis_index("left")
    right_index = lax.axis_index("right")
    occ_index = lax.axis_index("occ")
    amp_columns = lax.all_gather(amps[0], "right", axis=2, tiled=True)
    amp_all = lax.all_gather(amp_columns, "occ", axis=1, tiled=True)
    held = chol
    lefts, rights = [], []
    for step in range(NTV):
        later = shift(held, "left", NTV, 1) if step < NTV - 1 else None
        own = lax.dynamic_index_in_dim(held, left_index, 0, keepdims=False)
        own = own.reshape(a_count, TV, depth).transpose(1, 0, 2).reshape(row_count, depth)
        lefts.append([own] + [partner(own, "right", NTV, flip) for flip in range(1, NTV)])
        rights.append([held, partner(held, "occ", 2, 1)])
        held = later
    tiles = jnp.arange(NTV)
    own_c = lax.dynamic_index_in_dim(listed, left_index, 1, keepdims=False)
    live = lax.dynamic_index_in_dim(own_c, right_index, 1, keepdims=False)[tiles ^ right_index]
    partials = ladder(occ_index.reshape(1), live, lefts, rights, amp_all)
    summed = lax.dynamic_index_in_dim(partials, left_index ^ right_index, 0, keepdims=False)
    for step in range(1, NTV):
        target = (left_index + step) % NTV
        sent = lax.dynamic_index_in_dim(partials, target ^ right_index, 0, keepdims=False)
        summed = summed + shift(sent.astype(jnp.bfloat16), "left", NTV, step).astype(jnp.float32)
    pieces = []
    for flip in range(NTV):
        piece = lax.dynamic_slice_in_dim(summed, (right_index ^ flip) * columns, columns, 2)
        pieces.append(partner(piece, "right", NTV, flip) if flip else piece)
    result = jnp.stack(pieces)[tiles ^ right_index]
    result = result.reshape(NTV, GROUPS, TV // GROUPS, a_count, columns).transpose(0, 3, 2, 1, 4)
    return result.reshape(1, NTV, row_count, columns)


def broadcast(value, axis, source):
    kept = jnp.where(lax.axis_index(axis) == source, value, 0).astype(value.dtype)
    return lax.psum(kept, axis)


def on_device(sizes, chol, amps, listed):
    tile_count = chol.shape[0]
    if sizes == (NTV, NTV, 2) and tile_count == NTV:
        return on_square(chol, amps, listed)
    row_count = chol.shape[1]
    a_local = row_count // TV
    left_index = lax.axis_index("left")
    right_index = lax.axis_index("right")
    first_tile = right_index * tile_count
    full_vectors = lax.all_gather(chol, "left", axis=2, tiled=True)
    collected = []
    for a_tile in range(NTV):
        wanted = a_tile * NTV + left_index
        holder = wanted // tile_count
        holder_slot = wanted % tile_count
        offered = lax.dynamic_index_in_dim(full_vectors, holder_slot, 0, keepdims=False)
        collected.append(broadcast(offered, "right", holder))
    left_rows = jnp.stack(collected)
    own_c = lax.dynamic_index_in_dim(listed, left_index, 1, keepdims=False).reshape(NTV, NTV * NTV)
    live = lax.dynamic_slice_in_dim(own_c, first_tile, tile_count, 1).T.astype(jnp.float32)
    products = jnp.einsum(
        "xrq,tkq->txrk",
        left_rows,
        lax.all_gather(full_vectors, "occ", axis=1, tiled=True),
        preferred_element_type=jnp.float32,
    )
    inner = (products * live[:, :, None, None]).astype(jnp.bfloat16)
    swapped = inner.reshape(tile_count, NTV, a_local, TV, TV, TV).transpose(0, 1, 2, 4, 3, 5)
    swapped = swapped.reshape(tile_count, NTV * a_local * TV, PAIR)
    amp_columns = lax.all_gather(amps, "right", axis=3, tiled=True)
    d_first = first_tile % NTV
    own_amps = lax.dynamic_slice_in_dim(amp_columns[0], d_first, tile_count, 0)
    partial_sum = jnp.einsum(
        "trk,tkn->rn",
        swapped,
        lax.all_gather(own_amps, "occ", axis=1, tiled=True),
        preferred_element_type=jnp.float32,
    )
    partial_sum = partial_sum.reshape(NTV, row_count, NOP)
    owned_a = lax.psum_scatter(partial_sum, "left", scatter_dimension=0, tiled=True)
    b_tile = first_tile // NTV
    placed = lax.dynamic_update_slice_in_dim(
        jnp.zeros((NTV, row_count, NOP), jnp.float32), owned_a, b_tile, 0
    )
    summed = lax.psum_scatter(placed, "right", scatter_dimension=2, tiled=True)
    return summed.reshape(1, NTV, row_count, summed.shape[2])


def solution(mesh):
    placed = (P("right", "occ", "left"), P("left", None, "occ", "right"), P())
    return jax.shard_map(
        functools.partial(on_device, tuple(mesh.shape[axis] for axis in ("left", "right", "occ"))),
        mesh=mesh,
        in_specs=placed,
        out_specs=P("left", None, "occ", "right"),
        check_vma=False,
    )
```

```python
import functools

import jax
import jax.numpy as jnp
from jax import lax
from jax.experimental import pallas as pl
from jax.experimental.pallas import tpu as pltpu
from jax.sharding import PartitionSpec as P

TV = 32
NTV = 4
NOP = 512
PAIR = 1024
GROUPS = 4


def ladder_kernel(steps, half_ref, live_ref, *refs):
    lefts = [refs[s * NTV:(s + 1) * NTV] for s in range(steps)]
    rights = [refs[steps * NTV + 4 * s: steps * NTV + 4 * s + 4] for s in range(steps)]
    amp_ref, out_ref, ready = refs[steps * (NTV + 4):]
    d_tile = pl.program_id(0)
    rows, depth = lefts[0][0].shape
    a_count = rows // TV
    c_part = TV // GROUPS
    group_rows = rows // GROUPS
    wide = 2 * GROUPS * TV
    half_b = rows // (GROUPS * TV)
    lane_group = lax.broadcasted_iota(jnp.int32, (NTV * group_rows, wide), 1) // TV % GROUPS
    for half in range(2):
        first_b = (half_ref[0] if half == 0 else 1 - half_ref[0]) * half_b

        def column_block(p, _):
            products = []
            for j in range(GROUPS):
                total = None
                for s in range(steps):
                    left = jnp.concatenate(
                        [lefts[s][k][j * group_rows:(j + 1) * group_rows, :] for k in range(NTV)], axis=0
                    )
                    right = jnp.concatenate(
                        [
                            jnp.concatenate(
                                [
                                    part[0, pl.ds(pl.multiple_of(p * wide + (g // GROUPS * GROUPS + (g + j) % GROUPS) * TV, TV), TV), :]
                                    for g in range(2 * GROUPS)
                                ],
                                axis=0,
                            )
                            for part in rights[s][2 * half:2 * half + 2]
                        ],
                        axis=1,
                    )
                    term = lax.dot_general(
                        left, right, (((1,), (1,)), ((), ())), preferred_element_type=jnp.float32
                    )
                    total = term if total is None else total + term
                products.append(total.astype(jnp.bfloat16))
            for k in range(GROUPS):
                mixed = products[k]
                for g in range(1, GROUPS):
                    mixed = jnp.where(lane_group == g, products[(k - g) % GROUPS], mixed)
                mixed = mixed.reshape(NTV, c_part, a_count, wide)
                for b in range(2):
                    for c in range(c_part):
                        ready[k, :, first_b + 2 * p + b, :, c * GROUPS * TV:(c + 1) * GROUPS * TV] = mixed[
                            :, c, :, b * GROUPS * TV:(b + 1) * GROUPS * TV
                        ]
            return 0

        lax.fori_loop(0, half_b // 2, column_block, 0)

    for k in range(GROUPS):
        amp = jnp.concatenate(
            [
                amp_ref[0, pl.ds((((k - g) % GROUPS) * c_part + c) * TV, TV), :]
                for c in range(c_part)
                for g in range(GROUPS)
            ],
            axis=0,
        )
        block_rows = 2 * half_b * a_count
        terms = jnp.dot(
            ready[k].reshape(NTV * block_rows, TV * TV), amp, preferred_element_type=jnp.float32
        ).reshape(NTV, block_rows, amp.shape[1])
        for t in range(NTV):
            term = terms[t] * live_ref[t, d_tile].astype(jnp.float32)

            @pl.when(d_tile == 0)
            def _():
                out_ref[t, k] = term

            @pl.when(d_tile != 0)
            def _():
                out_ref[t, k] += term


def ladder(half, live, lefts, rights, amps):
    steps = len(lefts)
    rows, depth = lefts[0][0].shape
    columns = amps.shape[2]
    a_count = rows // TV
    b_blocks = TV // GROUPS
    left_spec = pl.BlockSpec((rows, depth), lambda d: (0, 0), pipeline_mode=pl.Buffered(1))
    right_spec = pl.BlockSpec((1, rows, depth // 2), lambda d: (d, 0, 0))
    result = (NTV, GROUPS, b_blocks * a_count, columns)
    flops = 2 * NTV * NTV * rows * 2 * rows * (steps * depth + columns)
    return pl.pallas_call(
        functools.partial(ladder_kernel, steps),
        grid=(NTV,),
        in_specs=[pl.BlockSpec(memory_space=pltpu.SMEM)] * 2
        + [left_spec] * (steps * NTV)
        + [right_spec] * (4 * steps)
        + [pl.BlockSpec((1, 2 * rows, columns), lambda d: (d, 0, 0))],
        out_specs=pl.BlockSpec(result, lambda d: (0, 0, 0, 0)),
        out_shape=jax.ShapeDtypeStruct(result, jnp.float32),
        scratch_shapes=[pltpu.VMEM((GROUPS, NTV, b_blocks, a_count, TV * TV), jnp.bfloat16)],
        compiler_params=pltpu.CompilerParams(vmem_limit_bytes=56 * 2**20),
        cost_estimate=pl.CostEstimate(flops=flops, bytes_accessed=32 * 2**20, transcendentals=0),
    )(half, live, *[x for step in lefts for x in step], *[x for step in rights for x in step], amps)


def partner(value, axis, size, flip):
    return lax.ppermute(value, axis, [(i, i ^ flip) for i in range(size)])


def shift(value, axis, size, step):
    return lax.ppermute(value, axis, [(i, (i + step) % size) for i in range(size)])


def on_square(chol, amps, listed):
    row_count, depth = chol.shape[1:]
    columns = amps.shape[3]
    a_count = row_count // TV
    left_index = lax.axis_index("left")
    right_index = lax.axis_index("right")
    occ_index = lax.axis_index("occ")
    amp_columns = lax.all_gather(amps[0], "right", axis=2, tiled=True)
    amp_all = lax.all_gather(amp_columns, "occ", axis=1, tiled=True)
    held = (chol[:, :, :depth // 2], chol[:, :, depth // 2:])
    lefts, rights = [], []
    for step in range(NTV):
        if step < NTV - 1:
            later = (shift(held[0], "left", NTV, 1), shift(held[1], "left", NTV, NTV - 1))
        own = jnp.concatenate(
            [lax.dynamic_index_in_dim(part, left_index, 0, keepdims=False) for part in held], axis=1
        )
        own = own.reshape(a_count, TV, depth).transpose(1, 0, 2).reshape(row_count, depth)
        lefts.append([own] + [partner(own, "right", NTV, flip) for flip in range(1, NTV)])
        rights.append([*held, *[partner(part, "occ", 2, 1) for part in held]])
        if step < NTV - 1:
            later, lefts[-1], rights[-1] = lax.optimization_barrier((later, lefts[-1], rights[-1]))
        held = later
    tiles = jnp.arange(NTV)
    own_c = lax.dynamic_index_in_dim(listed, left_index, 1, keepdims=False)
    live = lax.dynamic_index_in_dim(own_c, right_index, 1, keepdims=False)[tiles ^ right_index]
    partials = ladder(occ_index.reshape(1), live, lefts, rights, amp_all)
    summed = lax.dynamic_index_in_dim(partials, left_index ^ right_index, 0, keepdims=False)
    for step in range(1, NTV):
        target = (left_index + step) % NTV
        sent = lax.dynamic_index_in_dim(partials, target ^ right_index, 0, keepdims=False)
        summed = summed + shift(sent.astype(jnp.bfloat16), "left", NTV, step).astype(jnp.float32)
    pieces = []
    for flip in range(NTV):
        piece = lax.dynamic_slice_in_dim(summed, (right_index ^ flip) * columns, columns, 2)
        pieces.append(partner(piece, "right", NTV, flip) if flip else piece)
    result = jnp.stack(pieces)[tiles ^ right_index]
    result = result.reshape(NTV, GROUPS, TV // GROUPS, a_count, columns).transpose(0, 3, 2, 1, 4)
    return result.reshape(1, NTV, row_count, columns)


def broadcast(value, axis, source):
    kept = jnp.where(lax.axis_index(axis) == source, value, 0).astype(value.dtype)
    return lax.psum(kept, axis)


def on_device(sizes, chol, amps, listed):
    tile_count = chol.shape[0]
    if sizes == (NTV, NTV, 2) and tile_count == NTV:
        return on_square(chol, amps, listed)
    row_count = chol.shape[1]
    a_local = row_count // TV
    left_index = lax.axis_index("left")
    right_index = lax.axis_index("right")
    first_tile = right_index * tile_count
    full_vectors = lax.all_gather(chol, "left", axis=2, tiled=True)
    collected = []
    for a_tile in range(NTV):
        wanted = a_tile * NTV + left_index
        holder = wanted // tile_count
        holder_slot = wanted % tile_count
        offered = lax.dynamic_index_in_dim(full_vectors, holder_slot, 0, keepdims=False)
        collected.append(broadcast(offered, "right", holder))
    left_rows = jnp.stack(collected)
    own_c = lax.dynamic_index_in_dim(listed, left_index, 1, keepdims=False).reshape(NTV, NTV * NTV)
    live = lax.dynamic_slice_in_dim(own_c, first_tile, tile_count, 1).T.astype(jnp.float32)
    products = jnp.einsum(
        "xrq,tkq->txrk",
        left_rows,
        lax.all_gather(full_vectors, "occ", axis=1, tiled=True),
        preferred_element_type=jnp.float32,
    )
    inner = (products * live[:, :, None, None]).astype(jnp.bfloat16)
    swapped = inner.reshape(tile_count, NTV, a_local, TV, TV, TV).transpose(0, 1, 2, 4, 3, 5)
    swapped = swapped.reshape(tile_count, NTV * a_local * TV, PAIR)
    amp_columns = lax.all_gather(amps, "right", axis=3, tiled=True)
    d_first = first_tile % NTV
    own_amps = lax.dynamic_slice_in_dim(amp_columns[0], d_first, tile_count, 0)
    partial_sum = jnp.einsum(
        "trk,tkn->rn",
        swapped,
        lax.all_gather(own_amps, "occ", axis=1, tiled=True),
        preferred_element_type=jnp.float32,
    )
    partial_sum = partial_sum.reshape(NTV, row_count, NOP)
    owned_a = lax.psum_scatter(partial_sum, "left", scatter_dimension=0, tiled=True)
    b_tile = first_tile // NTV
    placed = lax.dynamic_update_slice_in_dim(
        jnp.zeros((NTV, row_count, NOP), jnp.float32), owned_a, b_tile, 0
    )
    summed = lax.psum_scatter(placed, "right", scatter_dimension=2, tiled=True)
    return summed.reshape(1, NTV, row_count, summed.shape[2])


def solution(mesh):
    placed = (P("right", "occ", "left"), P("left", None, "occ", "right"), P())
    return jax.shard_map(
        functools.partial(on_device, tuple(mesh.shape[axis] for axis in ("left", "right", "occ"))),
        mesh=mesh,
        in_specs=placed,
        out_specs=P("left", None, "occ", "right"),
        check_vma=False,
    )
```

```python
import functools

import jax
import jax.numpy as jnp
from jax import lax
from jax.experimental import pallas as pl
from jax.experimental.pallas import tpu as pltpu
from jax.sharding import PartitionSpec as P

TV = 32
NTV = 4
NOP = 512
PAIR = 1024
GROUPS = 4


def ladder_kernel(steps, first, half_ref, live_ref, *refs):
    lefts = [refs[s * NTV:(s + 1) * NTV] for s in range(steps)]
    rights = [refs[steps * NTV + 2 * s: steps * NTV + 2 * s + 2] for s in range(steps)]
    rest = refs[steps * (NTV + 2):]
    amp_ref = rest[0]
    before_ref = None if first else rest[1]
    out_ref, products, ready = rest[-3:]
    step = pl.program_id(0)
    group_rows = lefts[0][0].shape[0]
    c_part = TV // GROUPS
    a_count = group_rows // c_part
    wide = 2 * GROUPS * TV
    half_blocks = rights[0][0].shape[0] // wide

    @pl.when(step < GROUPS)
    def _():
        for half in range(2):
            start = (half_ref[0] if half == 0 else 1 - half_ref[0]) * half_blocks
            for p in range(half_blocks):
                total = None
                for s in range(steps):
                    left = jnp.concatenate([ref[...] for ref in lefts[s]], axis=0)
                    right = jnp.concatenate(
                        [
                            rights[s][half][
                                pl.ds(pl.multiple_of(p * wide + (g // GROUPS * GROUPS + (g + step) % GROUPS) * TV, TV), TV), :
                            ]
                            for g in range(2 * GROUPS)
                        ],
                        axis=0,
                    )
                    term = lax.dot_general(
                        left, right, (((1,), (1,)), ((), ())), preferred_element_type=jnp.float32
                    )
                    total = term if total is None else total + term
                products[step, start + p] = total.astype(jnp.bfloat16)

    @pl.when(step >= GROUPS)
    def _():
        k = step - GROUPS
        lane_group = lax.broadcasted_iota(jnp.int32, (NTV * group_rows, wide), 1) // TV % GROUPS
        for p in range(2 * half_blocks):
            mixed = products[k, p]
            for g in range(1, GROUPS):
                mixed = jnp.where(lane_group == g, products[(k + GROUPS - g) % GROUPS, p], mixed)
            mixed = mixed.reshape(NTV, c_part, a_count, wide)
            for b in range(2):
                for c in range(c_part):
                    ready[:, 2 * p + b, :, c * GROUPS * TV:(c + 1) * GROUPS * TV] = mixed[
                        :, c, :, b * GROUPS * TV:(b + 1) * GROUPS * TV
                    ]
        amp = jnp.concatenate(
            [
                amp_ref[pl.ds(pl.multiple_of(((k + GROUPS - g) % GROUPS * c_part + c) * TV, TV), TV), :]
                for c in range(c_part)
                for g in range(GROUPS)
            ],
            axis=0,
        )
        block_rows = TV // GROUPS * a_count
        terms = jnp.dot(
            ready[...].reshape(NTV * block_rows, TV * TV), amp, preferred_element_type=jnp.float32
        ).reshape(NTV, block_rows, amp.shape[1])
        for t in range(NTV):
            term = terms[t] * live_ref[t].astype(jnp.float32)
            out_ref[t, 0] = term if first else before_ref[t, 0] + term


def ladder(half, live, lefts, rights, amp, before):
    steps = len(lefts)
    rows, depth = lefts[0][0].shape
    columns = amp.shape[1]
    a_count = rows // TV
    b_blocks = TV // GROUPS
    wide = 2 * GROUPS * TV
    one = pl.Buffered(1)
    left_spec = pl.BlockSpec((rows // GROUPS, depth), lambda i: (jnp.minimum(i, GROUPS - 1), 0))
    right_spec = pl.BlockSpec((rows, depth), lambda i: (0, 0), pipeline_mode=one)
    amp_spec = pl.BlockSpec(amp.shape, lambda i: (0, 0), pipeline_mode=one)
    result = (NTV, GROUPS, b_blocks * a_count, columns)
    out_spec = pl.BlockSpec(
        (NTV, 1, b_blocks * a_count, columns), lambda i: (0, jnp.maximum(i - GROUPS, 0), 0, 0)
    )
    first = before is None
    flops = 2 * NTV * rows * 2 * rows * (steps * depth + columns)
    operands = [half, live, *[x for step in lefts for x in step], *[x for step in rights for x in step], amp]
    return pl.pallas_call(
        functools.partial(ladder_kernel, steps, first),
        grid=(2 * GROUPS,),
        in_specs=[pl.BlockSpec(memory_space=pltpu.SMEM)] * 2
        + [left_spec] * (steps * NTV)
        + [right_spec] * (2 * steps)
        + [amp_spec]
        + [out_spec] * (not first),
        out_specs=out_spec,
        out_shape=jax.ShapeDtypeStruct(result, jnp.float32),
        scratch_shapes=[
            pltpu.VMEM((GROUPS, 2 * rows // wide, NTV * rows // GROUPS, wide), jnp.bfloat16),
            pltpu.VMEM((NTV, b_blocks, a_count, TV * TV), jnp.bfloat16),
        ],
        input_output_aliases={} if first else {len(operands): 0},
        compiler_params=pltpu.CompilerParams(vmem_limit_bytes=40 * 2**20),
        cost_estimate=pl.CostEstimate(flops=flops, bytes_accessed=20 * 2**20, transcendentals=0),
    )(*operands, *([] if first else [before]))


def partner(value, axis, size, flip):
    return lax.ppermute(value, axis, [(i, i ^ flip) for i in range(size)])


def shift(value, axis, size, step):
    return lax.ppermute(value, axis, [(i, (i + step) % size) for i in range(size)])


def ring_order(size):
    return list(range(0, size, 2)) + list(range(size - 1, 0, -2))


HOPS = (
    (1, 2), (1, 1), (1, 0), (2, 1), (2, 0), (3, 0),
    (1, 3), (2, 3), (2, 2), (3, 2), (3, 1), (3, 3),
)
TURNS = {0: 4, 1: 6, 2: 8, 3: 10}


def on_square(chol, amps, listed):
    row_count, depth = chol.shape[1:]
    columns = amps.shape[3]
    a_count = row_count // TV
    left_index = lax.axis_index("left")
    right_index = lax.axis_index("right")
    occ_index = lax.axis_index("occ")
    order = ring_order(NTV)
    ring = [(order[p], order[(p + 1) % NTV]) for p in range(NTV)]
    near = [[order[(order.index(level) + i) % NTV] for i in range(NTV)] for level in range(NTV)]
    d_tiles = jnp.asarray(near, jnp.int32)[left_index]
    tiles = jnp.arange(NTV)
    own_c = lax.dynamic_index_in_dim(listed, left_index, 1, keepdims=False)
    live = lax.dynamic_index_in_dim(own_c, right_index, 1, keepdims=False)[tiles ^ right_index]
    amp_columns = lax.all_gather(amps[0], "right", axis=2, tiled=True)
    amp_all = lax.all_gather(amp_columns, "occ", axis=1, tiled=True)

    blocks = {(0, i): lax.dynamic_index_in_dim(chol, d_tiles[i], 0, keepdims=False) for i in range(NTV)}
    others, lefts = {}, {}

    def arrive(s, i):
        others[s, i] = partner(blocks[s, i], "occ", 2, 1)
        if i == 0:
            own = blocks[s, 0].reshape(a_count, TV, depth).transpose(1, 0, 2).reshape(row_count, depth)
            lefts[s] = [own] + [partner(own, "right", NTV, flip) for flip in range(1, NTV)]

    def contract(i, before):
        return ladder(
            occ_index.reshape(1),
            lax.dynamic_index_in_dim(live, d_tiles[i], 1, keepdims=False),
            [lefts[s] for s in range(NTV)],
            [(blocks[s, i], others[s, i]) for s in range(NTV)],
            lax.dynamic_index_in_dim(amp_all, d_tiles[i], 0, keepdims=False),
            before,
        )

    for i in range(NTV):
        arrive(0, i)
    partials = None
    for turn, (s, i) in enumerate(HOPS):
        sent = blocks[s - 1, (i + 1) % NTV]
        if turn >= 2:
            back = HOPS[turn - 2]
            sent, blocks[back] = lax.optimization_barrier((sent, blocks[back]))
            arrive(*back)
        if turn >= 4:
            back = HOPS[turn - 4]
            sent, others[back] = lax.optimization_barrier((sent, others[back]))
        for t in range(NTV):
            if TURNS[t] == turn:
                sent, lefts[t] = lax.optimization_barrier((sent, lefts[t]))
        if turn == len(HOPS) - 1:
            partials = contract(0, None)
            sent, partials = lax.optimization_barrier((sent, partials))
        blocks[s, i] = lax.ppermute(sent, "left", ring)
    for hop in HOPS[-2:]:
        arrive(*hop)
    for i in (2, 1, 3):
        partials = contract(i, partials)
    summed = lax.dynamic_index_in_dim(partials, left_index ^ right_index, 0, keepdims=False)
    for step in range(1, NTV):
        target = (left_index + step) % NTV
        sent = lax.dynamic_index_in_dim(partials, target ^ right_index, 0, keepdims=False)
        summed = summed + shift(sent.astype(jnp.bfloat16), "left", NTV, step).astype(jnp.float32)
    pieces = []
    for flip in range(NTV):
        piece = lax.dynamic_slice_in_dim(summed, (right_index ^ flip) * columns, columns, 2)
        pieces.append(partner(piece, "right", NTV, flip) if flip else piece)
    result = jnp.stack(pieces)[tiles ^ right_index]
    result = result.reshape(NTV, GROUPS, TV // GROUPS, a_count, columns).transpose(0, 3, 2, 1, 4)
    return result.reshape(1, NTV, row_count, columns)


def broadcast(value, axis, source):
    kept = jnp.where(lax.axis_index(axis) == source, value, 0).astype(value.dtype)
    return lax.psum(kept, axis)


def on_device(sizes, chol, amps, listed):
    tile_count = chol.shape[0]
    if sizes == (NTV, NTV, 2) and tile_count == NTV:
        return on_square(chol, amps, listed)
    row_count = chol.shape[1]
    a_local = row_count // TV
    left_index = lax.axis_index("left")
    right_index = lax.axis_index("right")
    first_tile = right_index * tile_count
    full_vectors = lax.all_gather(chol, "left", axis=2, tiled=True)
    collected = []
    for a_tile in range(NTV):
        wanted = a_tile * NTV + left_index
        holder = wanted // tile_count
        holder_slot = wanted % tile_count
        offered = lax.dynamic_index_in_dim(full_vectors, holder_slot, 0, keepdims=False)
        collected.append(broadcast(offered, "right", holder))
    left_rows = jnp.stack(collected)
    own_c = lax.dynamic_index_in_dim(listed, left_index, 1, keepdims=False).reshape(NTV, NTV * NTV)
    live = lax.dynamic_slice_in_dim(own_c, first_tile, tile_count, 1).T.astype(jnp.float32)
    products = jnp.einsum(
        "xrq,tkq->txrk",
        left_rows,
        lax.all_gather(full_vectors, "occ", axis=1, tiled=True),
        preferred_element_type=jnp.float32,
    )
    inner = (products * live[:, :, None, None]).astype(jnp.bfloat16)
    swapped = inner.reshape(tile_count, NTV, a_local, TV, TV, TV).transpose(0, 1, 2, 4, 3, 5)
    swapped = swapped.reshape(tile_count, NTV * a_local * TV, PAIR)
    amp_columns = lax.all_gather(amps, "right", axis=3, tiled=True)
    d_first = first_tile % NTV
    own_amps = lax.dynamic_slice_in_dim(amp_columns[0], d_first, tile_count, 0)
    partial_sum = jnp.einsum(
        "trk,tkn->rn",
        swapped,
        lax.all_gather(own_amps, "occ", axis=1, tiled=True),
        preferred_element_type=jnp.float32,
    )
    partial_sum = partial_sum.reshape(NTV, row_count, NOP)
    owned_a = lax.psum_scatter(partial_sum, "left", scatter_dimension=0, tiled=True)
    b_tile = first_tile // NTV
    placed = lax.dynamic_update_slice_in_dim(
        jnp.zeros((NTV, row_count, NOP), jnp.float32), owned_a, b_tile, 0
    )
    summed = lax.psum_scatter(placed, "right", scatter_dimension=2, tiled=True)
    return summed.reshape(1, NTV, row_count, summed.shape[2])


def solution(mesh):
    placed = (P("right", "occ", "left"), P("left", None, "occ", "right"), P())
    return jax.shard_map(
        functools.partial(on_device, tuple(mesh.shape[axis] for axis in ("left", "right", "occ"))),
        mesh=mesh,
        in_specs=placed,
        out_specs=P("left", None, "occ", "right"),
        check_vma=False,
    )
```

```python
import functools

import jax
import jax.numpy as jnp
from jax import lax
from jax.experimental import pallas as pl
from jax.experimental.pallas import tpu as pltpu
from jax.sharding import PartitionSpec as P

TV = 32
NTV = 4
NOP = 512
PAIR = 1024
GROUPS = 4


def ladder_kernel(steps, count, first, half_ref, live_ref, pick_ref, *refs):
    lefts = [refs[s * count:(s + 1) * count] for s in range(steps)]
    rights = [refs[steps * count + 2 * s: steps * count + 2 * s + 2] for s in range(steps)]
    rest = refs[steps * (count + 2):]
    amp_ref = rest[0]
    before_ref = None if first else rest[1]
    out_ref, products, ready = rest[-3:]
    step = pl.program_id(0)
    group_rows = lefts[0][0].shape[1]
    c_part = TV // GROUPS
    a_count = group_rows // c_part
    wide = 2 * GROUPS * TV
    half_blocks = rights[0][0].shape[0] // wide

    @pl.when(step < GROUPS)
    def _():
        for half in range(2):
            start = (half_ref[0] if half == 0 else 1 - half_ref[0]) * half_blocks
            for p in range(half_blocks):
                total = None
                for s in range(steps):
                    left = jnp.concatenate([ref[0] for ref in lefts[s]], axis=0)
                    right = jnp.concatenate(
                        [
                            rights[s][half][
                                pl.ds(pl.multiple_of(p * wide + (g // GROUPS * GROUPS + (g + step) % GROUPS) * TV, TV), TV), :
                            ]
                            for g in range(2 * GROUPS)
                        ],
                        axis=0,
                    )
                    term = lax.dot_general(
                        left, right, (((1,), (1,)), ((), ())), preferred_element_type=jnp.float32
                    )
                    total = term if total is None else total + term
                products[step, start + p] = total.astype(jnp.bfloat16)

    @pl.when(step >= GROUPS)
    def _():
        k = step - GROUPS
        lane_group = lax.broadcasted_iota(jnp.int32, (count * group_rows, wide), 1) // TV % GROUPS
        for p in range(2 * half_blocks):
            mixed = products[k, p]
            for g in range(1, GROUPS):
                mixed = jnp.where(lane_group == g, products[(k + GROUPS - g) % GROUPS, p], mixed)
            mixed = mixed.reshape(count, c_part, a_count, wide)
            for b in range(2):
                for c in range(c_part):
                    ready[:, 2 * p + b, :, c * GROUPS * TV:(c + 1) * GROUPS * TV] = mixed[
                        :, c, :, b * GROUPS * TV:(b + 1) * GROUPS * TV
                    ]
        amp = jnp.concatenate(
            [
                amp_ref[pl.ds(pl.multiple_of(((k + GROUPS - g) % GROUPS * c_part + c) * TV, TV), TV), :]
                for c in range(c_part)
                for g in range(GROUPS)
            ],
            axis=0,
        )
        block_rows = TV // GROUPS * a_count
        terms = jnp.dot(
            ready[...].reshape(count * block_rows, TV * TV), amp, preferred_element_type=jnp.float32
        ).reshape(count, block_rows, amp.shape[1])
        for t in range(count):
            term = terms[t] * live_ref[t].astype(jnp.float32)
            if not first:
                term = before_ref[t, 0] + term
            out_ref[t, 0] = term.astype(out_ref.dtype)


def ladder(half, live, pick, lefts, rights, amp, before, part=None, kind=jnp.float32):
    steps = len(lefts)
    rows, depth = lefts[0].shape[1:]
    columns = amp.shape[1]
    a_count = rows // TV
    b_blocks = TV // GROUPS
    wide = 2 * GROUPS * TV
    count = NTV if part is None else NTV // 2
    base = 0 if part is None else part * count
    one = pl.Buffered(1)

    def left_spec(t):
        return pl.BlockSpec(
            (1, rows // GROUPS, depth), lambda i, h, v, k: (k[t], jnp.minimum(i, GROUPS - 1), 0)
        )

    right_spec = pl.BlockSpec((rows, depth), lambda i, h, v, k: (0, 0), pipeline_mode=one)
    amp_spec = pl.BlockSpec(amp.shape, lambda i, h, v, k: (0, 0), pipeline_mode=one)

    def sum_spec(place):
        return pl.BlockSpec(
            (count, 1, b_blocks * a_count, columns),
            lambda i, h, v, k: (place, jnp.maximum(i - GROUPS, 0), 0, 0),
        )

    first = before is None
    flops = 2 * count * rows * 2 * rows * (steps * depth + columns)
    operands = [half, live[base:base + count], pick[base:base + count]]
    operands += [x for x in lefts for _ in range(count)] + [x for step in rights for x in step] + [amp]
    return pl.pallas_call(
        functools.partial(ladder_kernel, steps, count, first),
        grid_spec=pltpu.PrefetchScalarGridSpec(
            num_scalar_prefetch=3,
            grid=(2 * GROUPS,),
            in_specs=[left_spec(t) for _ in lefts for t in range(count)]
            + [right_spec] * (2 * steps)
            + [amp_spec]
            + [sum_spec(base // count)] * (not first),
            out_specs=sum_spec(0),
            scratch_shapes=[
                pltpu.VMEM((GROUPS, 2 * rows // wide, count * rows // GROUPS, wide), jnp.bfloat16),
                pltpu.VMEM((count, b_blocks, a_count, TV * TV), jnp.bfloat16),
            ],
        ),
        out_shape=jax.ShapeDtypeStruct((count, GROUPS, b_blocks * a_count, columns), kind),
        input_output_aliases={} if first or part is not None else {len(operands): 0},
        compiler_params=pltpu.CompilerParams(vmem_limit_bytes=40 * 2**20),
        cost_estimate=pl.CostEstimate(flops=flops, bytes_accessed=20 * 2**20, transcendentals=0),
    )(*operands, *([] if first else [before]))


def partner(value, axis, size, flip):
    return lax.ppermute(value, axis, [(i, i ^ flip) for i in range(size)])


def shift(value, axis, size, step):
    return lax.ppermute(value, axis, [(i, (i + step) % size) for i in range(size)])


def ring_order(size):
    return list(range(0, size, 2)) + list(range(size - 1, 0, -2))


HOPS = (
    (1, 2), (1, 1), (1, 0), (2, 1), (2, 0), (3, 0),
    (1, 3), (2, 3), (2, 2), (3, 2), (3, 1), (3, 3),
)
NEAR = {0: (0,), 3: (1,), 5: (2,), 6: (3,)}
FAR = {1: (0,), 4: (1,), 6: (2,), 8: (3,)}
NEAR_DONE = {1: (0,), 4: (1,), 6: (2,), 8: (3,)}
FAR_DONE = {2: (0,), 5: (1,), 8: (2,), 9: (3,)}
OTHER = {
    0: ((0, 0),), 1: ((0, 1), (1, 2)), 2: ((0, 2), (1, 1)), 3: ((0, 3),), 4: ((1, 0), (2, 1)), 5: ((2, 0),),
    7: ((3, 0), (1, 3)), 8: ((2, 3),), 9: ((2, 2),), 10: ((3, 2),), 11: ((3, 1),), 12: ((3, 3),),
}
AMP_RIGHT, AMP_OCC = 2, 7


def on_square(chol, amps, listed):
    row_count, depth = chol.shape[1:]
    columns = amps.shape[3]
    a_count = row_count // TV
    left_index = lax.axis_index("left")
    right_index = lax.axis_index("right")
    occ_index = lax.axis_index("occ")
    order = ring_order(NTV)
    ring = [(order[p], order[(p + 1) % NTV]) for p in range(NTV)]
    near = [[order[(order.index(level) + i) % NTV] for i in range(NTV)] for level in range(NTV)]
    d_tiles = jnp.asarray(near, jnp.int32)[left_index]
    tiles = jnp.arange(NTV)
    targets = (left_index + 1 + tiles) % NTV
    pick = (targets ^ right_index).astype(jnp.int32)
    own_c = lax.dynamic_index_in_dim(listed, left_index, 1, keepdims=False)
    live = lax.dynamic_index_in_dim(own_c, right_index, 1, keepdims=False)[targets]
    half = occ_index.reshape(1)

    held = {("block", 0, i): lax.dynamic_index_in_dim(chol, d_tiles[i], 0, keepdims=False) for i in range(NTV)}
    held["amp"] = amps[0]
    waiting = []

    def meet(keys):
        keys = list(dict.fromkeys(keys))
        for key, value in zip(keys, lax.optimization_barrier([held[key] for key in keys])):
            held[key] = value

    def own_left(s):
        own = held["block", s, 0].reshape(a_count, TV, depth)
        held["left", s, 0] = own.transpose(1, 0, 2).reshape(row_count, depth)

    def contract(i, before, part=None, kind=jnp.float32):
        return ladder(
            half,
            lax.dynamic_index_in_dim(live, d_tiles[i], 1, keepdims=False),
            pick,
            [held["lefts", s] for s in range(NTV)],
            [(held["block", s, i], held["other", s, i]) for s in range(NTV)],
            lax.dynamic_index_in_dim(held["amp"], d_tiles[i], 0, keepdims=False),
            before,
            part,
            kind,
        )

    last = len(HOPS)
    for slot in range(last + 1):
        hops = [0, 1] if slot == 0 else [slot + 1] if slot + 1 < last else []
        if slot == AMP_OCC:
            waiting.append("amp")
        if slot >= 1:
            waiting.append(("block", *HOPS[slot - 1]))
            waiting += [("left", s, flip) for s in NEAR_DONE.get(slot, ()) for flip in (1, 2)]
            waiting += [("left", s, 3) for s in FAR_DONE.get(slot, ())]
        for s in NEAR.get(slot, ()):
            own_left(s)
        starting = [("block", HOPS[u][0] - 1, (HOPS[u][1] + 1) % NTV) for u in hops]
        starting += [("left", s, 0) for s in NEAR.get(slot, ()) + FAR.get(slot, ())]
        starting += [("block", *unit) for unit in OTHER.get(slot, ())]
        starting += ["amp"] * (slot in (AMP_RIGHT, AMP_OCC))
        meet(waiting + starting)
        waiting = []
        for u in hops:
            s, i = HOPS[u]
            held["block", s, i] = lax.ppermute(held["block", s - 1, (i + 1) % NTV], "left", ring)
        for s in NEAR.get(slot, ()):
            for flip in (1, 2):
                held["left", s, flip] = partner(held["left", s, 0], "right", NTV, flip)
        for s in FAR.get(slot, ()):
            held["left", s, 3] = partner(held["left", s, 0], "right", NTV, 3)
        for s in FAR_DONE.get(slot, ()):
            held["lefts", s] = jnp.stack([held["left", s, flip] for flip in range(NTV)])
        for unit in OTHER.get(slot, ()):
            held["other", *unit] = partner(held["block", *unit], "occ", 2, 1)
            waiting.append(("other", *unit))
        if slot == AMP_RIGHT:
            held["amp"] = lax.all_gather(held["amp"], "right", axis=2, tiled=True)
        if slot == AMP_OCC:
            held["amp"] = lax.all_gather(held["amp"], "occ", axis=1, tiled=True)
        if slot == last - 3:
            held["sum"] = contract(0, None)
            waiting.append("sum")
        if slot == last - 1:
            held["sum"] = contract(2, held["sum"])
            waiting.append("sum")
    partials = contract(1, held["sum"])
    early = contract(3, partials, 0, jnp.bfloat16)
    moved = [shift(early[t], "left", NTV, t + 1) for t in range(NTV // 2)]
    late = contract(3, partials, 1)
    moved += [
        shift(late[t].astype(jnp.bfloat16), "left", NTV, NTV // 2 + t + 1) for t in range(NTV // 2 - 1)
    ]
    summed = late[NTV // 2 - 1]
    for piece in moved:
        summed = summed + piece.astype(jnp.float32)
    pieces = []
    for flip in range(NTV):
        piece = lax.dynamic_slice_in_dim(summed, (right_index ^ flip) * columns, columns, 2)
        pieces.append(partner(piece, "right", NTV, flip) if flip else piece)
    result = jnp.stack(pieces)[tiles ^ right_index]
    result = result.reshape(NTV, GROUPS, TV // GROUPS, a_count, columns).transpose(0, 3, 2, 1, 4)
    return result.reshape(1, NTV, row_count, columns)


def broadcast(value, axis, source):
    kept = jnp.where(lax.axis_index(axis) == source, value, 0).astype(value.dtype)
    return lax.psum(kept, axis)


def on_device(sizes, chol, amps, listed):
    tile_count = chol.shape[0]
    if sizes == (NTV, NTV, 2) and tile_count == NTV:
        return on_square(chol, amps, listed)
    row_count = chol.shape[1]
    a_local = row_count // TV
    left_index = lax.axis_index("left")
    right_index = lax.axis_index("right")
    first_tile = right_index * tile_count
    full_vectors = lax.all_gather(chol, "left", axis=2, tiled=True)
    collected = []
    for a_tile in range(NTV):
        wanted = a_tile * NTV + left_index
        holder = wanted // tile_count
        holder_slot = wanted % tile_count
        offered = lax.dynamic_index_in_dim(full_vectors, holder_slot, 0, keepdims=False)
        collected.append(broadcast(offered, "right", holder))
    left_rows = jnp.stack(collected)
    own_c = lax.dynamic_index_in_dim(listed, left_index, 1, keepdims=False).reshape(NTV, NTV * NTV)
    live = lax.dynamic_slice_in_dim(own_c, first_tile, tile_count, 1).T.astype(jnp.float32)
    products = jnp.einsum(
        "xrq,tkq->txrk",
        left_rows,
        lax.all_gather(full_vectors, "occ", axis=1, tiled=True),
        preferred_element_type=jnp.float32,
    )
    inner = (products * live[:, :, None, None]).astype(jnp.bfloat16)
    swapped = inner.reshape(tile_count, NTV, a_local, TV, TV, TV).transpose(0, 1, 2, 4, 3, 5)
    swapped = swapped.reshape(tile_count, NTV * a_local * TV, PAIR)
    amp_columns = lax.all_gather(amps, "right", axis=3, tiled=True)
    d_first = first_tile % NTV
    own_amps = lax.dynamic_slice_in_dim(amp_columns[0], d_first, tile_count, 0)
    partial_sum = jnp.einsum(
        "trk,tkn->rn",
        swapped,
        lax.all_gather(own_amps, "occ", axis=1, tiled=True),
        preferred_element_type=jnp.float32,
    )
    partial_sum = partial_sum.reshape(NTV, row_count, NOP)
    owned_a = lax.psum_scatter(partial_sum, "left", scatter_dimension=0, tiled=True)
    b_tile = first_tile // NTV
    placed = lax.dynamic_update_slice_in_dim(
        jnp.zeros((NTV, row_count, NOP), jnp.float32), owned_a, b_tile, 0
    )
    summed = lax.psum_scatter(placed, "right", scatter_dimension=2, tiled=True)
    return summed.reshape(1, NTV, row_count, summed.shape[2])


def solution(mesh):
    placed = (P("right", "occ", "left"), P("left", None, "occ", "right"), P())
    return jax.shard_map(
        functools.partial(on_device, tuple(mesh.shape[axis] for axis in ("left", "right", "occ"))),
        mesh=mesh,
        in_specs=placed,
        out_specs=P("left", None, "occ", "right"),
        check_vma=False,
    )
```

```python
import functools

import jax
import jax.numpy as jnp
from jax import lax
from jax.experimental import pallas as pl
from jax.experimental.pallas import tpu as pltpu
from jax.sharding import PartitionSpec as P

TV = 32
NTV = 4
NOP = 512
PAIR = 1024
GROUPS = 4


def ladder_kernel(steps, count, first, live_ref, pick_ref, tile_ref, *refs):
    lefts = [refs[s * count:(s + 1) * count] for s in range(steps)]
    rights = refs[steps * count:steps * (count + 1)]
    rest = refs[steps * (count + 1):]
    amp_ref = rest[0]
    before_ref = None if first else rest[1]
    out_ref, products, ready = rest[-3:]
    step = pl.program_id(0)
    group_rows = lefts[0][0].shape[1]
    c_part = TV // GROUPS
    a_count = group_rows // c_part
    wide = 2 * GROUPS * TV
    blocks = rights[0].shape[0] // wide

    @pl.when(step < GROUPS)
    def _():
        for p in range(blocks):
            total = None
            for s in range(steps):
                left = jnp.concatenate([ref[0] for ref in lefts[s]], axis=0)
                right = jnp.concatenate(
                    [
                        rights[s][
                            pl.ds(pl.multiple_of(p * wide + (g // GROUPS * GROUPS + (g + step) % GROUPS) * TV, TV), TV), :
                        ]
                        for g in range(2 * GROUPS)
                    ],
                    axis=0,
                )
                term = lax.dot_general(
                    left, right, (((1,), (1,)), ((), ())), preferred_element_type=jnp.float32
                )
                total = term if total is None else total + term
            products[step, p] = total.astype(jnp.bfloat16)

    @pl.when(step >= GROUPS)
    def _():
        k = step - GROUPS
        lane_group = lax.broadcasted_iota(jnp.int32, (count * group_rows, wide), 1) // TV % GROUPS
        for p in range(blocks):
            mixed = products[k, p]
            for g in range(1, GROUPS):
                mixed = jnp.where(lane_group == g, products[(k + GROUPS - g) % GROUPS, p], mixed)
            mixed = mixed.reshape(count, c_part, a_count, wide)
            for b in range(2):
                for c in range(c_part):
                    ready[:, 2 * p + b, :, c * GROUPS * TV:(c + 1) * GROUPS * TV] = mixed[
                        :, c, :, b * GROUPS * TV:(b + 1) * GROUPS * TV
                    ]
        amp = jnp.concatenate(
            [
                amp_ref[0, pl.ds(pl.multiple_of(((k + GROUPS - g) % GROUPS * c_part + c) * TV, TV), TV), :]
                for c in range(c_part)
                for g in range(GROUPS)
            ],
            axis=0,
        )
        block_rows = TV // GROUPS * a_count
        terms = jnp.dot(
            ready[...].reshape(count * block_rows, TV * TV), amp, preferred_element_type=jnp.float32
        ).reshape(count, block_rows, amp.shape[1])
        for t in range(count):
            term = terms[t] * live_ref[t].astype(jnp.float32)
            if not first:
                term = before_ref[t, 0] + term
            out_ref[t, 0] = term.astype(out_ref.dtype)


def ladder(live, pick, tile, lefts, rights, amp, before, part=None, kind=jnp.float32):
    steps = len(lefts)
    rows, depth = lefts[0].shape[1:]
    columns = amp.shape[2]
    a_count = rows // TV
    b_blocks = TV // GROUPS
    wide = 2 * GROUPS * TV
    count = NTV if part is None else NTV // 2
    base = 0 if part is None else part * count
    one = pl.Buffered(1)

    def left_spec(t):
        return pl.BlockSpec(
            (1, rows // GROUPS, depth), lambda i, v, k, d: (k[t], jnp.minimum(i, GROUPS - 1), 0)
        )

    right_spec = pl.BlockSpec((2 * rows, depth), lambda i, v, k, d: (0, 0), pipeline_mode=one)
    amp_spec = pl.BlockSpec((1, 2 * rows, columns), lambda i, v, k, d: (d[0], 0, 0), pipeline_mode=one)

    def sum_spec(place):
        return pl.BlockSpec(
            (count, 1, b_blocks * a_count, columns),
            lambda i, v, k, d: (place, jnp.maximum(i - GROUPS, 0), 0, 0),
        )

    first = before is None
    flops = 2 * count * rows * 2 * rows * (steps * depth + columns)
    operands = [live[base:base + count], pick[base:base + count], tile]
    operands += [x for x in lefts for _ in range(count)] + [*rights, amp]
    return pl.pallas_call(
        functools.partial(ladder_kernel, steps, count, first),
        grid_spec=pltpu.PrefetchScalarGridSpec(
            num_scalar_prefetch=3,
            grid=(2 * GROUPS,),
            in_specs=[left_spec(t) for _ in lefts for t in range(count)]
            + [right_spec] * steps
            + [amp_spec]
            + [sum_spec(base // count)] * (not first),
            out_specs=sum_spec(0),
            scratch_shapes=[
                pltpu.VMEM((GROUPS, 2 * rows // wide, count * rows // GROUPS, wide), jnp.bfloat16),
                pltpu.VMEM((count, b_blocks, a_count, TV * TV), jnp.bfloat16),
            ],
        ),
        out_shape=jax.ShapeDtypeStruct((count, GROUPS, b_blocks * a_count, columns), kind),
        input_output_aliases={} if first or part is not None else {len(operands): 0},
        compiler_params=pltpu.CompilerParams(vmem_limit_bytes=40 * 2**20),
        cost_estimate=pl.CostEstimate(flops=flops, bytes_accessed=20 * 2**20, transcendentals=0),
    )(*operands, *([] if first else [before]))


def partner(value, axis, size, flip):
    return lax.ppermute(value, axis, [(i, i ^ flip) for i in range(size)])


def shift(value, axis, size, step):
    return lax.ppermute(value, axis, [(i, (i + step) % size) for i in range(size)])


def ring_order(size):
    return list(range(0, size, 2)) + list(range(size - 1, 0, -2))


HOPS = (
    (1, 2), (1, 1), (1, 0), (2, 1), (2, 0), (3, 0),
    (1, 3), (2, 3), (2, 2), (3, 2), (3, 1), (3, 3),
)
AMP = "amp"
NEAR = {0: (0,), 2: (AMP,), 3: (1,), 5: (2,), 6: (3,)}
FAR = {1: (0,), 3: (AMP,), 4: (1,), 6: (2,), 7: (3,)}
STACK = {2: (0,), 4: (AMP,), 5: (1,), 7: (2,), 8: (3,)}
OTHER = {
    0: ((0, 0),), 1: ((0, 2), (1, 2)), 2: ((0, 1), (1, 1)), 3: ((1, 0),), 4: ((0, 3), (2, 1)), 5: ((2, 0),),
    6: ((3, 0),), 7: ((1, 3),), 8: ((2, 3),), 9: ((2, 2),), 10: ((3, 2),), 11: ((3, 1),), 12: ((3, 3),),
}
CONTRACT = {8: 0, 10: 2, 11: 1}


def on_square(chol, amps, listed):
    row_count, depth = chol.shape[1:]
    columns = amps.shape[3]
    a_count = row_count // TV
    left_index = lax.axis_index("left")
    right_index = lax.axis_index("right")
    order = ring_order(NTV)
    ring = [(order[p], order[(p + 1) % NTV]) for p in range(NTV)]
    near = [[order[(order.index(level) + i) % NTV] for i in range(NTV)] for level in range(NTV)]
    d_tiles = jnp.asarray(near, jnp.int32)[left_index]
    tiles = jnp.arange(NTV)
    targets = (left_index + 1 + tiles) % NTV
    pick = (targets ^ right_index).astype(jnp.int32)
    own_c = lax.dynamic_index_in_dim(listed, left_index, 1, keepdims=False)
    live = lax.dynamic_index_in_dim(own_c, right_index, 1, keepdims=False)[targets]

    held = {("block", 0, i): lax.dynamic_index_in_dim(chol, d_tiles[i], 0, keepdims=False) for i in range(NTV)}
    held["left", AMP, 0] = amps[0]
    last = len(HOPS)
    waiting = {slot: [] for slot in range(last + 3)}

    def meet(keys):
        keys = list(dict.fromkeys(keys))
        for key, value in zip(keys, lax.optimization_barrier([held[key] for key in keys])):
            held[key] = value

    def own_left(s):
        own = held["block", s, 0].reshape(a_count, TV, depth)
        held["left", s, 0] = own.transpose(1, 0, 2).reshape(row_count, depth)

    def contract(i, before, part=None, kind=jnp.float32):
        return ladder(
            lax.dynamic_index_in_dim(live, d_tiles[i], 1, keepdims=False),
            pick,
            d_tiles[i:i + 1],
            [held["lefts", s] for s in range(NTV)],
            [held["both", s, i] for s in range(NTV)],
            held["amp"],
            before,
            part,
            kind,
        )

    for slot in range(last + 1):
        hops = [0, 1] if slot == 0 else [slot + 1] if slot + 1 < last else []
        now = waiting[slot]
        if slot >= 1:
            now.append(("block", *HOPS[slot - 1]))
        for s in NEAR.get(slot, ()):
            if s != AMP:
                own_left(s)
        now += [("block", HOPS[u][0] - 1, (HOPS[u][1] + 1) % NTV) for u in hops]
        now += [("left", s, 0) for s in NEAR.get(slot, ())]
        now += [("left", s, flip) for s in FAR.get(slot, ()) for flip in (1, 2)]
        now += [("left", s, part) for s in STACK.get(slot, ()) for part in ("a", "b")]
        now += [("block", *unit) for unit in OTHER.get(slot, ())]
        meet(now)
        for u in hops:
            s, i = HOPS[u]
            held["block", s, i] = lax.ppermute(held["block", s - 1, (i + 1) % NTV], "left", ring)
        for s in FAR.get(slot, ()):
            middle = held["left", s, 0].shape[0] // 2
            held["left", s, "a"] = partner(held["left", s, 1][:middle], "right", NTV, 2)
            held["left", s, "b"] = partner(held["left", s, 2][middle:], "right", NTV, 1)
        for s in NEAR.get(slot, ()):
            for flip in (1, 2):
                held["left", s, flip] = partner(held["left", s, 0], "right", NTV, flip)
        for s in STACK.get(slot, ()):
            far = jnp.concatenate([held["left", s, "a"], held["left", s, "b"]], axis=0)
            every = [held["left", s, 0], held["left", s, 1], held["left", s, 2], far]
            if s == AMP:
                held["amp"] = lax.all_gather(jnp.concatenate(every, axis=2), "occ", axis=1, tiled=True)
                waiting[slot + 2].append("amp")
            else:
                held["lefts", s] = jnp.stack(every)
                waiting[slot + 1].append(("lefts", s))
        for unit in OTHER.get(slot, ()):
            held["both", *unit] = lax.all_gather(held["block", *unit], "occ", axis=0, tiled=True)
            waiting[slot + 2].append(("both", *unit))
        if slot in CONTRACT:
            held["sum"] = contract(CONTRACT[slot], held.get("sum"))
            waiting[slot + 1].append("sum")
    partials = held["sum"]
    early = contract(3, partials, 0, jnp.bfloat16)
    moved = [shift(early[t], "left", NTV, t + 1) for t in range(NTV // 2)]
    late = contract(3, partials, 1)
    moved += [
        shift(late[t].astype(jnp.bfloat16), "left", NTV, NTV // 2 + t + 1) for t in range(NTV // 2 - 1)
    ]
    summed = late[NTV // 2 - 1]
    for piece in moved:
        summed = summed + piece.astype(jnp.float32)
    pieces = []
    for flip in range(NTV):
        piece = summed[:, :, flip * columns:(flip + 1) * columns]
        pieces.append(partner(piece, "right", NTV, flip) if flip else piece)
    result = jnp.stack(pieces)[tiles ^ right_index]
    result = result.reshape(NTV, GROUPS, TV // GROUPS, a_count, columns).transpose(0, 3, 2, 1, 4)
    return result.reshape(1, NTV, row_count, columns)


def broadcast(value, axis, source):
    kept = jnp.where(lax.axis_index(axis) == source, value, 0).astype(value.dtype)
    return lax.psum(kept, axis)


def on_device(sizes, chol, amps, listed):
    tile_count = chol.shape[0]
    if sizes == (NTV, NTV, 2) and tile_count == NTV:
        return on_square(chol, amps, listed)
    row_count = chol.shape[1]
    a_local = row_count // TV
    left_index = lax.axis_index("left")
    right_index = lax.axis_index("right")
    first_tile = right_index * tile_count
    full_vectors = lax.all_gather(chol, "left", axis=2, tiled=True)
    collected = []
    for a_tile in range(NTV):
        wanted = a_tile * NTV + left_index
        holder = wanted // tile_count
        holder_slot = wanted % tile_count
        offered = lax.dynamic_index_in_dim(full_vectors, holder_slot, 0, keepdims=False)
        collected.append(broadcast(offered, "right", holder))
    left_rows = jnp.stack(collected)
    own_c = lax.dynamic_index_in_dim(listed, left_index, 1, keepdims=False).reshape(NTV, NTV * NTV)
    live = lax.dynamic_slice_in_dim(own_c, first_tile, tile_count, 1).T.astype(jnp.float32)
    products = jnp.einsum(
        "xrq,tkq->txrk",
        left_rows,
        lax.all_gather(full_vectors, "occ", axis=1, tiled=True),
        preferred_element_type=jnp.float32,
    )
    inner = (products * live[:, :, None, None]).astype(jnp.bfloat16)
    swapped = inner.reshape(tile_count, NTV, a_local, TV, TV, TV).transpose(0, 1, 2, 4, 3, 5)
    swapped = swapped.reshape(tile_count, NTV * a_local * TV, PAIR)
    amp_columns = lax.all_gather(amps, "right", axis=3, tiled=True)
    d_first = first_tile % NTV
    own_amps = lax.dynamic_slice_in_dim(amp_columns[0], d_first, tile_count, 0)
    partial_sum = jnp.einsum(
        "trk,tkn->rn",
        swapped,
        lax.all_gather(own_amps, "occ", axis=1, tiled=True),
        preferred_element_type=jnp.float32,
    )
    partial_sum = partial_sum.reshape(NTV, row_count, NOP)
    owned_a = lax.psum_scatter(partial_sum, "left", scatter_dimension=0, tiled=True)
    b_tile = first_tile // NTV
    placed = lax.dynamic_update_slice_in_dim(
        jnp.zeros((NTV, row_count, NOP), jnp.float32), owned_a, b_tile, 0
    )
    summed = lax.psum_scatter(placed, "right", scatter_dimension=2, tiled=True)
    return summed.reshape(1, NTV, row_count, summed.shape[2])


def solution(mesh):
    placed = (P("right", "occ", "left"), P("left", None, "occ", "right"), P())
    return jax.shard_map(
        functools.partial(on_device, tuple(mesh.shape[axis] for axis in ("left", "right", "occ"))),
        mesh=mesh,
        in_specs=placed,
        out_specs=P("left", None, "occ", "right"),
        check_vma=False,
    )
```

```python
import functools

import jax
import jax.numpy as jnp
from jax import lax
from jax.experimental import pallas as pl
from jax.experimental.pallas import tpu as pltpu
from jax.sharding import PartitionSpec as P

TV = 32
NTV = 4
NOP = 512
PAIR = 1024
GROUPS = 4


def ladder_kernel(steps, count, first, half_ref, live_ref, pick_ref, tile_ref, *refs):
    lefts = [refs[s * count:(s + 1) * count] for s in range(steps)]
    rights = [refs[steps * count + 2 * s: steps * count + 2 * s + 2] for s in range(steps)]
    rest = refs[steps * (count + 2):]
    amp_ref = rest[0]
    before_ref = None if first else rest[1]
    out_ref, products, ready = rest[-3:]
    step = pl.program_id(0)
    group_rows = lefts[0][0].shape[1]
    c_part = TV // GROUPS
    a_count = group_rows // c_part
    wide = 2 * GROUPS * TV
    half_blocks = rights[0][0].shape[1] // wide

    @pl.when(step < GROUPS)
    def _():
        for half in range(2):
            start = (half_ref[0] if half == 0 else 1 - half_ref[0]) * half_blocks
            for p in range(half_blocks):
                left = jnp.concatenate(
                    [jnp.concatenate([part[t][0] for part in lefts], axis=1) for t in range(count)], axis=0
                )
                right = jnp.concatenate(
                    [
                        jnp.concatenate(
                            [
                                part[half][
                                    0,
                                    pl.ds(
                                        pl.multiple_of(
                                            p * wide + (g // GROUPS * GROUPS + (g + step) % GROUPS) * TV, TV
                                        ),
                                        TV,
                                    ),
                                    :,
                                ]
                                for g in range(2 * GROUPS)
                            ],
                            axis=0,
                        )
                        for part in rights
                    ],
                    axis=1,
                )
                total = lax.dot_general(
                    left, right, (((1,), (1,)), ((), ())), preferred_element_type=jnp.float32
                )
                products[step, start + p] = total.astype(jnp.bfloat16)

    @pl.when(step >= GROUPS)
    def _():
        k = step - GROUPS
        lane_group = lax.broadcasted_iota(jnp.int32, (count * group_rows, wide), 1) // TV % GROUPS
        for p in range(2 * half_blocks):
            mixed = products[k, p]
            for g in range(1, GROUPS):
                mixed = jnp.where(lane_group == g, products[(k + GROUPS - g) % GROUPS, p], mixed)
            mixed = mixed.reshape(count, c_part, a_count, wide)
            for b in range(2):
                for c in range(c_part):
                    ready[:, 2 * p + b, :, c * GROUPS * TV:(c + 1) * GROUPS * TV] = mixed[
                        :, c, :, b * GROUPS * TV:(b + 1) * GROUPS * TV
                    ]
        amp = jnp.concatenate(
            [
                amp_ref[0, pl.ds(pl.multiple_of(((k + GROUPS - g) % GROUPS * c_part + c) * TV, TV), TV), :]
                for c in range(c_part)
                for g in range(GROUPS)
            ],
            axis=0,
        )
        block_rows = TV // GROUPS * a_count
        terms = jnp.dot(
            ready[...].reshape(count * block_rows, TV * TV), amp, preferred_element_type=jnp.float32
        ).reshape(count, block_rows, amp.shape[1])
        for t in range(count):
            term = terms[t] * live_ref[t].astype(jnp.float32)
            if not first:
                term = before_ref[t, 0] + term
            out_ref[t, 0] = term.astype(out_ref.dtype)


def ladder(half, live, pick, tile, lefts, rights, amp, before, part=None, kind=jnp.float32):
    steps = len(lefts)
    rows, depth = lefts[0].shape[1:]
    columns = amp.shape[2]
    a_count = rows // TV
    b_blocks = TV // GROUPS
    wide = 2 * GROUPS * TV
    count = NTV if part is None else NTV // 2
    base = 0 if part is None else part * count
    one = pl.Buffered(1)

    def left_spec(t):
        return pl.BlockSpec(
            (1, rows // GROUPS, depth), lambda i, h, v, k, d: (k[t], jnp.minimum(i, GROUPS - 1), 0)
        )

    def right_spec(place):
        return pl.BlockSpec(
            (1, rows, depth),
            lambda i, h, v, k, d: (d[0] if place is None else place, 0, 0),
            pipeline_mode=one,
        )

    amp_spec = pl.BlockSpec((1, 2 * rows, columns), lambda i, h, v, k, d: (d[0], 0, 0), pipeline_mode=one)

    def sum_spec(place):
        return pl.BlockSpec(
            (count, 1, b_blocks * a_count, columns),
            lambda i, h, v, k, d: (place, jnp.maximum(i - GROUPS, 0), 0, 0),
        )

    first = before is None
    flops = 2 * count * rows * 2 * rows * (steps * depth + columns)
    operands = [half, live[base:base + count], pick[base:base + count], tile]
    operands += [x for x in lefts for _ in range(count)] + [x for own, other, _ in rights for x in (own, other)] + [amp]
    return pl.pallas_call(
        functools.partial(ladder_kernel, steps, count, first),
        grid_spec=pltpu.PrefetchScalarGridSpec(
            num_scalar_prefetch=4,
            grid=(2 * GROUPS,),
            in_specs=[left_spec(t) for _ in lefts for t in range(count)]
            + [right_spec(place) for _, _, place in rights for _ in range(2)]
            + [amp_spec]
            + [sum_spec(base // count)] * (not first),
            out_specs=sum_spec(0),
            scratch_shapes=[
                pltpu.VMEM((GROUPS, 2 * rows // wide, count * rows // GROUPS, wide), jnp.bfloat16),
                pltpu.VMEM((count, b_blocks, a_count, TV * TV), jnp.bfloat16),
            ],
        ),
        out_shape=jax.ShapeDtypeStruct((count, GROUPS, b_blocks * a_count, columns), kind),
        input_output_aliases={} if first or part is not None else {len(operands): 0},
        compiler_params=pltpu.CompilerParams(vmem_limit_bytes=40 * 2**20),
        cost_estimate=pl.CostEstimate(flops=flops, bytes_accessed=20 * 2**20, transcendentals=0),
    )(*operands, *([] if first else [before]))


def partner(value, axis, size, flip):
    return lax.ppermute(value, axis, [(i, i ^ flip) for i in range(size)])


def shift(value, axis, size, step):
    return lax.ppermute(value, axis, [(i, (i + step) % size) for i in range(size)])


def ring_order(size):
    return list(range(0, size, 2)) + list(range(size - 1, 0, -2))


HOPS = (
    (1, 2), (1, 1), (1, 0), (2, 1), (2, 0), (3, 0),
    (1, 3), (2, 3), (2, 2), (3, 2), (3, 1), (3, 3),
)
AMP = "amp"
NEAR = {0: 0, 2: AMP, 4: 1, 6: 2, 8: 3}
FAR = {1: 0, 3: AMP, 5: 1, 7: 2, 9: 3}
STACK = {2: 0, 4: AMP, 6: 1, 8: 2, 10: 3}
CONTRACT = {10: 0, 11: 2, 12: 1}


def on_square(chol, amps, listed):
    row_count, depth = chol.shape[1:]
    columns = amps.shape[3]
    a_count = row_count // TV
    left_index = lax.axis_index("left")
    right_index = lax.axis_index("right")
    occ_index = lax.axis_index("occ")
    order = ring_order(NTV)
    ring = [(order[p], order[(p + 1) % NTV]) for p in range(NTV)]
    near = [[order[(order.index(level) + i) % NTV] for level in range(NTV)] for i in range(NTV)]

    def at_level(table):
        value = jnp.int32(table[0])
        for level in range(1, NTV):
            value = jnp.where(left_index == level, jnp.int32(table[level]), value)
        return value

    d_tiles = [at_level(table) for table in near]
    tiles = jnp.arange(NTV)
    targets = (left_index + 1 + tiles) % NTV
    pick = (targets ^ right_index).astype(jnp.int32)
    own_c = lax.dynamic_index_in_dim(listed, left_index, 1, keepdims=False)
    live = lax.dynamic_index_in_dim(own_c, right_index, 1, keepdims=False)[targets]
    half = occ_index.reshape(1)

    held = {("block", 0, i): lax.dynamic_slice_in_dim(chol, d_tiles[i], 1, 0) for i in (3, 2, 0, 1)}
    held["chol"] = chol
    held["left", AMP, 0] = amps[0]
    last = len(HOPS)
    waiting = {slot: [] for slot in range(last + 4)}

    def meet(keys):
        keys = list(dict.fromkeys(keys))
        for key, value in zip(keys, lax.optimization_barrier([held[key] for key in keys])):
            held[key] = value

    def contract(i, before, part=None, kind=jnp.float32):
        sides = [(held["chol"], held["other", "chol"], None)]
        sides += [(held["block", s, i], held["other", s, i], 0) for s in range(1, NTV)]
        return ladder(
            half,
            lax.dynamic_index_in_dim(live, d_tiles[i], 1, keepdims=False),
            pick,
            d_tiles[i].reshape(1),
            [held["lefts", s] for s in range(NTV)],
            sides,
            held["amp"],
            before,
            part,
            kind,
        )

    for slot in range(last + 1):
        hops = [0, 1] if slot == 0 else [slot + 1] if slot + 1 < last else []
        near_block, far_block, stack_block = NEAR.get(slot), FAR.get(slot), STACK.get(slot)
        now = waiting[slot]
        if slot >= 1:
            now.append(("block", *HOPS[slot - 1]))
        if near_block is not None:
            if near_block != AMP:
                own = held["block", near_block, 0].reshape(a_count, TV, depth)
                held["left", near_block, 0] = own.transpose(1, 0, 2).reshape(row_count, depth)
            now.append(("left", near_block, 0))
        if far_block is not None:
            now += [("left", far_block, flip) for flip in range(3)]
        if stack_block is not None:
            now.append(("left", stack_block, 3))
        now += [("block", HOPS[u][0] - 1, (HOPS[u][1] + 1) % NTV) for u in hops]
        if slot == 1:
            now.append("chol")
        meet(now)
        for u in hops:
            s, i = HOPS[u]
            held["block", s, i] = lax.ppermute(held["block", s - 1, (i + 1) % NTV], "left", ring)
        if near_block is not None:
            for flip in (1, 2):
                held["left", near_block, flip] = partner(held["left", near_block, 0], "right", NTV, flip)
        if far_block is not None:
            held["left", far_block, 3] = partner(held["left", far_block, 0], "right", NTV, 3)
        if slot == 1:
            held["other", "chol"] = partner(held["chol"], "occ", 2, 1)
            waiting[slot + 1].append(("other", "chol"))
        if slot >= 1:
            unit = HOPS[slot - 1]
            held["other", *unit] = partner(held["block", *unit], "occ", 2, 1)
            waiting[slot + 1].append(("other", *unit))
        if stack_block is not None:
            every = [held["left", stack_block, flip] for flip in range(NTV)]
            if stack_block == AMP:
                held["amp"] = lax.all_gather(jnp.concatenate(every, axis=2), "occ", axis=1, tiled=True)
                waiting[slot + 3].append("amp")
            else:
                held["lefts", stack_block] = jnp.stack(every)
                waiting[slot + 1].append(("lefts", stack_block))
        if slot in CONTRACT:
            held["sum"] = contract(CONTRACT[slot], held.get("sum"))
            waiting[slot + 1].append("sum")
    partials = held["sum"]
    early = contract(3, partials, 0, jnp.bfloat16)
    moved = [shift(early[t], "left", NTV, t + 1) for t in range(NTV // 2)]
    late = contract(3, partials, 1)
    moved += [
        shift(late[t].astype(jnp.bfloat16), "left", NTV, NTV // 2 + t + 1) for t in range(NTV // 2 - 1)
    ]
    summed = late[NTV // 2 - 1]
    for piece in moved:
        summed = summed + piece.astype(jnp.float32)
    pieces = []
    for flip in range(NTV):
        piece = summed[:, :, flip * columns:(flip + 1) * columns]
        pieces.append(partner(piece, "right", NTV, flip) if flip else piece)
    result = jnp.stack(pieces)[tiles ^ right_index]
    result = result.reshape(NTV, GROUPS, TV // GROUPS, a_count, columns).transpose(0, 3, 2, 1, 4)
    return result.reshape(1, NTV, row_count, columns)


def broadcast(value, axis, source):
    kept = jnp.where(lax.axis_index(axis) == source, value, 0).astype(value.dtype)
    return lax.psum(kept, axis)


def on_device(sizes, chol, amps, listed):
    tile_count = chol.shape[0]
    if sizes == (NTV, NTV, 2) and tile_count == NTV:
        return on_square(chol, amps, listed)
    row_count = chol.shape[1]
    a_local = row_count // TV
    left_index = lax.axis_index("left")
    right_index = lax.axis_index("right")
    first_tile = right_index * tile_count
    full_vectors = lax.all_gather(chol, "left", axis=2, tiled=True)
    collected = []
    for a_tile in range(NTV):
        wanted = a_tile * NTV + left_index
        holder = wanted // tile_count
        holder_slot = wanted % tile_count
        offered = lax.dynamic_index_in_dim(full_vectors, holder_slot, 0, keepdims=False)
        collected.append(broadcast(offered, "right", holder))
    left_rows = jnp.stack(collected)
    own_c = lax.dynamic_index_in_dim(listed, left_index, 1, keepdims=False).reshape(NTV, NTV * NTV)
    live = lax.dynamic_slice_in_dim(own_c, first_tile, tile_count, 1).T.astype(jnp.float32)
    products = jnp.einsum(
        "xrq,tkq->txrk",
        left_rows,
        lax.all_gather(full_vectors, "occ", axis=1, tiled=True),
        preferred_element_type=jnp.float32,
    )
    inner = (products * live[:, :, None, None]).astype(jnp.bfloat16)
    swapped = inner.reshape(tile_count, NTV, a_local, TV, TV, TV).transpose(0, 1, 2, 4, 3, 5)
    swapped = swapped.reshape(tile_count, NTV * a_local * TV, PAIR)
    amp_columns = lax.all_gather(amps, "right", axis=3, tiled=True)
    d_first = first_tile % NTV
    own_amps = lax.dynamic_slice_in_dim(amp_columns[0], d_first, tile_count, 0)
    partial_sum = jnp.einsum(
        "trk,tkn->rn",
        swapped,
        lax.all_gather(own_amps, "occ", axis=1, tiled=True),
        preferred_element_type=jnp.float32,
    )
    partial_sum = partial_sum.reshape(NTV, row_count, NOP)
    owned_a = lax.psum_scatter(partial_sum, "left", scatter_dimension=0, tiled=True)
    b_tile = first_tile // NTV
    placed = lax.dynamic_update_slice_in_dim(
        jnp.zeros((NTV, row_count, NOP), jnp.float32), owned_a, b_tile, 0
    )
    summed = lax.psum_scatter(placed, "right", scatter_dimension=2, tiled=True)
    return summed.reshape(1, NTV, row_count, summed.shape[2])


def solution(mesh):
    placed = (P("right", "occ", "left"), P("left", None, "occ", "right"), P())
    return jax.shard_map(
        functools.partial(on_device, tuple(mesh.shape[axis] for axis in ("left", "right", "occ"))),
        mesh=mesh,
        in_specs=placed,
        out_specs=P("left", None, "occ", "right"),
        check_vma=False,
    )
```

```python
import functools

import jax
import jax.numpy as jnp
from jax import lax
from jax.experimental import pallas as pl
from jax.experimental.pallas import tpu as pltpu
from jax.sharding import PartitionSpec as P

TV = 32
NTV = 4
NOP = 512
PAIR = 1024
GROUPS = 4


def ladder_kernel(steps, count, first, half_ref, live_ref, pick_ref, tile_ref, *refs):
    lefts = [refs[s * count:(s + 1) * count] for s in range(steps)]
    rights = [refs[steps * count + 2 * s: steps * count + 2 * s + 2] for s in range(steps)]
    rest = refs[steps * (count + 2):]
    amp_ref = rest[0]
    before_ref = None if first else rest[1]
    out_ref, products, ready = rest[-3:]
    step = pl.program_id(0)
    group_rows = lefts[0][0].shape[1]
    c_part = TV // GROUPS
    a_count = group_rows // c_part
    wide = 2 * GROUPS * TV
    half_blocks = rights[0][0].shape[1] // wide

    @pl.when(step < GROUPS)
    def _():
        for half in range(2):
            start = (half_ref[0] if half == 0 else 1 - half_ref[0]) * half_blocks
            for p in range(half_blocks):
                left = jnp.concatenate(
                    [jnp.concatenate([part[t][0] for part in lefts], axis=1) for t in range(count)], axis=0
                )
                right = jnp.concatenate(
                    [
                        jnp.concatenate(
                            [
                                part[half][
                                    0,
                                    pl.ds(
                                        pl.multiple_of(
                                            p * wide + (g // GROUPS * GROUPS + (g + step) % GROUPS) * TV, TV
                                        ),
                                        TV,
                                    ),
                                    :,
                                ]
                                for g in range(2 * GROUPS)
                            ],
                            axis=0,
                        )
                        for part in rights
                    ],
                    axis=1,
                )
                total = lax.dot_general(
                    left, right, (((1,), (1,)), ((), ())), preferred_element_type=jnp.float32
                )
                products[step, start + p] = total.astype(jnp.bfloat16)

    @pl.when(step >= GROUPS)
    def _():
        k = step - GROUPS
        lane_group = lax.broadcasted_iota(jnp.int32, (count * group_rows, wide), 1) // TV % GROUPS
        for p in range(2 * half_blocks):
            mixed = products[k, p]
            for g in range(1, GROUPS):
                mixed = jnp.where(lane_group == g, products[(k + GROUPS - g) % GROUPS, p], mixed)
            mixed = mixed.reshape(count, c_part, a_count, wide)
            for b in range(2):
                for c in range(c_part):
                    ready[:, 2 * p + b, :, c * GROUPS * TV:(c + 1) * GROUPS * TV] = mixed[
                        :, c, :, b * GROUPS * TV:(b + 1) * GROUPS * TV
                    ]
        amp = jnp.concatenate(
            [
                amp_ref[0, pl.ds(pl.multiple_of(((k + GROUPS - g) % GROUPS * c_part + c) * TV, TV), TV), :]
                for c in range(c_part)
                for g in range(GROUPS)
            ],
            axis=0,
        )
        block_rows = TV // GROUPS * a_count
        terms = jnp.dot(
            ready[...].reshape(count * block_rows, TV * TV), amp, preferred_element_type=jnp.float32
        ).reshape(count, block_rows, amp.shape[1])
        for t in range(count):
            term = terms[t] * live_ref[t].astype(jnp.float32)
            if not first:
                term = before_ref[t, 0] + term
            out_ref[t, 0] = term.astype(out_ref.dtype)


def ladder(half, live, pick, tile, lefts, rights, amp, before, part=None, kind=jnp.float32):
    steps = len(lefts)
    rows, depth = lefts[0].shape[1:]
    columns = amp.shape[2]
    a_count = rows // TV
    b_blocks = TV // GROUPS
    wide = 2 * GROUPS * TV
    count = NTV if part is None else NTV // 2
    base = 0 if part is None else part * count
    one = pl.Buffered(1)

    def left_spec(t):
        return pl.BlockSpec(
            (1, rows // GROUPS, depth), lambda i, h, v, k, d: (k[t], jnp.minimum(i, GROUPS - 1), 0)
        )

    def right_spec(place, other):
        return pl.BlockSpec(
            (1, rows, depth),
            lambda i, h, v, k, d: (d[0] if place is None else place, 1 - h[0] if other else 0, 0),
            pipeline_mode=one,
        )

    amp_spec = pl.BlockSpec((1, 2 * rows, columns), lambda i, h, v, k, d: (d[0], 0, 0), pipeline_mode=one)

    def sum_spec(place):
        return pl.BlockSpec(
            (count, 1, b_blocks * a_count, columns),
            lambda i, h, v, k, d: (place, jnp.maximum(i - GROUPS, 0), 0, 0),
        )

    first = before is None
    flops = 2 * count * rows * 2 * rows * (steps * depth + columns)
    operands = [half, live[base:base + count], pick[base:base + count], tile]
    operands += [x for x in lefts for _ in range(count)] + [x for own, other, _ in rights for x in (own, other)] + [amp]
    return pl.pallas_call(
        functools.partial(ladder_kernel, steps, count, first),
        grid_spec=pltpu.PrefetchScalarGridSpec(
            num_scalar_prefetch=4,
            grid=(2 * GROUPS,),
            in_specs=[left_spec(t) for _ in lefts for t in range(count)]
            + [
                right_spec(place, other)
                for own, both, place in rights
                for other in (False, both.shape[1] > own.shape[1])
            ]
            + [amp_spec]
            + [sum_spec(base // count)] * (not first),
            out_specs=sum_spec(0),
            scratch_shapes=[
                pltpu.VMEM((GROUPS, 2 * rows // wide, count * rows // GROUPS, wide), jnp.bfloat16),
                pltpu.VMEM((count, b_blocks, a_count, TV * TV), jnp.bfloat16),
            ],
        ),
        out_shape=jax.ShapeDtypeStruct((count, GROUPS, b_blocks * a_count, columns), kind),
        input_output_aliases={} if first or part is not None else {len(operands): 0},
        compiler_params=pltpu.CompilerParams(vmem_limit_bytes=40 * 2**20),
        cost_estimate=pl.CostEstimate(flops=flops, bytes_accessed=20 * 2**20, transcendentals=0),
    )(*operands, *([] if first else [before]))


def partner(value, axis, size, flip):
    return lax.ppermute(value, axis, [(i, i ^ flip) for i in range(size)])


def shift(value, axis, size, step):
    return lax.ppermute(value, axis, [(i, (i + step) % size) for i in range(size)])


def ring_order(size):
    return list(range(0, size, 2)) + list(range(size - 1, 0, -2))


HOPS = (
    (1, 2), (1, 1), (1, 0), (2, 1), (2, 0), (3, 0),
    (1, 3), (2, 3), (2, 2), (3, 2), (3, 1), (3, 3),
)
AMP = "amp"
NEAR = {0: 0, 2: AMP, 4: 1, 6: 2, 8: 3}
FAR = {1: 0, 3: AMP, 5: 1, 7: 2, 9: 3}
STACK = {3: 0, 5: AMP, 7: 1, 9: 2, 10: 3}
CROSS = {10: (8, 9), 11: (10,), 12: (11,)}
GATHERED = 8
CONTRACT = {10: 0, 11: 2, 12: 1}


def on_square(chol, amps, listed):
    row_count, depth = chol.shape[1:]
    columns = amps.shape[3]
    a_count = row_count // TV
    left_index = lax.axis_index("left")
    right_index = lax.axis_index("right")
    occ_index = lax.axis_index("occ")
    order = ring_order(NTV)
    ring = [(order[p], order[(p + 1) % NTV]) for p in range(NTV)]
    near = [[order[(order.index(level) + i) % NTV] for level in range(NTV)] for i in range(NTV)]

    def at_level(table):
        value = jnp.int32(table[0])
        for level in range(1, NTV):
            value = jnp.where(left_index == level, jnp.int32(table[level]), value)
        return value

    d_tiles = [at_level(table) for table in near]
    tiles = jnp.arange(NTV)
    targets = (left_index + 1 + tiles) % NTV
    pick = (targets ^ right_index).astype(jnp.int32)
    own_c = lax.dynamic_index_in_dim(listed, left_index, 1, keepdims=False)
    live = lax.dynamic_index_in_dim(own_c, right_index, 1, keepdims=False)[targets]
    half = occ_index.reshape(1)

    held = {("block", 0, i): lax.dynamic_slice_in_dim(chol, d_tiles[i], 1, 0) for i in (3, 2, 0, 1)}
    held["chol"] = chol
    held["left", AMP, 0] = amps[0]
    last = len(HOPS)
    waiting = {slot: [] for slot in range(last + 4)}

    def meet(keys):
        keys = list(dict.fromkeys(keys))
        for key, value in zip(keys, lax.optimization_barrier([held[key] for key in keys])):
            held[key] = value

    def contract(i, before, part=None, kind=jnp.float32):
        sides = [(held["chol"], held["other", "chol"], None)]
        sides += [(held["block", s, i], held["other", s, i], 0) for s in range(1, NTV)]
        return ladder(
            half,
            lax.dynamic_index_in_dim(live, d_tiles[i], 1, keepdims=False),
            pick,
            d_tiles[i].reshape(1),
            [held["lefts", s] for s in range(NTV)],
            sides,
            held["amp"],
            before,
            part,
            kind,
        )

    for slot in range(last + 1):
        hops = [0, 1] if slot == 0 else [slot + 1] if slot + 1 < last else []
        near_block, far_block, stack_block = NEAR.get(slot), FAR.get(slot), STACK.get(slot)
        now = waiting[slot]
        if slot >= 1:
            now.append(("block", *HOPS[slot - 1]))
        if near_block is not None:
            if near_block != AMP:
                own = held["block", near_block, 0].reshape(a_count, TV, depth)
                held["left", near_block, 0] = own.transpose(1, 0, 2).reshape(row_count, depth)
            now.append(("left", near_block, 0))
        if far_block is not None:
            now.append(("left", far_block, 0))
        if stack_block is not None:
            now += [("left", stack_block, flip) for flip in range(NTV)]
        now += [("block", HOPS[u][0] - 1, (HOPS[u][1] + 1) % NTV) for u in hops]
        if slot == 0:
            now.append("chol")
        meet(now)
        for u in hops:
            s, i = HOPS[u]
            held["block", s, i] = lax.ppermute(held["block", s - 1, (i + 1) % NTV], "left", ring)
        if near_block is not None:
            for flip in (1, 2):
                held["left", near_block, flip] = partner(held["left", near_block, 0], "right", NTV, flip)
            waiting[min(slot + 2, last - 2)] += [("left", near_block, 1), ("left", near_block, 2)]
        if far_block is not None:
            held["left", far_block, 3] = partner(held["left", far_block, 0], "right", NTV, 3)
        if slot == 0:
            held["other", "chol"] = lax.all_gather(held["chol"], "occ", axis=1, tiled=True)
            waiting[slot + 3].append(("other", "chol"))
        if 1 <= slot <= GATHERED:
            unit = HOPS[slot - 1]
            held["other", *unit] = lax.all_gather(held["block", *unit], "occ", axis=1, tiled=True)
            waiting[slot + 3].append(("other", *unit))
        for u in CROSS.get(slot, ()):
            unit = HOPS[u]
            held["other", *unit] = partner(held["block", *unit], "occ", 2, 1)
            waiting[slot + 1].append(("other", *unit))
        if stack_block is not None:
            every = [held["left", stack_block, flip] for flip in range(NTV)]
            if stack_block == AMP:
                held["amp"] = lax.all_gather(jnp.concatenate(every, axis=2), "occ", axis=1, tiled=True)
                waiting[slot + 3].append("amp")
            else:
                held["lefts", stack_block] = jnp.stack(every)
                waiting[slot + 1].append(("lefts", stack_block))
        if slot in CONTRACT:
            held["sum"] = contract(CONTRACT[slot], held.get("sum"))
            waiting[slot + 1].append("sum")
    partials = held["sum"]
    early = contract(3, partials, 0, jnp.bfloat16)
    moved = [shift(early[t], "left", NTV, t + 1) for t in range(NTV // 2)]
    late = contract(3, partials, 1)
    moved += [
        shift(late[t].astype(jnp.bfloat16), "left", NTV, NTV // 2 + t + 1) for t in range(NTV // 2 - 1)
    ]
    summed = late[NTV // 2 - 1]
    for piece in moved:
        summed = summed + piece.astype(jnp.float32)
    pieces = []
    for flip in range(NTV):
        piece = summed[:, :, flip * columns:(flip + 1) * columns]
        pieces.append(partner(piece, "right", NTV, flip) if flip else piece)
    result = jnp.stack(pieces)[tiles ^ right_index]
    result = result.reshape(NTV, GROUPS, TV // GROUPS, a_count, columns).transpose(0, 3, 2, 1, 4)
    return result.reshape(1, NTV, row_count, columns)


def broadcast(value, axis, source):
    kept = jnp.where(lax.axis_index(axis) == source, value, 0).astype(value.dtype)
    return lax.psum(kept, axis)


def on_device(sizes, chol, amps, listed):
    tile_count = chol.shape[0]
    if sizes == (NTV, NTV, 2) and tile_count == NTV:
        return on_square(chol, amps, listed)
    row_count = chol.shape[1]
    a_local = row_count // TV
    left_index = lax.axis_index("left")
    right_index = lax.axis_index("right")
    first_tile = right_index * tile_count
    full_vectors = lax.all_gather(chol, "left", axis=2, tiled=True)
    collected = []
    for a_tile in range(NTV):
        wanted = a_tile * NTV + left_index
        holder = wanted // tile_count
        holder_slot = wanted % tile_count
        offered = lax.dynamic_index_in_dim(full_vectors, holder_slot, 0, keepdims=False)
        collected.append(broadcast(offered, "right", holder))
    left_rows = jnp.stack(collected)
    own_c = lax.dynamic_index_in_dim(listed, left_index, 1, keepdims=False).reshape(NTV, NTV * NTV)
    live = lax.dynamic_slice_in_dim(own_c, first_tile, tile_count, 1).T.astype(jnp.float32)
    products = jnp.einsum(
        "xrq,tkq->txrk",
        left_rows,
        lax.all_gather(full_vectors, "occ", axis=1, tiled=True),
        preferred_element_type=jnp.float32,
    )
    inner = (products * live[:, :, None, None]).astype(jnp.bfloat16)
    swapped = inner.reshape(tile_count, NTV, a_local, TV, TV, TV).transpose(0, 1, 2, 4, 3, 5)
    swapped = swapped.reshape(tile_count, NTV * a_local * TV, PAIR)
    amp_columns = lax.all_gather(amps, "right", axis=3, tiled=True)
    d_first = first_tile % NTV
    own_amps = lax.dynamic_slice_in_dim(amp_columns[0], d_first, tile_count, 0)
    partial_sum = jnp.einsum(
        "trk,tkn->rn",
        swapped,
        lax.all_gather(own_amps, "occ", axis=1, tiled=True),
        preferred_element_type=jnp.float32,
    )
    partial_sum = partial_sum.reshape(NTV, row_count, NOP)
    owned_a = lax.psum_scatter(partial_sum, "left", scatter_dimension=0, tiled=True)
    b_tile = first_tile // NTV
    placed = lax.dynamic_update_slice_in_dim(
        jnp.zeros((NTV, row_count, NOP), jnp.float32), owned_a, b_tile, 0
    )
    summed = lax.psum_scatter(placed, "right", scatter_dimension=2, tiled=True)
    return summed.reshape(1, NTV, row_count, summed.shape[2])


def solution(mesh):
    placed = (P("right", "occ", "left"), P("left", None, "occ", "right"), P())
    return jax.shard_map(
        functools.partial(on_device, tuple(mesh.shape[axis] for axis in ("left", "right", "occ"))),
        mesh=mesh,
        in_specs=placed,
        out_specs=P("left", None, "occ", "right"),
        check_vma=False,
    )
```

```python
import functools

import jax
import jax.numpy as jnp
from jax import lax
from jax.experimental import pallas as pl
from jax.experimental.pallas import tpu as pltpu
from jax.sharding import PartitionSpec as P

TV = 32
NTV = 4
NOP = 512
PAIR = 1024
GROUPS = 4


def ladder_kernel(steps, count, first, half_ref, live_ref, pick_ref, tile_ref, *refs):
    lefts = [refs[s * count:(s + 1) * count] for s in range(steps)]
    rights = [refs[steps * count + 2 * s: steps * count + 2 * s + 2] for s in range(steps)]
    rest = refs[steps * (count + 2):]
    amp_ref = rest[0]
    before_ref = None if first else rest[1]
    out_ref, products, ready, gathered = rest[-4:]
    step = pl.program_id(0)
    group_rows = lefts[0][0].shape[1]
    c_part = TV // GROUPS
    a_count = group_rows // c_part
    wide = 2 * GROUPS * TV
    half_blocks = rights[0][0].shape[1] // wide

    @pl.when(step < GROUPS)
    def _():
        for t in range(count):
            for s in range(steps):
                rows = lefts[s][t][0]
                gathered[t * group_rows:(t + 1) * group_rows, s * rows.shape[1]:(s + 1) * rows.shape[1]] = rows
        for half in range(2):
            start = (half_ref[0] if half == 0 else 1 - half_ref[0]) * half_blocks
            for p in range(half_blocks):
                right = jnp.concatenate(
                    [
                        jnp.concatenate(
                            [
                                part[half][
                                    0,
                                    pl.ds(
                                        pl.multiple_of(
                                            p * wide + (g // GROUPS * GROUPS + (g + step) % GROUPS) * TV, TV
                                        ),
                                        TV,
                                    ),
                                    :,
                                ]
                                for g in range(2 * GROUPS)
                            ],
                            axis=0,
                        )
                        for part in rights
                    ],
                    axis=1,
                )
                total = lax.dot_general(
                    gathered[...], right, (((1,), (1,)), ((), ())), preferred_element_type=jnp.float32
                )
                products[step, start + p] = total.astype(jnp.bfloat16)

    @pl.when(step >= GROUPS)
    def _():
        k = step - GROUPS
        lane_group = lax.broadcasted_iota(jnp.int32, (count * group_rows, wide), 1) // TV % GROUPS
        for p in range(2 * half_blocks):
            mixed = products[k, p]
            for g in range(1, GROUPS):
                mixed = jnp.where(lane_group == g, products[(k + GROUPS - g) % GROUPS, p], mixed)
            mixed = mixed.reshape(count, c_part, a_count, wide)
            for b in range(2):
                for c in range(c_part):
                    ready[:, 2 * p + b, :, c * GROUPS * TV:(c + 1) * GROUPS * TV] = mixed[
                        :, c, :, b * GROUPS * TV:(b + 1) * GROUPS * TV
                    ]
        amp = jnp.concatenate(
            [
                amp_ref[0, pl.ds(pl.multiple_of(((k + GROUPS - g) % GROUPS * c_part + c) * TV, TV), TV), :]
                for c in range(c_part)
                for g in range(GROUPS)
            ],
            axis=0,
        )
        block_rows = TV // GROUPS * a_count
        terms = jnp.dot(
            ready[...].reshape(count * block_rows, TV * TV), amp, preferred_element_type=jnp.float32
        ).reshape(count, block_rows, amp.shape[1])
        for t in range(count):
            term = terms[t] * live_ref[t].astype(jnp.float32)
            if not first:
                term = before_ref[t, 0] + term
            out_ref[t, 0] = term.astype(out_ref.dtype)


def ladder(half, live, pick, tile, lefts, rights, amp, before, part=None, kind=jnp.float32):
    steps = len(lefts)
    rows, depth = lefts[0].shape[1:]
    columns = amp.shape[2]
    a_count = rows // TV
    b_blocks = TV // GROUPS
    wide = 2 * GROUPS * TV
    count = NTV if part is None else NTV // 2
    base = 0 if part is None else part * count
    one = pl.Buffered(1)

    def left_spec(t):
        return pl.BlockSpec(
            (1, rows // GROUPS, depth), lambda i, h, v, k, d: (k[t], jnp.minimum(i, GROUPS - 1), 0)
        )

    def right_spec(place):
        return pl.BlockSpec(
            (1, rows, depth),
            lambda i, h, v, k, d: (d[0] if place is None else place, 0, 0),
            pipeline_mode=one,
        )

    amp_spec = pl.BlockSpec((1, 2 * rows, columns), lambda i, h, v, k, d: (d[0], 0, 0), pipeline_mode=one)

    def sum_spec(place):
        return pl.BlockSpec(
            (count, 1, b_blocks * a_count, columns),
            lambda i, h, v, k, d: (place, jnp.maximum(i - GROUPS, 0), 0, 0),
        )

    first = before is None
    flops = 2 * count * rows * 2 * rows * (steps * depth + columns)
    operands = [half, live[base:base + count], pick[base:base + count], tile]
    operands += [x for x in lefts for _ in range(count)] + [x for own, other, _ in rights for x in (own, other)] + [amp]
    return pl.pallas_call(
        functools.partial(ladder_kernel, steps, count, first),
        grid_spec=pltpu.PrefetchScalarGridSpec(
            num_scalar_prefetch=4,
            grid=(2 * GROUPS,),
            in_specs=[left_spec(t) for _ in lefts for t in range(count)]
            + [right_spec(place) for _, _, place in rights for _ in range(2)]
            + [amp_spec]
            + [sum_spec(base // count)] * (not first),
            out_specs=sum_spec(0),
            scratch_shapes=[
                pltpu.VMEM((GROUPS, 2 * rows // wide, count * rows // GROUPS, wide), jnp.bfloat16),
                pltpu.VMEM((count, b_blocks, a_count, TV * TV), jnp.bfloat16),
                pltpu.VMEM((count * rows // GROUPS, steps * depth), jnp.bfloat16),
            ],
        ),
        out_shape=jax.ShapeDtypeStruct((count, GROUPS, b_blocks * a_count, columns), kind),
        input_output_aliases={} if first or part is not None else {len(operands): 0},
        compiler_params=pltpu.CompilerParams(vmem_limit_bytes=40 * 2**20),
        cost_estimate=pl.CostEstimate(flops=flops, bytes_accessed=20 * 2**20, transcendentals=0),
    )(*operands, *([] if first else [before]))


def partner(value, axis, size, flip):
    return lax.ppermute(value, axis, [(i, i ^ flip) for i in range(size)])


def shift(value, axis, size, step):
    return lax.ppermute(value, axis, [(i, (i + step) % size) for i in range(size)])


def ring_order(size):
    return list(range(0, size, 2)) + list(range(size - 1, 0, -2))


HOPS = (
    (1, 2), (1, 1), (1, 0), (2, 1), (2, 0), (3, 0),
    (1, 3), (2, 3), (2, 2), (3, 2), (3, 1), (3, 3),
)
AMP = "amp"
NEAR = {0: 0, 2: AMP, 4: 1, 6: 2, 8: 3}
FAR = {1: 0, 3: AMP, 5: 1, 7: 2, 9: 3}
STACK = {2: 0, 4: AMP, 6: 1, 8: 2, 10: 3}
CONTRACT = {10: 0, 11: 2, 12: 1}


def on_square(chol, amps, listed):
    row_count, depth = chol.shape[1:]
    columns = amps.shape[3]
    a_count = row_count // TV
    left_index = lax.axis_index("left")
    right_index = lax.axis_index("right")
    occ_index = lax.axis_index("occ")
    order = ring_order(NTV)
    ring = [(order[p], order[(p + 1) % NTV]) for p in range(NTV)]
    near = [[order[(order.index(level) + i) % NTV] for level in range(NTV)] for i in range(NTV)]

    def at_level(table):
        value = jnp.int32(table[0])
        for level in range(1, NTV):
            value = jnp.where(left_index == level, jnp.int32(table[level]), value)
        return value

    d_tiles = [at_level(table) for table in near]
    tiles = jnp.arange(NTV)
    targets = (left_index + 1 + tiles) % NTV
    pick = (targets ^ right_index).astype(jnp.int32)
    own_c = lax.dynamic_index_in_dim(listed, left_index, 1, keepdims=False)
    live = lax.dynamic_index_in_dim(own_c, right_index, 1, keepdims=False)[targets]
    half = occ_index.reshape(1)

    held = {("block", 0, i): lax.dynamic_slice_in_dim(chol, d_tiles[i], 1, 0) for i in (3, 2, 0, 1)}
    held["chol"] = chol
    held["left", AMP, 0] = amps[0]
    last = len(HOPS)
    waiting = {slot: [] for slot in range(last + 4)}

    def meet(keys):
        keys = list(dict.fromkeys(keys))
        for key, value in zip(keys, lax.optimization_barrier([held[key] for key in keys])):
            held[key] = value

    def contract(i, before, part=None, kind=jnp.float32):
        sides = [(held["chol"], held["other", "chol"], None)]
        sides += [(held["block", s, i], held["other", s, i], 0) for s in range(1, NTV)]
        return ladder(
            half,
            lax.dynamic_index_in_dim(live, d_tiles[i], 1, keepdims=False),
            pick,
            d_tiles[i].reshape(1),
            [held["lefts", s] for s in range(NTV)],
            sides,
            held["amp"],
            before,
            part,
            kind,
        )

    for slot in range(last + 1):
        hops = [0, 1] if slot == 0 else [slot + 1] if slot + 1 < last else []
        near_block, far_block, stack_block = NEAR.get(slot), FAR.get(slot), STACK.get(slot)
        now = waiting[slot]
        if slot >= 1:
            now.append(("block", *HOPS[slot - 1]))
        if near_block is not None:
            if near_block != AMP:
                own = held["block", near_block, 0].reshape(a_count, TV, depth)
                held["left", near_block, 0] = own.transpose(1, 0, 2).reshape(row_count, depth)
            now.append(("left", near_block, 0))
        if far_block is not None:
            now += [("left", far_block, flip) for flip in range(3)]
        if stack_block is not None:
            now += [("left", stack_block, "first"), ("left", stack_block, "second")]
        now += [("block", HOPS[u][0] - 1, (HOPS[u][1] + 1) % NTV) for u in hops]
        if slot == 1:
            now.append("chol")
        meet(now)
        for u in hops:
            s, i = HOPS[u]
            held["block", s, i] = lax.ppermute(held["block", s - 1, (i + 1) % NTV], "left", ring)
        if near_block is not None:
            for flip in (1, 2):
                held["left", near_block, flip] = partner(held["left", near_block, 0], "right", NTV, flip)
        if far_block is not None:
            middle = held["left", far_block, 0].shape[0] // 2
            held["left", far_block, "first"] = partner(held["left", far_block, 1][:middle], "right", NTV, 2)
            held["left", far_block, "second"] = partner(held["left", far_block, 2][middle:], "right", NTV, 1)
        if slot == 1:
            held["other", "chol"] = partner(held["chol"], "occ", 2, 1)
            waiting[slot + 1].append(("other", "chol"))
        if slot >= 1:
            unit = HOPS[slot - 1]
            held["other", *unit] = partner(held["block", *unit], "occ", 2, 1)
            waiting[slot + 1].append(("other", *unit))
        if stack_block is not None:
            every = [held["left", stack_block, flip] for flip in range(3)]
            every.append(jnp.concatenate([held["left", stack_block, half_of] for half_of in ("first", "second")]))
            if stack_block == AMP:
                held["amp"] = lax.all_gather(jnp.concatenate(every, axis=2), "occ", axis=1, tiled=True)
                waiting[slot + 3].append("amp")
            else:
                held["lefts", stack_block] = jnp.stack(every)
                waiting[slot + 1].append(("lefts", stack_block))
        if slot in CONTRACT:
            held["sum"] = contract(CONTRACT[slot], held.get("sum"))
            waiting[slot + 1].append("sum")
    partials = held["sum"]
    early = contract(3, partials, 0, jnp.bfloat16)
    moved = [shift(early[t], "left", NTV, t + 1) for t in range(NTV // 2)]
    late = contract(3, partials, 1)
    moved += [
        shift(late[t].astype(jnp.bfloat16), "left", NTV, NTV // 2 + t + 1) for t in range(NTV // 2 - 1)
    ]
    summed = late[NTV // 2 - 1]
    for piece in moved:
        summed = summed + piece.astype(jnp.float32)
    pieces = []
    for flip in range(NTV):
        piece = summed[:, :, flip * columns:(flip + 1) * columns]
        pieces.append(partner(piece, "right", NTV, flip) if flip else piece)
    result = jnp.stack(pieces)[tiles ^ right_index]
    result = result.reshape(NTV, GROUPS, TV // GROUPS, a_count, columns).transpose(0, 3, 2, 1, 4)
    return result.reshape(1, NTV, row_count, columns)


def broadcast(value, axis, source):
    kept = jnp.where(lax.axis_index(axis) == source, value, 0).astype(value.dtype)
    return lax.psum(kept, axis)


def on_device(sizes, chol, amps, listed):
    tile_count = chol.shape[0]
    if sizes == (NTV, NTV, 2) and tile_count == NTV:
        return on_square(chol, amps, listed)
    row_count = chol.shape[1]
    a_local = row_count // TV
    left_index = lax.axis_index("left")
    right_index = lax.axis_index("right")
    first_tile = right_index * tile_count
    full_vectors = lax.all_gather(chol, "left", axis=2, tiled=True)
    collected = []
    for a_tile in range(NTV):
        wanted = a_tile * NTV + left_index
        holder = wanted // tile_count
        holder_slot = wanted % tile_count
        offered = lax.dynamic_index_in_dim(full_vectors, holder_slot, 0, keepdims=False)
        collected.append(broadcast(offered, "right", holder))
    left_rows = jnp.stack(collected)
    own_c = lax.dynamic_index_in_dim(listed, left_index, 1, keepdims=False).reshape(NTV, NTV * NTV)
    live = lax.dynamic_slice_in_dim(own_c, first_tile, tile_count, 1).T.astype(jnp.float32)
    products = jnp.einsum(
        "xrq,tkq->txrk",
        left_rows,
        lax.all_gather(full_vectors, "occ", axis=1, tiled=True),
        preferred_element_type=jnp.float32,
    )
    inner = (products * live[:, :, None, None]).astype(jnp.bfloat16)
    swapped = inner.reshape(tile_count, NTV, a_local, TV, TV, TV).transpose(0, 1, 2, 4, 3, 5)
    swapped = swapped.reshape(tile_count, NTV * a_local * TV, PAIR)
    amp_columns = lax.all_gather(amps, "right", axis=3, tiled=True)
    d_first = first_tile % NTV
    own_amps = lax.dynamic_slice_in_dim(amp_columns[0], d_first, tile_count, 0)
    partial_sum = jnp.einsum(
        "trk,tkn->rn",
        swapped,
        lax.all_gather(own_amps, "occ", axis=1, tiled=True),
        preferred_element_type=jnp.float32,
    )
    partial_sum = partial_sum.reshape(NTV, row_count, NOP)
    owned_a = lax.psum_scatter(partial_sum, "left", scatter_dimension=0, tiled=True)
    b_tile = first_tile // NTV
    placed = lax.dynamic_update_slice_in_dim(
        jnp.zeros((NTV, row_count, NOP), jnp.float32), owned_a, b_tile, 0
    )
    summed = lax.psum_scatter(placed, "right", scatter_dimension=2, tiled=True)
    return summed.reshape(1, NTV, row_count, summed.shape[2])


def solution(mesh):
    placed = (P("right", "occ", "left"), P("left", None, "occ", "right"), P())
    return jax.shard_map(
        functools.partial(on_device, tuple(mesh.shape[axis] for axis in ("left", "right", "occ"))),
        mesh=mesh,
        in_specs=placed,
        out_specs=P("left", None, "occ", "right"),
        check_vma=False,
    )
```

```python
import functools

import jax
import jax.numpy as jnp
from jax import lax
from jax.experimental import pallas as pl
from jax.experimental.pallas import tpu as pltpu
from jax.sharding import PartitionSpec as P

TV = 32
NTV = 4
NOP = 512
PAIR = 1024
GROUPS = 4


def ladder_kernel(steps, count, half_ref, live_ref, pick_ref, tile_ref, *refs):
    kinds = NTV + 1
    lefts = [refs[s * kinds:(s + 1) * kinds] for s in range(steps)]
    rest = refs[steps * kinds:]
    whole, rest = rest[:2], rest[2:]
    tiles = [rest[2 * n:2 * n + 2] for n in range((steps - 1) * NTV)]
    amp_ref, out_ref, total_ref, products, ready, left_buf, right_buf, left_sem, right_sem = rest[
        2 * (steps - 1) * NTV:
    ]
    d_tile, step = pl.program_id(0), pl.program_id(1)
    rows = left_buf.shape[2]
    group_rows = rows // GROUPS
    c_part = TV // GROUPS
    a_count = group_rows // c_part
    wide = 2 * GROUPS * TV
    half_blocks = rows // wide
    block_rows = TV // GROUPS * a_count
    slot = d_tile % 2

    def right_copies(i):
        copies = []
        for s in range(steps):
            for side in range(2):
                source = whole[side].at[tile_ref[i]] if s == 0 else tiles[(s - 1) * NTV + i][side].at[0]
                place = (i % 2, s, side)
                copies.append(pltpu.make_async_copy(source, right_buf.at[place], right_sem.at[place]))
        return copies

    @pl.when((d_tile == 0) & (step == 0))
    def _():
        for t in range(count):
            for s in range(steps):
                for k in range(NTV - 1):

                    @pl.when(pick_ref[t] == k)
                    def _():
                        pltpu.make_async_copy(lefts[s][k], left_buf.at[t, s], left_sem.at[t, s]).start()

                @pl.when(pick_ref[t] == NTV - 1)
                def _():
                    for part in range(2):
                        place = pl.ds(part * (rows // 2), rows // 2)
                        pltpu.make_async_copy(
                            lefts[s][NTV - 1 + part], left_buf.at[t, s, place], left_sem.at[t, s]
                        ).start()
        for copy in right_copies(0):
            copy.start()
        for t in range(count):
            for s in range(steps):
                pltpu.make_async_copy(lefts[s][0], left_buf.at[t, s], left_sem.at[t, s]).wait()

    for i in range(NTV):

        @pl.when((d_tile == i) & (step == 0))
        def _():
            for copy in right_copies(i):
                copy.wait()
            if i + 1 < NTV:
                for copy in right_copies(i + 1):
                    copy.start()

    @pl.when(step < GROUPS)
    def _():
        group = pl.ds(pl.multiple_of(step * group_rows, group_rows), group_rows)
        for half in range(2):
            start = (half_ref[0] if half == 0 else 1 - half_ref[0]) * half_blocks
            for p in range(half_blocks):
                left = jnp.concatenate(
                    [
                        jnp.concatenate([left_buf[t, s, group, :] for s in range(steps)], axis=1)
                        for t in range(count)
                    ],
                    axis=0,
                )
                right = jnp.concatenate(
                    [
                        jnp.concatenate(
                            [
                                right_buf[
                                    slot,
                                    s,
                                    half,
                                    pl.ds(
                                        pl.multiple_of(
                                            p * wide + (g // GROUPS * GROUPS + (g + step) % GROUPS) * TV, TV
                                        ),
                                        TV,
                                    ),
                                    :,
                                ]
                                for g in range(2 * GROUPS)
                            ],
                            axis=0,
                        )
                        for s in range(steps)
                    ],
                    axis=1,
                )
                products[step, start + p] = lax.dot_general(
                    left, right, (((1,), (1,)), ((), ())), preferred_element_type=jnp.float32
                ).astype(jnp.bfloat16)

    @pl.when(step >= GROUPS)
    def _():
        k = step - GROUPS
        lane_group = lax.broadcasted_iota(jnp.int32, (count * group_rows, wide), 1) // TV % GROUPS
        for p in range(2 * half_blocks):
            mixed = products[k, p]
            for g in range(1, GROUPS):
                mixed = jnp.where(lane_group == g, products[(k + GROUPS - g) % GROUPS, p], mixed)
            mixed = mixed.reshape(count, c_part, a_count, wide)
            for b in range(2):
                for c in range(c_part):
                    ready[:, 2 * p + b, :, c * GROUPS * TV:(c + 1) * GROUPS * TV] = mixed[
                        :, c, :, b * GROUPS * TV:(b + 1) * GROUPS * TV
                    ]
        amp = jnp.concatenate(
            [
                amp_ref[0, pl.ds(pl.multiple_of(((k + GROUPS - g) % GROUPS * c_part + c) * TV, TV), TV), :]
                for c in range(c_part)
                for g in range(GROUPS)
            ],
            axis=0,
        )
        terms = jnp.dot(
            ready[...].reshape(count * block_rows, TV * TV), amp, preferred_element_type=jnp.float32
        ).reshape(count, block_rows, amp.shape[1])
        for t in range(count):
            term = terms[t] * live_ref[d_tile, t].astype(jnp.float32)

            @pl.when(d_tile == 0)
            def _():
                total_ref[t, k] = term

            @pl.when((d_tile > 0) & (d_tile < NTV - 1))
            def _():
                total_ref[t, k] += term

            @pl.when(d_tile == NTV - 1)
            def _():
                out_ref[t, k] = (total_ref[t, k] + term).astype(out_ref.dtype)


def ladder(half, live, pick, tile, lefts, whole, tiles, amp, part, kind):
    steps = len(lefts)
    rows, depth = whole[0].shape[1:]
    columns = amp.shape[2]
    a_count = rows // TV
    b_blocks = TV // GROUPS
    wide = 2 * GROUPS * TV
    count = NTV // 2
    base = part * count
    result = (count, GROUPS, b_blocks * a_count, columns)
    flops = 2 * NTV * count * rows * 2 * rows * (steps * depth + columns)
    anywhere = pl.BlockSpec(memory_space=pl.ANY)
    copied = [x for step in lefts for x in step] + [*whole] + [x for pair in tiles for x in pair]
    return pl.pallas_call(
        functools.partial(ladder_kernel, steps, count),
        grid_spec=pltpu.PrefetchScalarGridSpec(
            num_scalar_prefetch=4,
            grid=(NTV, 2 * GROUPS),
            in_specs=[anywhere] * len(copied)
            + [pl.BlockSpec((1, 2 * rows, columns), lambda i, j, h, v, k, d: (d[i], 0, 0))],
            out_specs=pl.BlockSpec(result, lambda i, j, h, v, k, d: (0, 0, 0, 0)),
            scratch_shapes=[
                pltpu.VMEM(result, jnp.float32),
                pltpu.VMEM((GROUPS, 2 * rows // wide, count * rows // GROUPS, wide), jnp.bfloat16),
                pltpu.VMEM((count, b_blocks, a_count, TV * TV), jnp.bfloat16),
                pltpu.VMEM((count, steps, rows, depth), jnp.bfloat16),
                pltpu.VMEM((2, steps, 2, rows, depth), jnp.bfloat16),
                pltpu.SemaphoreType.DMA((count, steps)),
                pltpu.SemaphoreType.DMA((2, steps, 2)),
            ],
        ),
        out_shape=jax.ShapeDtypeStruct(result, kind),
        compiler_params=pltpu.CompilerParams(vmem_limit_bytes=40 * 2**20),
        cost_estimate=pl.CostEstimate(flops=flops, bytes_accessed=28 * 2**20, transcendentals=0),
    )(half, live[:, base:base + count], pick[base:base + count], tile, *copied, amp)


def partner(value, axis, size, flip):
    return lax.ppermute(value, axis, [(i, i ^ flip) for i in range(size)])


def shift(value, axis, size, step):
    return lax.ppermute(value, axis, [(i, (i + step) % size) for i in range(size)])


def ring_order(size):
    return list(range(0, size, 2)) + list(range(size - 1, 0, -2))


HOPS = (
    (1, 2), (1, 1), (1, 0), (2, 1), (2, 0), (3, 0),
    (1, 3), (2, 3), (2, 2), (3, 2), (3, 1), (3, 3),
)
AMP = "amp"
NEAR = {0: 0, 2: AMP, 4: 1, 6: 2, 8: 3}
FAR = {1: 0, 3: AMP, 5: 1, 7: 2, 9: 3}
FAR_DONE = {2: 0, 4: AMP, 6: 1, 8: 2, 10: 3}


def on_square(chol, amps, listed):
    row_count, depth = chol.shape[1:]
    columns = amps.shape[3]
    a_count = row_count // TV
    left_index = lax.axis_index("left")
    right_index = lax.axis_index("right")
    occ_index = lax.axis_index("occ")
    order = ring_order(NTV)
    ring = [(order[p], order[(p + 1) % NTV]) for p in range(NTV)]
    near = [[order[(order.index(level) + i) % NTV] for level in range(NTV)] for i in range(NTV)]

    def at_level(table):
        value = jnp.int32(table[0])
        for level in range(1, NTV):
            value = jnp.where(left_index == level, jnp.int32(table[level]), value)
        return value

    d_tiles = [at_level(table) for table in near]
    tiles = jnp.arange(NTV)
    targets = (left_index + 1 + tiles) % NTV
    pick = (targets ^ right_index).astype(jnp.int32)
    own_c = lax.dynamic_index_in_dim(listed, left_index, 1, keepdims=False)
    live = lax.dynamic_index_in_dim(own_c, right_index, 1, keepdims=False)[targets]
    half = occ_index.reshape(1)

    held = {("block", 0, i): lax.dynamic_slice_in_dim(chol, d_tiles[i], 1, 0) for i in (3, 2, 0, 1)}
    held["chol"] = chol
    held["left", AMP, 0] = amps[0]
    last = len(HOPS)
    waiting = {slot: [] for slot in range(last + 4)}

    def meet(keys):
        keys = list(dict.fromkeys(keys))
        for key, value in zip(keys, lax.optimization_barrier([held[key] for key in keys])):
            held[key] = value

    for slot in range(last + 1):
        hops = [0, 1] if slot == 0 else [slot + 1] if slot + 1 < last else []
        near_block, far_block, done_block = NEAR.get(slot), FAR.get(slot), FAR_DONE.get(slot)
        now = waiting[slot]
        if slot >= 1:
            now.append(("block", *HOPS[slot - 1]))
        if near_block is not None:
            if near_block != AMP:
                own = held["block", near_block, 0].reshape(a_count, TV, depth)
                held["left", near_block, 0] = own.transpose(1, 0, 2).reshape(row_count, depth)
            now.append(("left", near_block, 0))
        if far_block is not None:
            now += [("left", far_block, flip) for flip in range(3)]
        if done_block is not None:
            now += [("left", done_block, "first"), ("left", done_block, "second")]
        now += [("block", HOPS[u][0] - 1, (HOPS[u][1] + 1) % NTV) for u in hops]
        if slot == 1:
            now.append("chol")
        meet(now)
        for u in hops:
            s, i = HOPS[u]
            held["block", s, i] = lax.ppermute(held["block", s - 1, (i + 1) % NTV], "left", ring)
        if near_block is not None:
            for flip in (1, 2):
                held["left", near_block, flip] = partner(held["left", near_block, 0], "right", NTV, flip)
        if far_block is not None:
            middle = held["left", far_block, 0].shape[0] // 2
            held["left", far_block, "first"] = partner(held["left", far_block, 1][:middle], "right", NTV, 2)
            held["left", far_block, "second"] = partner(held["left", far_block, 2][middle:], "right", NTV, 1)
        if slot == 1:
            held["other", "chol"] = partner(held["chol"], "occ", 2, 1)
            waiting[slot + 1].append(("other", "chol"))
        if slot >= 1:
            unit = HOPS[slot - 1]
            held["other", *unit] = partner(held["block", *unit], "occ", 2, 1)
            waiting[slot + 1].append(("other", *unit))
        if done_block == AMP:
            far = jnp.concatenate([held["left", AMP, "first"], held["left", AMP, "second"]])
            every = [held["left", AMP, flip] for flip in range(3)] + [far]
            held["amp"] = lax.all_gather(jnp.concatenate(every, axis=2), "occ", axis=1, tiled=True)
            waiting[slot + 3].append("amp")
    d_order = jnp.stack(d_tiles)
    contract = functools.partial(
        ladder,
        half,
        live[:, d_order].T,
        pick,
        d_order,
        [[held["left", s, part] for part in (0, 1, 2, "first", "second")] for s in range(NTV)],
        (held["chol"], held["other", "chol"]),
        [(held["block", s, i], held["other", s, i]) for s in range(1, NTV) for i in range(NTV)],
        held["amp"],
    )
    early = contract(0, jnp.bfloat16)
    moved = [shift(early[t], "left", NTV, t + 1) for t in range(NTV // 2)]
    late = contract(1, jnp.float32)
    moved += [
        shift(late[t].astype(jnp.bfloat16), "left", NTV, NTV // 2 + t + 1) for t in range(NTV // 2 - 1)
    ]
    summed = late[NTV // 2 - 1]
    for piece in moved:
        summed = summed + piece.astype(jnp.float32)
    pieces = []
    for flip in range(NTV):
        piece = summed[:, :, flip * columns:(flip + 1) * columns]
        pieces.append(partner(piece, "right", NTV, flip) if flip else piece)
    result = jnp.stack(pieces)[tiles ^ right_index]
    result = result.reshape(NTV, GROUPS, TV // GROUPS, a_count, columns).transpose(0, 3, 2, 1, 4)
    return result.reshape(1, NTV, row_count, columns)


def broadcast(value, axis, source):
    kept = jnp.where(lax.axis_index(axis) == source, value, 0).astype(value.dtype)
    return lax.psum(kept, axis)


def on_device(sizes, chol, amps, listed):
    tile_count = chol.shape[0]
    if sizes == (NTV, NTV, 2) and tile_count == NTV:
        return on_square(chol, amps, listed)
    row_count = chol.shape[1]
    a_local = row_count // TV
    left_index = lax.axis_index("left")
    right_index = lax.axis_index("right")
    first_tile = right_index * tile_count
    full_vectors = lax.all_gather(chol, "left", axis=2, tiled=True)
    collected = []
    for a_tile in range(NTV):
        wanted = a_tile * NTV + left_index
        holder = wanted // tile_count
        holder_slot = wanted % tile_count
        offered = lax.dynamic_index_in_dim(full_vectors, holder_slot, 0, keepdims=False)
        collected.append(broadcast(offered, "right", holder))
    left_rows = jnp.stack(collected)
    own_c = lax.dynamic_index_in_dim(listed, left_index, 1, keepdims=False).reshape(NTV, NTV * NTV)
    live = lax.dynamic_slice_in_dim(own_c, first_tile, tile_count, 1).T.astype(jnp.float32)
    products = jnp.einsum(
        "xrq,tkq->txrk",
        left_rows,
        lax.all_gather(full_vectors, "occ", axis=1, tiled=True),
        preferred_element_type=jnp.float32,
    )
    inner = (products * live[:, :, None, None]).astype(jnp.bfloat16)
    swapped = inner.reshape(tile_count, NTV, a_local, TV, TV, TV).transpose(0, 1, 2, 4, 3, 5)
    swapped = swapped.reshape(tile_count, NTV * a_local * TV, PAIR)
    amp_columns = lax.all_gather(amps, "right", axis=3, tiled=True)
    d_first = first_tile % NTV
    own_amps = lax.dynamic_slice_in_dim(amp_columns[0], d_first, tile_count, 0)
    partial_sum = jnp.einsum(
        "trk,tkn->rn",
        swapped,
        lax.all_gather(own_amps, "occ", axis=1, tiled=True),
        preferred_element_type=jnp.float32,
    )
    partial_sum = partial_sum.reshape(NTV, row_count, NOP)
    owned_a = lax.psum_scatter(partial_sum, "left", scatter_dimension=0, tiled=True)
    b_tile = first_tile // NTV
    placed = lax.dynamic_update_slice_in_dim(
        jnp.zeros((NTV, row_count, NOP), jnp.float32), owned_a, b_tile, 0
    )
    summed = lax.psum_scatter(placed, "right", scatter_dimension=2, tiled=True)
    return summed.reshape(1, NTV, row_count, summed.shape[2])


def solution(mesh):
    placed = (P("right", "occ", "left"), P("left", None, "occ", "right"), P())
    return jax.shard_map(
        functools.partial(on_device, tuple(mesh.shape[axis] for axis in ("left", "right", "occ"))),
        mesh=mesh,
        in_specs=placed,
        out_specs=P("left", None, "occ", "right"),
        check_vma=False,
    )
```

```python
import functools

import jax
import jax.numpy as jnp
from jax import lax
from jax.experimental import pallas as pl
from jax.experimental.pallas import tpu as pltpu
from jax.sharding import PartitionSpec as P

TV = 32
NTV = 4
NOP = 512
PAIR = 1024
GROUPS = 4


def ladder_kernel(steps, count, half_ref, live_ref, pick_ref, tile_ref, *refs):
    kinds = NTV + 1
    lefts = [refs[s * kinds:(s + 1) * kinds] for s in range(steps)]
    rest = refs[steps * kinds:]
    whole, rest = rest[:2], rest[2:]
    tiles = [rest[2 * n:2 * n + 2] for n in range((steps - 1) * NTV)]
    amp_ref, out_ref, total_ref, products, ready, left_buf, right_buf, left_sem, right_sem = rest[
        2 * (steps - 1) * NTV:
    ]
    d_tile, step = pl.program_id(0), pl.program_id(1)
    rows = left_buf.shape[0] // count
    depth = left_buf.shape[1] // steps
    group_rows = rows // GROUPS
    c_part = TV // GROUPS
    a_count = group_rows // c_part
    wide = 2 * GROUPS * TV
    half_blocks = rows // wide
    block_rows = TV // GROUPS * a_count
    slot = d_tile % 2

    def right_copies(i):
        copies = []
        for s in range(steps):
            for side in range(2):
                source = whole[side].at[tile_ref[i]] if s == 0 else tiles[(s - 1) * NTV + i][side].at[0]
                target = right_buf.at[i % 2, side, :, pl.ds(s * depth, depth)]
                copies.append(pltpu.make_async_copy(source, target, right_sem.at[i % 2, s, side]))
        return copies

    def left_place(t, s, first, size):
        return left_buf.at[pl.ds(t * rows + first, size), pl.ds(s * depth, depth)]

    @pl.when((d_tile == 0) & (step == 0))
    def _():
        for t in range(count):
            for s in range(steps):
                for k in range(NTV - 1):

                    @pl.when(pick_ref[t] == k)
                    def _():
                        pltpu.make_async_copy(lefts[s][k], left_place(t, s, 0, rows), left_sem.at[t, s]).start()

                @pl.when(pick_ref[t] == NTV - 1)
                def _():
                    for part in range(2):
                        target = left_place(t, s, part * (rows // 2), rows // 2)
                        pltpu.make_async_copy(lefts[s][NTV - 1 + part], target, left_sem.at[t, s]).start()
        for copy in right_copies(0):
            copy.start()
        for t in range(count):
            for s in range(steps):
                pltpu.make_async_copy(lefts[s][0], left_place(t, s, 0, rows), left_sem.at[t, s]).wait()

    for i in range(NTV):

        @pl.when((d_tile == i) & (step == 0))
        def _():
            for copy in right_copies(i):
                copy.wait()
            if i + 1 < NTV:
                for copy in right_copies(i + 1):
                    copy.start()

    @pl.when(step < GROUPS)
    def _():
        half, p = step // half_blocks, step % half_blocks
        side = jnp.where(half == 0, half_ref[0], 1 - half_ref[0])
        result = lax.dot_general(
            left_buf[...],
            right_buf[slot, half, pl.ds(pl.multiple_of(p * wide, wide), wide), :],
            (((1,), (1,)), ((), ())),
            preferred_element_type=jnp.float32,
        )
        lanes = GROUPS * TV
        for j in range(GROUPS):
            for t in range(count):
                first = t * rows + j * group_rows
                for b in range(2):
                    piece = result[first:first + group_rows, b * lanes:(b + 1) * lanes]
                    if j:
                        piece = pltpu.roll(piece, lanes - j * TV, 1)
                    products[
                        j, side * half_blocks + p, t * group_rows:(t + 1) * group_rows, b * lanes:(b + 1) * lanes
                    ] = piece.astype(jnp.bfloat16)

    @pl.when(step >= GROUPS)
    def _():
        k = step - GROUPS
        lane_group = lax.broadcasted_iota(jnp.int32, (count * group_rows, wide), 1) // TV % GROUPS
        for p in range(2 * half_blocks):
            mixed = products[k, p]
            for g in range(1, GROUPS):
                mixed = jnp.where(lane_group == g, products[(k + GROUPS - g) % GROUPS, p], mixed)
            mixed = mixed.reshape(count, c_part, a_count, wide)
            for b in range(2):
                for c in range(c_part):
                    ready[:, 2 * p + b, :, c * GROUPS * TV:(c + 1) * GROUPS * TV] = mixed[
                        :, c, :, b * GROUPS * TV:(b + 1) * GROUPS * TV
                    ]
        amp = jnp.concatenate(
            [
                amp_ref[0, pl.ds(pl.multiple_of(((k + GROUPS - g) % GROUPS * c_part + c) * TV, TV), TV), :]
                for c in range(c_part)
                for g in range(GROUPS)
            ],
            axis=0,
        )
        terms = jnp.dot(
            ready[...].reshape(count * block_rows, TV * TV), amp, preferred_element_type=jnp.float32
        ).reshape(count, block_rows, amp.shape[1])
        for t in range(count):
            term = terms[t] * live_ref[d_tile, t].astype(jnp.float32)

            @pl.when(d_tile == 0)
            def _():
                total_ref[t, k] = term

            @pl.when((d_tile > 0) & (d_tile < NTV - 1))
            def _():
                total_ref[t, k] += term

            @pl.when(d_tile == NTV - 1)
            def _():
                out_ref[t, k] = (total_ref[t, k] + term).astype(out_ref.dtype)


def ladder(half, live, pick, tile, lefts, whole, tiles, amp, part, kind):
    steps = len(lefts)
    rows, depth = whole[0].shape[1:]
    columns = amp.shape[2]
    a_count = rows // TV
    b_blocks = TV // GROUPS
    wide = 2 * GROUPS * TV
    count = NTV // 2
    base = part * count
    result = (count, GROUPS, b_blocks * a_count, columns)
    flops = 2 * NTV * count * rows * 2 * rows * (steps * depth + columns)
    anywhere = pl.BlockSpec(memory_space=pl.ANY)
    copied = [x for step in lefts for x in step] + [*whole] + [x for pair in tiles for x in pair]
    return pl.pallas_call(
        functools.partial(ladder_kernel, steps, count),
        grid_spec=pltpu.PrefetchScalarGridSpec(
            num_scalar_prefetch=4,
            grid=(NTV, 2 * GROUPS),
            in_specs=[anywhere] * len(copied)
            + [pl.BlockSpec((1, 2 * rows, columns), lambda i, j, h, v, k, d: (d[i], 0, 0))],
            out_specs=pl.BlockSpec(result, lambda i, j, h, v, k, d: (0, 0, 0, 0)),
            scratch_shapes=[
                pltpu.VMEM(result, jnp.float32),
                pltpu.VMEM((GROUPS, 2 * rows // wide, count * rows // GROUPS, wide), jnp.bfloat16),
                pltpu.VMEM((count, b_blocks, a_count, TV * TV), jnp.bfloat16),
                pltpu.VMEM((count * rows, steps * depth), jnp.bfloat16),
                pltpu.VMEM((2, 2, rows, steps * depth), jnp.bfloat16),
                pltpu.SemaphoreType.DMA((count, steps)),
                pltpu.SemaphoreType.DMA((2, steps, 2)),
            ],
        ),
        out_shape=jax.ShapeDtypeStruct(result, kind),
        compiler_params=pltpu.CompilerParams(vmem_limit_bytes=60 * 2**20),
        cost_estimate=pl.CostEstimate(flops=flops, bytes_accessed=28 * 2**20, transcendentals=0),
    )(half, live[:, base:base + count], pick[base:base + count], tile, *copied, amp)


def partner(value, axis, size, flip):
    return lax.ppermute(value, axis, [(i, i ^ flip) for i in range(size)])


def shift(value, axis, size, step):
    return lax.ppermute(value, axis, [(i, (i + step) % size) for i in range(size)])


def ring_order(size):
    return list(range(0, size, 2)) + list(range(size - 1, 0, -2))


HOPS = (
    (1, 2), (1, 1), (1, 0), (2, 1), (2, 0), (3, 0),
    (1, 3), (2, 3), (2, 2), (3, 2), (3, 1), (3, 3),
)
AMP = "amp"
NEAR = {0: 0, 2: AMP, 4: 1, 6: 2, 8: 3}
FAR = {1: 0, 3: AMP, 5: 1, 7: 2, 9: 3}
FAR_DONE = {2: 0, 4: AMP, 6: 1, 8: 2, 10: 3}


def on_square(chol, amps, listed):
    row_count, depth = chol.shape[1:]
    columns = amps.shape[3]
    a_count = row_count // TV
    left_index = lax.axis_index("left")
    right_index = lax.axis_index("right")
    occ_index = lax.axis_index("occ")
    order = ring_order(NTV)
    ring = [(order[p], order[(p + 1) % NTV]) for p in range(NTV)]
    near = [[order[(order.index(level) + i) % NTV] for level in range(NTV)] for i in range(NTV)]

    def at_level(table):
        value = jnp.int32(table[0])
        for level in range(1, NTV):
            value = jnp.where(left_index == level, jnp.int32(table[level]), value)
        return value

    d_tiles = [at_level(table) for table in near]
    tiles = jnp.arange(NTV)
    targets = (left_index + 1 + tiles) % NTV
    pick = (targets ^ right_index).astype(jnp.int32)
    own_c = lax.dynamic_index_in_dim(listed, left_index, 1, keepdims=False)
    live = lax.dynamic_index_in_dim(own_c, right_index, 1, keepdims=False)[targets]
    half = occ_index.reshape(1)

    held = {("block", 0, i): lax.dynamic_slice_in_dim(chol, d_tiles[i], 1, 0) for i in (3, 2, 0, 1)}
    held["chol"] = chol
    held["left", AMP, 0] = amps[0]
    last = len(HOPS)
    waiting = {slot: [] for slot in range(last + 4)}

    def meet(keys):
        keys = list(dict.fromkeys(keys))
        for key, value in zip(keys, lax.optimization_barrier([held[key] for key in keys])):
            held[key] = value

    for slot in range(last + 1):
        hops = [0, 1] if slot == 0 else [slot + 1] if slot + 1 < last else []
        near_block, far_block, done_block = NEAR.get(slot), FAR.get(slot), FAR_DONE.get(slot)
        now = waiting[slot]
        if slot >= 1:
            now.append(("block", *HOPS[slot - 1]))
        if near_block is not None:
            if near_block != AMP:
                own = held["block", near_block, 0].reshape(a_count, TV, depth)
                held["left", near_block, 0] = own.transpose(1, 0, 2).reshape(row_count, depth)
            now.append(("left", near_block, 0))
        if far_block is not None:
            now += [("left", far_block, flip) for flip in range(3)]
        if done_block is not None:
            now += [("left", done_block, "first"), ("left", done_block, "second")]
        now += [("block", HOPS[u][0] - 1, (HOPS[u][1] + 1) % NTV) for u in hops]
        if slot == 1:
            now.append("chol")
        meet(now)
        for u in hops:
            s, i = HOPS[u]
            held["block", s, i] = lax.ppermute(held["block", s - 1, (i + 1) % NTV], "left", ring)
        if near_block is not None:
            for flip in (1, 2):
                held["left", near_block, flip] = partner(held["left", near_block, 0], "right", NTV, flip)
        if far_block is not None:
            middle = held["left", far_block, 0].shape[0] // 2
            held["left", far_block, "first"] = partner(held["left", far_block, 1][:middle], "right", NTV, 2)
            held["left", far_block, "second"] = partner(held["left", far_block, 2][middle:], "right", NTV, 1)
        if slot == 1:
            held["other", "chol"] = partner(held["chol"], "occ", 2, 1)
            waiting[slot + 1].append(("other", "chol"))
        if slot >= 1:
            unit = HOPS[slot - 1]
            held["other", *unit] = partner(held["block", *unit], "occ", 2, 1)
            waiting[slot + 1].append(("other", *unit))
        if done_block == AMP:
            far = jnp.concatenate([held["left", AMP, "first"], held["left", AMP, "second"]])
            every = [held["left", AMP, flip] for flip in range(3)] + [far]
            held["amp"] = lax.all_gather(jnp.concatenate(every, axis=2), "occ", axis=1, tiled=True)
            waiting[slot + 3].append("amp")
    d_order = jnp.stack(d_tiles)
    contract = functools.partial(
        ladder,
        half,
        live[:, d_order].T,
        pick,
        d_order,
        [[held["left", s, part] for part in (0, 1, 2, "first", "second")] for s in range(NTV)],
        (held["chol"], held["other", "chol"]),
        [(held["block", s, i], held["other", s, i]) for s in range(1, NTV) for i in range(NTV)],
        held["amp"],
    )
    early = contract(0, jnp.bfloat16)
    moved = [shift(early[t], "left", NTV, t + 1) for t in range(NTV // 2)]
    late = contract(1, jnp.float32)
    moved += [
        shift(late[t].astype(jnp.bfloat16), "left", NTV, NTV // 2 + t + 1) for t in range(NTV // 2 - 1)
    ]
    summed = late[NTV // 2 - 1]
    for piece in moved:
        summed = summed + piece.astype(jnp.float32)
    pieces = []
    for flip in range(NTV):
        piece = summed[:, :, flip * columns:(flip + 1) * columns]
        pieces.append(partner(piece, "right", NTV, flip) if flip else piece)
    result = jnp.stack(pieces)[tiles ^ right_index]
    result = result.reshape(NTV, GROUPS, TV // GROUPS, a_count, columns).transpose(0, 3, 2, 1, 4)
    return result.reshape(1, NTV, row_count, columns)


def broadcast(value, axis, source):
    kept = jnp.where(lax.axis_index(axis) == source, value, 0).astype(value.dtype)
    return lax.psum(kept, axis)


def on_device(sizes, chol, amps, listed):
    tile_count = chol.shape[0]
    if sizes == (NTV, NTV, 2) and tile_count == NTV:
        return on_square(chol, amps, listed)
    row_count = chol.shape[1]
    a_local = row_count // TV
    left_index = lax.axis_index("left")
    right_index = lax.axis_index("right")
    first_tile = right_index * tile_count
    full_vectors = lax.all_gather(chol, "left", axis=2, tiled=True)
    collected = []
    for a_tile in range(NTV):
        wanted = a_tile * NTV + left_index
        holder = wanted // tile_count
        holder_slot = wanted % tile_count
        offered = lax.dynamic_index_in_dim(full_vectors, holder_slot, 0, keepdims=False)
        collected.append(broadcast(offered, "right", holder))
    left_rows = jnp.stack(collected)
    own_c = lax.dynamic_index_in_dim(listed, left_index, 1, keepdims=False).reshape(NTV, NTV * NTV)
    live = lax.dynamic_slice_in_dim(own_c, first_tile, tile_count, 1).T.astype(jnp.float32)
    products = jnp.einsum(
        "xrq,tkq->txrk",
        left_rows,
        lax.all_gather(full_vectors, "occ", axis=1, tiled=True),
        preferred_element_type=jnp.float32,
    )
    inner = (products * live[:, :, None, None]).astype(jnp.bfloat16)
    swapped = inner.reshape(tile_count, NTV, a_local, TV, TV, TV).transpose(0, 1, 2, 4, 3, 5)
    swapped = swapped.reshape(tile_count, NTV * a_local * TV, PAIR)
    amp_columns = lax.all_gather(amps, "right", axis=3, tiled=True)
    d_first = first_tile % NTV
    own_amps = lax.dynamic_slice_in_dim(amp_columns[0], d_first, tile_count, 0)
    partial_sum = jnp.einsum(
        "trk,tkn->rn",
        swapped,
        lax.all_gather(own_amps, "occ", axis=1, tiled=True),
        preferred_element_type=jnp.float32,
    )
    partial_sum = partial_sum.reshape(NTV, row_count, NOP)
    owned_a = lax.psum_scatter(partial_sum, "left", scatter_dimension=0, tiled=True)
    b_tile = first_tile // NTV
    placed = lax.dynamic_update_slice_in_dim(
        jnp.zeros((NTV, row_count, NOP), jnp.float32), owned_a, b_tile, 0
    )
    summed = lax.psum_scatter(placed, "right", scatter_dimension=2, tiled=True)
    return summed.reshape(1, NTV, row_count, summed.shape[2])


def solution(mesh):
    placed = (P("right", "occ", "left"), P("left", None, "occ", "right"), P())
    return jax.shard_map(
        functools.partial(on_device, tuple(mesh.shape[axis] for axis in ("left", "right", "occ"))),
        mesh=mesh,
        in_specs=placed,
        out_specs=P("left", None, "occ", "right"),
        check_vma=False,
    )
```

```python
import functools

import jax
import jax.numpy as jnp
from jax import lax
from jax.experimental import pallas as pl
from jax.experimental.pallas import tpu as pltpu
from jax.sharding import PartitionSpec as P

TV = 32
NTV = 4
NOP = 512
PAIR = 1024
GROUPS = 4


def ladder_kernel(steps, count, tile_count, first, half_ref, live_ref, pick_ref, tile_ref, *refs):
    kinds = NTV + 1
    lefts = [refs[s * kinds:(s + 1) * kinds] for s in range(steps)]
    rest = refs[steps * kinds:]
    whole, rest = rest[:2], rest[2:]
    tiles = [rest[2 * n:2 * n + 2] for n in range((steps - 1) * tile_count)]
    rest = rest[2 * (steps - 1) * tile_count:]
    amp_ref = rest[0]
    before_ref = None if first else rest[1]
    out_ref, total_ref, products, ready, left_buf, right_buf, left_sem, right_sem = rest[-8:]
    d_tile, step = pl.program_id(0), pl.program_id(1)
    rows = left_buf.shape[0] // count
    depth = left_buf.shape[1] // steps
    group_rows = rows // GROUPS
    c_part = TV // GROUPS
    a_count = group_rows // c_part
    wide = 2 * GROUPS * TV
    half_blocks = rows // wide
    block_rows = TV // GROUPS * a_count
    slot = d_tile % 2

    def right_copies(i):
        copies = []
        for s in range(steps):
            for side in range(2):
                source = whole[side].at[tile_ref[i]] if s == 0 else tiles[(s - 1) * tile_count + i][side].at[0]
                target = right_buf.at[i % 2, side, :, pl.ds(s * depth, depth)]
                copies.append(pltpu.make_async_copy(source, target, right_sem.at[i % 2, s, side]))
        return copies

    def left_place(t, s, first, size):
        return left_buf.at[pl.ds(t * rows + first, size), pl.ds(s * depth, depth)]

    @pl.when((d_tile == 0) & (step == 0))
    def _():
        for t in range(count):
            for s in range(steps):
                for k in range(NTV - 1):

                    @pl.when(pick_ref[t] == k)
                    def _():
                        pltpu.make_async_copy(lefts[s][k], left_place(t, s, 0, rows), left_sem.at[t, s]).start()

                @pl.when(pick_ref[t] == NTV - 1)
                def _():
                    for part in range(2):
                        target = left_place(t, s, part * (rows // 2), rows // 2)
                        pltpu.make_async_copy(lefts[s][NTV - 1 + part], target, left_sem.at[t, s]).start()
        for copy in right_copies(0):
            copy.start()
        for t in range(count):
            for s in range(steps):
                pltpu.make_async_copy(lefts[s][0], left_place(t, s, 0, rows), left_sem.at[t, s]).wait()

    for i in range(tile_count):

        @pl.when((d_tile == i) & (step == 0))
        def _():
            for copy in right_copies(i):
                copy.wait()
            if i + 1 < tile_count:
                for copy in right_copies(i + 1):
                    copy.start()

    @pl.when(step < GROUPS)
    def _():
        left = jnp.concatenate(
            [
                left_buf[pl.ds(pl.multiple_of(t * rows + step * group_rows, group_rows), group_rows), :]
                for t in range(count)
            ],
            axis=0,
        )
        for half in range(2):
            start = (half_ref[0] if half == 0 else 1 - half_ref[0]) * half_blocks
            for p in range(half_blocks):
                right = jnp.concatenate(
                    [
                        right_buf[
                            slot,
                            half,
                            pl.ds(
                                pl.multiple_of(
                                    p * wide + (g // GROUPS * GROUPS + (g + step) % GROUPS) * TV, TV
                                ),
                                TV,
                            ),
                            :,
                        ]
                        for g in range(2 * GROUPS)
                    ],
                    axis=0,
                )
                products[step, start + p] = lax.dot_general(
                    left, right, (((1,), (1,)), ((), ())), preferred_element_type=jnp.float32
                ).astype(jnp.bfloat16)

    @pl.when(step >= GROUPS)
    def _():
        k = step - GROUPS
        lane_group = lax.broadcasted_iota(jnp.int32, (count * group_rows, wide), 1) // TV % GROUPS
        for p in range(2 * half_blocks):
            mixed = products[k, p]
            for g in range(1, GROUPS):
                mixed = jnp.where(lane_group == g, products[(k + GROUPS - g) % GROUPS, p], mixed)
            mixed = mixed.reshape(count, c_part, a_count, wide)
            for b in range(2):
                for c in range(c_part):
                    ready[:, 2 * p + b, :, c * GROUPS * TV:(c + 1) * GROUPS * TV] = mixed[
                        :, c, :, b * GROUPS * TV:(b + 1) * GROUPS * TV
                    ]
        amp = jnp.concatenate(
            [
                amp_ref[0, pl.ds(pl.multiple_of(((k + GROUPS - g) % GROUPS * c_part + c) * TV, TV), TV), :]
                for c in range(c_part)
                for g in range(GROUPS)
            ],
            axis=0,
        )
        terms = jnp.dot(
            ready[...].reshape(count * block_rows, TV * TV), amp, preferred_element_type=jnp.float32
        ).reshape(count, block_rows, amp.shape[1])
        for t in range(count):
            term = terms[t] * live_ref[d_tile, t].astype(jnp.float32)

            @pl.when(d_tile == 0)
            def _():
                total_ref[t, k] = term if first else before_ref[t, k] + term

            @pl.when((d_tile > 0) & (d_tile < tile_count - 1))
            def _():
                total_ref[t, k] += term

            @pl.when(d_tile == tile_count - 1)
            def _():
                out_ref[t, k] = (total_ref[t, k] + term).astype(out_ref.dtype)


def ladder(half, live, pick, tile, lefts, whole, tiles, amp, before, part, kind):
    steps = len(lefts)
    rows, depth = whole[0].shape[1:]
    columns = amp.shape[2]
    a_count = rows // TV
    b_blocks = TV // GROUPS
    wide = 2 * GROUPS * TV
    tile_count = live.shape[0]
    first = before is None
    count = NTV if first else NTV // 2
    base = part * count
    result = (count, GROUPS, b_blocks * a_count, columns)
    flops = 2 * tile_count * count * rows * 2 * rows * (steps * depth + columns)
    anywhere = pl.BlockSpec(memory_space=pl.ANY)
    copied = [x for step in lefts for x in step] + [*whole] + [x for pair in tiles for x in pair]
    return pl.pallas_call(
        functools.partial(ladder_kernel, steps, count, tile_count, first),
        grid_spec=pltpu.PrefetchScalarGridSpec(
            num_scalar_prefetch=4,
            grid=(tile_count, 2 * GROUPS),
            in_specs=[anywhere] * len(copied)
            + [pl.BlockSpec((1, 2 * rows, columns), lambda i, j, h, v, k, d: (d[i], 0, 0))]
            + [
                pl.BlockSpec(result, lambda i, j, h, v, k, d: (part, 0, 0, 0), pipeline_mode=pl.Buffered(1))
            ]
            * (not first),
            out_specs=pl.BlockSpec(result, lambda i, j, h, v, k, d: (0, 0, 0, 0)),
            scratch_shapes=[
                pltpu.VMEM(result, jnp.float32),
                pltpu.VMEM((GROUPS, 2 * rows // wide, count * rows // GROUPS, wide), jnp.bfloat16),
                pltpu.VMEM((count, b_blocks, a_count, TV * TV), jnp.bfloat16),
                pltpu.VMEM((count * rows, steps * depth), jnp.bfloat16),
                pltpu.VMEM((2, 2, rows, steps * depth), jnp.bfloat16),
                pltpu.SemaphoreType.DMA((count, steps)),
                pltpu.SemaphoreType.DMA((2, steps, 2)),
            ],
        ),
        out_shape=jax.ShapeDtypeStruct(result, kind),
        compiler_params=pltpu.CompilerParams(vmem_limit_bytes=60 * 2**20),
        cost_estimate=pl.CostEstimate(flops=flops, bytes_accessed=28 * 2**20, transcendentals=0),
    )(half, live[:, base:base + count], pick[base:base + count], tile, *copied, amp, *([] if first else [before]))


def partner(value, axis, size, flip):
    return lax.ppermute(value, axis, [(i, i ^ flip) for i in range(size)])


def shift(value, axis, size, step):
    return lax.ppermute(value, axis, [(i, (i + step) % size) for i in range(size)])


def ring_order(size):
    return list(range(0, size, 2)) + list(range(size - 1, 0, -2))


HOPS = (
    (1, 2), (1, 1), (1, 0), (2, 1), (2, 0), (3, 0),
    (1, 3), (2, 3), (2, 2), (3, 2), (3, 1), (3, 3),
)
AMP = "amp"
NEAR = {0: 0, 2: AMP, 4: 1, 6: 2, 8: 3}
FAR = {1: 0, 3: AMP, 5: 1, 7: 2, 9: 3}
FAR_DONE = {2: 0, 4: AMP, 6: 1, 8: 2, 10: 3}


def on_square(chol, amps, listed):
    row_count, depth = chol.shape[1:]
    columns = amps.shape[3]
    a_count = row_count // TV
    left_index = lax.axis_index("left")
    right_index = lax.axis_index("right")
    occ_index = lax.axis_index("occ")
    order = ring_order(NTV)
    ring = [(order[p], order[(p + 1) % NTV]) for p in range(NTV)]
    near = [[order[(order.index(level) + i) % NTV] for level in range(NTV)] for i in range(NTV)]

    def at_level(table):
        value = jnp.int32(table[0])
        for level in range(1, NTV):
            value = jnp.where(left_index == level, jnp.int32(table[level]), value)
        return value

    d_tiles = [at_level(table) for table in near]
    tiles = jnp.arange(NTV)
    targets = (left_index + 1 + tiles) % NTV
    pick = (targets ^ right_index).astype(jnp.int32)
    own_c = lax.dynamic_index_in_dim(listed, left_index, 1, keepdims=False)
    live = lax.dynamic_index_in_dim(own_c, right_index, 1, keepdims=False)[targets]
    half = occ_index.reshape(1)

    held = {("block", 0, i): lax.dynamic_slice_in_dim(chol, d_tiles[i], 1, 0) for i in (3, 2, 0, 1)}
    held["chol"] = chol
    held["left", AMP, 0] = amps[0]
    last = len(HOPS)
    waiting = {slot: [] for slot in range(last + 4)}

    def meet(keys):
        keys = list(dict.fromkeys(keys))
        for key, value in zip(keys, lax.optimization_barrier([held[key] for key in keys])):
            held[key] = value

    def contract(chosen, before, part, kind):
        d_order = jnp.stack([d_tiles[i] for i in chosen])
        return ladder(
            half,
            live[:, d_order].T,
            pick,
            d_order,
            [[held["left", s, piece] for piece in (0, 1, 2, "first", "second")] for s in range(NTV)],
            (held["chol"], held["other", "chol"]),
            [(held["block", s, i], held["other", s, i]) for s in range(1, NTV) for i in chosen],
            held["amp"],
            before,
            part,
            kind,
        )

    for slot in range(last + 1):
        hops = [0, 1] if slot == 0 else [slot + 1] if slot + 1 < last else []
        near_block, far_block, done_block = NEAR.get(slot), FAR.get(slot), FAR_DONE.get(slot)
        now = waiting[slot]
        if slot >= 1:
            now.append(("block", *HOPS[slot - 1]))
        if near_block is not None:
            if near_block != AMP:
                own = held["block", near_block, 0].reshape(a_count, TV, depth)
                held["left", near_block, 0] = own.transpose(1, 0, 2).reshape(row_count, depth)
            now.append(("left", near_block, 0))
        if far_block is not None:
            now += [("left", far_block, flip) for flip in range(3)]
        if done_block is not None:
            now += [("left", done_block, "first"), ("left", done_block, "second")]
        now += [("block", HOPS[u][0] - 1, (HOPS[u][1] + 1) % NTV) for u in hops]
        if slot == 1:
            now.append("chol")
        meet(now)
        for u in hops:
            s, i = HOPS[u]
            held["block", s, i] = lax.ppermute(held["block", s - 1, (i + 1) % NTV], "left", ring)
        if near_block is not None:
            for flip in (1, 2):
                held["left", near_block, flip] = partner(held["left", near_block, 0], "right", NTV, flip)
        if far_block is not None:
            middle = held["left", far_block, 0].shape[0] // 2
            held["left", far_block, "first"] = partner(held["left", far_block, 1][:middle], "right", NTV, 2)
            held["left", far_block, "second"] = partner(held["left", far_block, 2][middle:], "right", NTV, 1)
        if slot == 1:
            held["other", "chol"] = partner(held["chol"], "occ", 2, 1)
            waiting[slot + 1].append(("other", "chol"))
        if slot >= 1:
            unit = HOPS[slot - 1]
            held["other", *unit] = partner(held["block", *unit], "occ", 2, 1)
            waiting[slot + 1].append(("other", *unit))
        if done_block == AMP:
            far = jnp.concatenate([held["left", AMP, "first"], held["left", AMP, "second"]])
            every = [held["left", AMP, flip] for flip in range(3)] + [far]
            held["amp"] = lax.all_gather(jnp.concatenate(every, axis=2), "occ", axis=1, tiled=True)
            waiting[slot + 3].append("amp")
        if slot == last - 1:
            held["sum"] = contract((0, 2), None, 0, jnp.float32)
            waiting[slot + 1].append("sum")
    early = contract((1, 3), held["sum"], 0, jnp.bfloat16)
    moved = [shift(early[t], "left", NTV, t + 1) for t in range(NTV // 2)]
    late = contract((1, 3), held["sum"], 1, jnp.float32)
    moved += [
        shift(late[t].astype(jnp.bfloat16), "left", NTV, NTV // 2 + t + 1) for t in range(NTV // 2 - 1)
    ]
    summed = late[NTV // 2 - 1]
    for piece in moved:
        summed = summed + piece.astype(jnp.float32)
    pieces = []
    for flip in range(NTV):
        piece = summed[:, :, flip * columns:(flip + 1) * columns]
        pieces.append(partner(piece, "right", NTV, flip) if flip else piece)
    result = jnp.stack(pieces)[tiles ^ right_index]
    result = result.reshape(NTV, GROUPS, TV // GROUPS, a_count, columns).transpose(0, 3, 2, 1, 4)
    return result.reshape(1, NTV, row_count, columns)


def broadcast(value, axis, source):
    kept = jnp.where(lax.axis_index(axis) == source, value, 0).astype(value.dtype)
    return lax.psum(kept, axis)


def on_device(sizes, chol, amps, listed):
    tile_count = chol.shape[0]
    if sizes == (NTV, NTV, 2) and tile_count == NTV:
        return on_square(chol, amps, listed)
    row_count = chol.shape[1]
    a_local = row_count // TV
    left_index = lax.axis_index("left")
    right_index = lax.axis_index("right")
    first_tile = right_index * tile_count
    full_vectors = lax.all_gather(chol, "left", axis=2, tiled=True)
    collected = []
    for a_tile in range(NTV):
        wanted = a_tile * NTV + left_index
        holder = wanted // tile_count
        holder_slot = wanted % tile_count
        offered = lax.dynamic_index_in_dim(full_vectors, holder_slot, 0, keepdims=False)
        collected.append(broadcast(offered, "right", holder))
    left_rows = jnp.stack(collected)
    own_c = lax.dynamic_index_in_dim(listed, left_index, 1, keepdims=False).reshape(NTV, NTV * NTV)
    live = lax.dynamic_slice_in_dim(own_c, first_tile, tile_count, 1).T.astype(jnp.float32)
    products = jnp.einsum(
        "xrq,tkq->txrk",
        left_rows,
        lax.all_gather(full_vectors, "occ", axis=1, tiled=True),
        preferred_element_type=jnp.float32,
    )
    inner = (products * live[:, :, None, None]).astype(jnp.bfloat16)
    swapped = inner.reshape(tile_count, NTV, a_local, TV, TV, TV).transpose(0, 1, 2, 4, 3, 5)
    swapped = swapped.reshape(tile_count, NTV * a_local * TV, PAIR)
    amp_columns = lax.all_gather(amps, "right", axis=3, tiled=True)
    d_first = first_tile % NTV
    own_amps = lax.dynamic_slice_in_dim(amp_columns[0], d_first, tile_count, 0)
    partial_sum = jnp.einsum(
        "trk,tkn->rn",
        swapped,
        lax.all_gather(own_amps, "occ", axis=1, tiled=True),
        preferred_element_type=jnp.float32,
    )
    partial_sum = partial_sum.reshape(NTV, row_count, NOP)
    owned_a = lax.psum_scatter(partial_sum, "left", scatter_dimension=0, tiled=True)
    b_tile = first_tile // NTV
    placed = lax.dynamic_update_slice_in_dim(
        jnp.zeros((NTV, row_count, NOP), jnp.float32), owned_a, b_tile, 0
    )
    summed = lax.psum_scatter(placed, "right", scatter_dimension=2, tiled=True)
    return summed.reshape(1, NTV, row_count, summed.shape[2])


def solution(mesh):
    placed = (P("right", "occ", "left"), P("left", None, "occ", "right"), P())
    return jax.shard_map(
        functools.partial(on_device, tuple(mesh.shape[axis] for axis in ("left", "right", "occ"))),
        mesh=mesh,
        in_specs=placed,
        out_specs=P("left", None, "occ", "right"),
        check_vma=False,
    )
```

```python
import functools

import jax
import jax.numpy as jnp
from jax import lax
from jax.experimental import pallas as pl
from jax.experimental.pallas import tpu as pltpu
from jax.sharding import PartitionSpec as P

TV = 32
NTV = 4
NOP = 512
PAIR = 1024
GROUPS = 4


def ladder_kernel(steps, count, tile_count, first, half_ref, live_ref, pick_ref, tile_ref, *refs):
    kinds = NTV + 1
    lefts = [refs[s * kinds:(s + 1) * kinds] for s in range(steps)]
    rest = refs[steps * kinds:]
    whole, rest = rest[:2], rest[2:]
    tiles = [rest[2 * n:2 * n + 2] for n in range((steps - 1) * tile_count)]
    rest = rest[2 * (steps - 1) * tile_count:]
    amp_ref = rest[0]
    before_ref = None if first else rest[1]
    out_ref, total_ref, products, ready, left_buf, right_buf, left_sem, right_sem = rest[-8:]
    d_tile, step = pl.program_id(0), pl.program_id(1)
    rows = left_buf.shape[0] // count
    depth = left_buf.shape[1] // steps
    group_rows = rows // GROUPS
    c_part = TV // GROUPS
    a_count = group_rows // c_part
    wide = 2 * GROUPS * TV
    half_blocks = rows // wide
    block_rows = TV // GROUPS * a_count
    slot = d_tile % 2

    def right_copies(i):
        copies = []
        for s in range(steps):
            for side in range(2):
                source = whole[side].at[tile_ref[i]] if s == 0 else tiles[(s - 1) * tile_count + i][side].at[0]
                target = right_buf.at[i % 2, side, :, pl.ds(s * depth, depth)]
                copies.append(pltpu.make_async_copy(source, target, right_sem.at[i % 2, s, side]))
        return copies

    def left_place(t, s, first, size):
        return left_buf.at[pl.ds(t * rows + first, size), pl.ds(s * depth, depth)]

    @pl.when((d_tile == 0) & (step == 0))
    def _():
        for t in range(count):
            for s in range(steps):
                for k in range(NTV - 1):

                    @pl.when(pick_ref[t] == k)
                    def _():
                        pltpu.make_async_copy(lefts[s][k], left_place(t, s, 0, rows), left_sem.at[t, s]).start()

                @pl.when(pick_ref[t] == NTV - 1)
                def _():
                    for part in range(2):
                        target = left_place(t, s, part * (rows // 2), rows // 2)
                        pltpu.make_async_copy(lefts[s][NTV - 1 + part], target, left_sem.at[t, s]).start()
        for copy in right_copies(0):
            copy.start()
        for t in range(count):
            for s in range(steps):
                pltpu.make_async_copy(lefts[s][0], left_place(t, s, 0, rows), left_sem.at[t, s]).wait()

    for i in range(tile_count):

        @pl.when((d_tile == i) & (step == 0))
        def _():
            for copy in right_copies(i):
                copy.wait()
            if i + 1 < tile_count:
                for copy in right_copies(i + 1):
                    copy.start()

    @pl.when(step < GROUPS)
    def _():
        left = jnp.concatenate(
            [
                left_buf[pl.ds(pl.multiple_of(t * rows + step * group_rows, group_rows), group_rows), :]
                for t in range(count)
            ],
            axis=0,
        )
        for half in range(2):
            start = (half_ref[0] if half == 0 else 1 - half_ref[0]) * half_blocks
            for p in range(half_blocks):
                right = jnp.concatenate(
                    [
                        right_buf[
                            slot,
                            half,
                            pl.ds(
                                pl.multiple_of(
                                    p * wide + (g // GROUPS * GROUPS + (g + step) % GROUPS) * TV, TV
                                ),
                                TV,
                            ),
                            :,
                        ]
                        for g in range(2 * GROUPS)
                    ],
                    axis=0,
                )
                products[step, start + p] = lax.dot_general(
                    left, right, (((1,), (1,)), ((), ())), preferred_element_type=jnp.float32
                ).astype(jnp.bfloat16)

    @pl.when(step >= GROUPS)
    def _():
        k = step - GROUPS
        lane_group = lax.broadcasted_iota(jnp.int32, (a_count, wide), 1) // TV % GROUPS
        masks = [lane_group == g for g in range(GROUPS)]
        lanes = GROUPS * TV
        for p in range(2 * half_blocks):
            for t in range(count):
                for c in range(c_part):
                    place = pl.ds(t * group_rows + c * a_count, a_count)
                    mixed = products[k, p, place, :]
                    for g in range(1, GROUPS):
                        mixed = jnp.where(masks[g], products[(k + GROUPS - g) % GROUPS, p, place, :], mixed)
                    for b in range(2):
                        ready[t, 2 * p + b, :, c * lanes:(c + 1) * lanes] = mixed[:, b * lanes:(b + 1) * lanes]
        amp = jnp.concatenate(
            [
                amp_ref[0, pl.ds(pl.multiple_of(((k + GROUPS - g) % GROUPS * c_part + c) * TV, TV), TV), :]
                for c in range(c_part)
                for g in range(GROUPS)
            ],
            axis=0,
        )
        terms = jnp.dot(
            ready[...].reshape(count * block_rows, TV * TV), amp, preferred_element_type=jnp.float32
        ).reshape(count, block_rows, amp.shape[1])
        for t in range(count):
            term = terms[t] * live_ref[d_tile, t].astype(jnp.float32)

            @pl.when(d_tile == 0)
            def _():
                total_ref[t, k] = term if first else before_ref[t, k] + term

            @pl.when((d_tile > 0) & (d_tile < tile_count - 1))
            def _():
                total_ref[t, k] += term

            @pl.when(d_tile == tile_count - 1)
            def _():
                out_ref[t, k] = (total_ref[t, k] + term).astype(out_ref.dtype)


def ladder(half, live, pick, tile, lefts, whole, tiles, amp, before, part, kind):
    steps = len(lefts)
    rows, depth = whole[0].shape[1:]
    columns = amp.shape[2]
    a_count = rows // TV
    b_blocks = TV // GROUPS
    wide = 2 * GROUPS * TV
    tile_count = live.shape[0]
    first = before is None
    count = NTV if first else NTV // 2
    base = part * count
    result = (count, GROUPS, b_blocks * a_count, columns)
    flops = 2 * tile_count * count * rows * 2 * rows * (steps * depth + columns)
    anywhere = pl.BlockSpec(memory_space=pl.ANY)
    copied = [x for step in lefts for x in step] + [*whole] + [x for pair in tiles for x in pair]
    return pl.pallas_call(
        functools.partial(ladder_kernel, steps, count, tile_count, first),
        grid_spec=pltpu.PrefetchScalarGridSpec(
            num_scalar_prefetch=4,
            grid=(tile_count, 2 * GROUPS),
            in_specs=[anywhere] * len(copied)
            + [pl.BlockSpec((1, 2 * rows, columns), lambda i, j, h, v, k, d: (d[i], 0, 0))]
            + [
                pl.BlockSpec(result, lambda i, j, h, v, k, d: (part, 0, 0, 0), pipeline_mode=pl.Buffered(1))
            ]
            * (not first),
            out_specs=pl.BlockSpec(result, lambda i, j, h, v, k, d: (0, 0, 0, 0)),
            scratch_shapes=[
                pltpu.VMEM(result, jnp.float32),
                pltpu.VMEM((GROUPS, 2 * rows // wide, count * rows // GROUPS, wide), jnp.bfloat16),
                pltpu.VMEM((count, b_blocks, a_count, TV * TV), jnp.bfloat16),
                pltpu.VMEM((count * rows, steps * depth), jnp.bfloat16),
                pltpu.VMEM((2, 2, rows, steps * depth), jnp.bfloat16),
                pltpu.SemaphoreType.DMA((count, steps)),
                pltpu.SemaphoreType.DMA((2, steps, 2)),
            ],
        ),
        out_shape=jax.ShapeDtypeStruct(result, kind),
        compiler_params=pltpu.CompilerParams(vmem_limit_bytes=60 * 2**20),
        cost_estimate=pl.CostEstimate(flops=flops, bytes_accessed=28 * 2**20, transcendentals=0),
    )(half, live[:, base:base + count], pick[base:base + count], tile, *copied, amp, *([] if first else [before]))


def partner(value, axis, size, flip):
    return lax.ppermute(value, axis, [(i, i ^ flip) for i in range(size)])


def shift(value, axis, size, step):
    return lax.ppermute(value, axis, [(i, (i + step) % size) for i in range(size)])


def ring_order(size):
    return list(range(0, size, 2)) + list(range(size - 1, 0, -2))


HOPS = (
    (1, 2), (1, 1), (1, 0), (2, 1), (2, 0), (3, 0),
    (1, 3), (2, 3), (2, 2), (3, 2), (3, 1), (3, 3),
)
AMP = "amp"
NEAR = {0: 0, 2: AMP, 4: 1, 6: 2, 8: 3}
FAR = {1: 0, 3: AMP, 5: 1, 7: 2, 9: 3}
FAR_DONE = {2: 0, 4: AMP, 6: 1, 8: 2, 10: 3}


def on_square(chol, amps, listed):
    row_count, depth = chol.shape[1:]
    columns = amps.shape[3]
    a_count = row_count // TV
    left_index = lax.axis_index("left")
    right_index = lax.axis_index("right")
    occ_index = lax.axis_index("occ")
    order = ring_order(NTV)
    ring = [(order[p], order[(p + 1) % NTV]) for p in range(NTV)]
    near = [[order[(order.index(level) + i) % NTV] for level in range(NTV)] for i in range(NTV)]

    def at_level(table):
        value = jnp.int32(table[0])
        for level in range(1, NTV):
            value = jnp.where(left_index == level, jnp.int32(table[level]), value)
        return value

    d_tiles = [at_level(table) for table in near]
    tiles = jnp.arange(NTV)
    targets = (left_index + 1 + tiles) % NTV
    pick = (targets ^ right_index).astype(jnp.int32)
    own_c = lax.dynamic_index_in_dim(listed, left_index, 1, keepdims=False)
    live = lax.dynamic_index_in_dim(own_c, right_index, 1, keepdims=False)[targets]
    half = occ_index.reshape(1)

    held = {("block", 0, i): lax.dynamic_slice_in_dim(chol, d_tiles[i], 1, 0) for i in (3, 2, 0, 1)}
    held["chol"] = chol
    held["left", AMP, 0] = amps[0]
    last = len(HOPS)
    waiting = {slot: [] for slot in range(last + 4)}

    def meet(keys):
        keys = list(dict.fromkeys(keys))
        for key, value in zip(keys, lax.optimization_barrier([held[key] for key in keys])):
            held[key] = value

    def contract(chosen, before, part, kind):
        d_order = jnp.stack([d_tiles[i] for i in chosen])
        return ladder(
            half,
            live[:, d_order].T,
            pick,
            d_order,
            [[held["left", s, piece] for piece in (0, 1, 2, "first", "second")] for s in range(NTV)],
            (held["chol"], held["other", "chol"]),
            [(held["block", s, i], held["other", s, i]) for s in range(1, NTV) for i in chosen],
            held["amp"],
            before,
            part,
            kind,
        )

    for slot in range(last + 1):
        hops = [0, 1] if slot == 0 else [slot + 1] if slot + 1 < last else []
        near_block, far_block, done_block = NEAR.get(slot), FAR.get(slot), FAR_DONE.get(slot)
        now = waiting[slot]
        if slot >= 1:
            now.append(("block", *HOPS[slot - 1]))
        if near_block is not None:
            if near_block != AMP:
                own = held["block", near_block, 0].reshape(a_count, TV, depth)
                held["left", near_block, 0] = own.transpose(1, 0, 2).reshape(row_count, depth)
            now.append(("left", near_block, 0))
        if far_block is not None:
            now += [("left", far_block, flip) for flip in range(3)]
        if done_block is not None:
            now += [("left", done_block, "first"), ("left", done_block, "second")]
        now += [("block", HOPS[u][0] - 1, (HOPS[u][1] + 1) % NTV) for u in hops]
        if slot == 1:
            now.append("chol")
        meet(now)
        for u in hops:
            s, i = HOPS[u]
            held["block", s, i] = lax.ppermute(held["block", s - 1, (i + 1) % NTV], "left", ring)
        if near_block is not None:
            for flip in (1, 2):
                held["left", near_block, flip] = partner(held["left", near_block, 0], "right", NTV, flip)
        if far_block is not None:
            middle = held["left", far_block, 0].shape[0] // 2
            held["left", far_block, "first"] = partner(held["left", far_block, 1][:middle], "right", NTV, 2)
            held["left", far_block, "second"] = partner(held["left", far_block, 2][middle:], "right", NTV, 1)
        if slot == 1:
            held["other", "chol"] = partner(held["chol"], "occ", 2, 1)
            waiting[slot + 1].append(("other", "chol"))
        if slot >= 1:
            unit = HOPS[slot - 1]
            held["other", *unit] = partner(held["block", *unit], "occ", 2, 1)
            waiting[slot + 1].append(("other", *unit))
        if done_block == AMP:
            far = jnp.concatenate([held["left", AMP, "first"], held["left", AMP, "second"]])
            every = [held["left", AMP, flip] for flip in range(3)] + [far]
            held["amp"] = lax.all_gather(jnp.concatenate(every, axis=2), "occ", axis=1, tiled=True)
            waiting[slot + 3].append("amp")
        if slot == last - 1:
            held["sum"] = contract((0, 2), None, 0, jnp.float32)
            waiting[slot + 1].append("sum")
    early = contract((1, 3), held["sum"], 0, jnp.bfloat16)
    moved = [shift(early[t], "left", NTV, t + 1) for t in range(NTV // 2)]
    late = contract((1, 3), held["sum"], 1, jnp.float32)
    moved += [
        shift(late[t].astype(jnp.bfloat16), "left", NTV, NTV // 2 + t + 1) for t in range(NTV // 2 - 1)
    ]
    summed = late[NTV // 2 - 1]
    for piece in moved:
        summed = summed + piece.astype(jnp.float32)
    pieces = []
    for flip in range(NTV):
        piece = summed[:, :, flip * columns:(flip + 1) * columns]
        if flip:
            piece = partner(piece.astype(jnp.bfloat16), "right", NTV, flip).astype(jnp.float32)
        pieces.append(piece)
    result = jnp.stack(pieces)[tiles ^ right_index]
    result = result.reshape(NTV, GROUPS, TV // GROUPS, a_count, columns).transpose(0, 3, 2, 1, 4)
    return result.reshape(1, NTV, row_count, columns)


def broadcast(value, axis, source):
    kept = jnp.where(lax.axis_index(axis) == source, value, 0).astype(value.dtype)
    return lax.psum(kept, axis)


def on_device(sizes, chol, amps, listed):
    tile_count = chol.shape[0]
    if sizes == (NTV, NTV, 2) and tile_count == NTV:
        return on_square(chol, amps, listed)
    row_count = chol.shape[1]
    a_local = row_count // TV
    left_index = lax.axis_index("left")
    right_index = lax.axis_index("right")
    first_tile = right_index * tile_count
    full_vectors = lax.all_gather(chol, "left", axis=2, tiled=True)
    collected = []
    for a_tile in range(NTV):
        wanted = a_tile * NTV + left_index
        holder = wanted // tile_count
        holder_slot = wanted % tile_count
        offered = lax.dynamic_index_in_dim(full_vectors, holder_slot, 0, keepdims=False)
        collected.append(broadcast(offered, "right", holder))
    left_rows = jnp.stack(collected)
    own_c = lax.dynamic_index_in_dim(listed, left_index, 1, keepdims=False).reshape(NTV, NTV * NTV)
    live = lax.dynamic_slice_in_dim(own_c, first_tile, tile_count, 1).T.astype(jnp.float32)
    products = jnp.einsum(
        "xrq,tkq->txrk",
        left_rows,
        lax.all_gather(full_vectors, "occ", axis=1, tiled=True),
        preferred_element_type=jnp.float32,
    )
    inner = (products * live[:, :, None, None]).astype(jnp.bfloat16)
    swapped = inner.reshape(tile_count, NTV, a_local, TV, TV, TV).transpose(0, 1, 2, 4, 3, 5)
    swapped = swapped.reshape(tile_count, NTV * a_local * TV, PAIR)
    amp_columns = lax.all_gather(amps, "right", axis=3, tiled=True)
    d_first = first_tile % NTV
    own_amps = lax.dynamic_slice_in_dim(amp_columns[0], d_first, tile_count, 0)
    partial_sum = jnp.einsum(
        "trk,tkn->rn",
        swapped,
        lax.all_gather(own_amps, "occ", axis=1, tiled=True),
        preferred_element_type=jnp.float32,
    )
    partial_sum = partial_sum.reshape(NTV, row_count, NOP)
    owned_a = lax.psum_scatter(partial_sum, "left", scatter_dimension=0, tiled=True)
    b_tile = first_tile // NTV
    placed = lax.dynamic_update_slice_in_dim(
        jnp.zeros((NTV, row_count, NOP), jnp.float32), owned_a, b_tile, 0
    )
    summed = lax.psum_scatter(placed, "right", scatter_dimension=2, tiled=True)
    return summed.reshape(1, NTV, row_count, summed.shape[2])


def solution(mesh):
    placed = (P("right", "occ", "left"), P("left", None, "occ", "right"), P())
    return jax.shard_map(
        functools.partial(on_device, tuple(mesh.shape[axis] for axis in ("left", "right", "occ"))),
        mesh=mesh,
        in_specs=placed,
        out_specs=P("left", None, "occ", "right"),
        check_vma=False,
    )
```

```python
import functools

import jax
import jax.numpy as jnp
from jax import lax
from jax.experimental import pallas as pl
from jax.experimental.pallas import tpu as pltpu
from jax.sharding import PartitionSpec as P

TV = 32
NTV = 4
NOP = 512
PAIR = 1024
GROUPS = 4


def ladder_kernel(steps, count, tile_count, first, half_ref, live_ref, pick_ref, tile_ref, *refs):
    kinds = NTV + 1
    lefts = [refs[s * kinds:(s + 1) * kinds] for s in range(steps)]
    rest = refs[steps * kinds:]
    whole, rest = rest[:2], rest[2:]
    tiles = [rest[2 * n:2 * n + 2] for n in range((steps - 1) * tile_count)]
    rest = rest[2 * (steps - 1) * tile_count:]
    amp_ref = rest[0]
    before_ref = None if first else rest[1]
    out_ref, total_ref, products, ready, left_buf, right_buf, left_sem, right_sem = rest[-8:]
    d_tile, step = pl.program_id(0), pl.program_id(1)
    rows = left_buf.shape[0] // count
    depth = left_buf.shape[1] // steps
    group_rows = rows // GROUPS
    c_part = TV // GROUPS
    a_count = group_rows // c_part
    wide = 2 * GROUPS * TV
    half_blocks = rows // wide
    block_rows = TV // GROUPS * a_count
    slot = d_tile % 2

    def right_copies(i):
        copies = []
        for s in range(steps):
            for side in range(2):
                source = whole[side].at[tile_ref[i]] if s == 0 else tiles[(s - 1) * tile_count + i][side].at[0]
                target = right_buf.at[i % 2, side, :, pl.ds(s * depth, depth)]
                copies.append(pltpu.make_async_copy(source, target, right_sem.at[i % 2, s, side]))
        return copies

    def left_place(t, s, first, size):
        return left_buf.at[pl.ds(t * rows + first, size), pl.ds(s * depth, depth)]

    @pl.when((d_tile == 0) & (step == 0))
    def _():
        for t in range(count):
            for s in range(steps):
                for k in range(NTV - 1):

                    @pl.when(pick_ref[t] == k)
                    def _():
                        pltpu.make_async_copy(lefts[s][k], left_place(t, s, 0, rows), left_sem.at[t, s]).start()

                @pl.when(pick_ref[t] == NTV - 1)
                def _():
                    for part in range(2):
                        target = left_place(t, s, part * (rows // 2), rows // 2)
                        pltpu.make_async_copy(lefts[s][NTV - 1 + part], target, left_sem.at[t, s]).start()
        for copy in right_copies(0):
            copy.start()
        for t in range(count):
            for s in range(steps):
                pltpu.make_async_copy(lefts[s][0], left_place(t, s, 0, rows), left_sem.at[t, s]).wait()

    for i in range(tile_count):

        @pl.when((d_tile == i) & (step == 0))
        def _():
            for copy in right_copies(i):
                copy.wait()
            if i + 1 < tile_count:
                for copy in right_copies(i + 1):
                    copy.start()

    @pl.when(step < GROUPS)
    def _():
        left = jnp.concatenate(
            [
                left_buf[pl.ds(pl.multiple_of(t * rows + step * group_rows, group_rows), group_rows), :]
                for t in range(count)
            ],
            axis=0,
        )
        for half in range(2):
            start = (half_ref[0] if half == 0 else 1 - half_ref[0]) * half_blocks
            for p in range(half_blocks):
                right = jnp.concatenate(
                    [
                        right_buf[
                            slot,
                            half,
                            pl.ds(
                                pl.multiple_of(
                                    p * wide + (g // GROUPS * GROUPS + (g + step) % GROUPS) * TV, TV
                                ),
                                TV,
                            ),
                            :,
                        ]
                        for g in range(2 * GROUPS)
                    ],
                    axis=0,
                )
                products[step, start + p] = lax.dot_general(
                    left, right, (((1,), (1,)), ((), ())), preferred_element_type=jnp.float32
                ).astype(jnp.bfloat16)

    @pl.when(step >= GROUPS)
    def _():
        k = step - GROUPS
        lane_group = lax.broadcasted_iota(jnp.int32, (a_count, wide), 1) // TV % GROUPS
        masks = [lane_group == g for g in range(GROUPS)]
        lanes = GROUPS * TV
        for p in range(2 * half_blocks):
            for t in range(count):
                for c in range(c_part):
                    place = pl.ds(t * group_rows + c * a_count, a_count)
                    mixed = products[k, p, place, :]
                    for g in range(1, GROUPS):
                        mixed = jnp.where(masks[g], products[(k + GROUPS - g) % GROUPS, p, place, :], mixed)
                    for b in range(2):
                        ready[t, 2 * p + b, :, c * lanes:(c + 1) * lanes] = mixed[:, b * lanes:(b + 1) * lanes]
        amp = jnp.concatenate(
            [
                amp_ref[0, pl.ds(pl.multiple_of(((k + GROUPS - g) % GROUPS * c_part + c) * TV, TV), TV), :]
                for c in range(c_part)
                for g in range(GROUPS)
            ],
            axis=0,
        )
        terms = jnp.dot(
            ready[...].reshape(count * block_rows, TV * TV), amp, preferred_element_type=jnp.float32
        ).reshape(count, block_rows, amp.shape[1])
        for t in range(count):
            term = terms[t] * live_ref[d_tile, t].astype(jnp.float32)

            @pl.when(d_tile == 0)
            def _():
                total_ref[t, k] = term if first else before_ref[t, k] + term

            @pl.when((d_tile > 0) & (d_tile < tile_count - 1))
            def _():
                total_ref[t, k] += term

            @pl.when(d_tile == tile_count - 1)
            def _():
                out_ref[t, k] = (total_ref[t, k] + term).astype(out_ref.dtype)


def ladder(half, live, pick, tile, lefts, whole, tiles, amp, before, part, kind):
    steps = len(lefts)
    rows, depth = whole[0].shape[1:]
    columns = amp.shape[2]
    a_count = rows // TV
    b_blocks = TV // GROUPS
    wide = 2 * GROUPS * TV
    tile_count = live.shape[0]
    first = before is None
    base, count = part
    result = (count, GROUPS, b_blocks * a_count, columns)
    flops = 2 * tile_count * count * rows * 2 * rows * (steps * depth + columns)
    anywhere = pl.BlockSpec(memory_space=pl.ANY)
    copied = [x for step in lefts for x in step] + [*whole] + [x for pair in tiles for x in pair]
    return pl.pallas_call(
        functools.partial(ladder_kernel, steps, count, tile_count, first),
        grid_spec=pltpu.PrefetchScalarGridSpec(
            num_scalar_prefetch=4,
            grid=(tile_count, 2 * GROUPS),
            in_specs=[anywhere] * len(copied)
            + [pl.BlockSpec((1, 2 * rows, columns), lambda i, j, h, v, k, d: (d[i], 0, 0))]
            + [
                pl.BlockSpec(result, lambda i, j, h, v, k, d: (base // count, 0, 0, 0), pipeline_mode=pl.Buffered(1))
            ]
            * (not first),
            out_specs=pl.BlockSpec(result, lambda i, j, h, v, k, d: (0, 0, 0, 0)),
            scratch_shapes=[
                pltpu.VMEM(result, jnp.float32),
                pltpu.VMEM((GROUPS, 2 * rows // wide, count * rows // GROUPS, wide), jnp.bfloat16),
                pltpu.VMEM((count, b_blocks, a_count, TV * TV), jnp.bfloat16),
                pltpu.VMEM((count * rows, steps * depth), jnp.bfloat16),
                pltpu.VMEM((2, 2, rows, steps * depth), jnp.bfloat16),
                pltpu.SemaphoreType.DMA((count, steps)),
                pltpu.SemaphoreType.DMA((2, steps, 2)),
            ],
        ),
        out_shape=jax.ShapeDtypeStruct(result, kind),
        compiler_params=pltpu.CompilerParams(vmem_limit_bytes=60 * 2**20),
        cost_estimate=pl.CostEstimate(flops=flops, bytes_accessed=28 * 2**20, transcendentals=0),
    )(half, live[:, base:base + count], pick[base:base + count], tile, *copied, amp, *([] if first else [before]))


def partner(value, axis, size, flip):
    return lax.ppermute(value, axis, [(i, i ^ flip) for i in range(size)])


def shift(value, axis, size, step):
    return lax.ppermute(value, axis, [(i, (i + step) % size) for i in range(size)])


def ring_order(size):
    return list(range(0, size, 2)) + list(range(size - 1, 0, -2))


HOPS = (
    (1, 2), (1, 1), (1, 0), (2, 1), (2, 0), (3, 0),
    (1, 3), (2, 3), (2, 2), (3, 2), (3, 1), (3, 3),
)
AMP = "amp"
NEAR = {0: 0, 2: AMP, 4: 1, 6: 2, 8: 3}
FAR = {1: 0, 3: AMP, 5: 1, 7: 2, 9: 3}
FAR_DONE = {2: 0, 4: AMP, 6: 1, 8: 2, 10: 3}


def on_square(chol, amps, listed):
    row_count, depth = chol.shape[1:]
    columns = amps.shape[3]
    a_count = row_count // TV
    left_index = lax.axis_index("left")
    right_index = lax.axis_index("right")
    occ_index = lax.axis_index("occ")
    order = ring_order(NTV)
    ring = [(order[p], order[(p + 1) % NTV]) for p in range(NTV)]
    near = [[order[(order.index(level) + i) % NTV] for level in range(NTV)] for i in range(NTV)]

    def at_level(table):
        value = jnp.int32(table[0])
        for level in range(1, NTV):
            value = jnp.where(left_index == level, jnp.int32(table[level]), value)
        return value

    d_tiles = [at_level(table) for table in near]
    tiles = jnp.arange(NTV)
    targets = (left_index + 1 + tiles) % NTV
    pick = (targets ^ right_index).astype(jnp.int32)
    own_c = lax.dynamic_index_in_dim(listed, left_index, 1, keepdims=False)
    live = lax.dynamic_index_in_dim(own_c, right_index, 1, keepdims=False)[targets]
    half = occ_index.reshape(1)

    held = {("block", 0, i): lax.dynamic_slice_in_dim(chol, d_tiles[i], 1, 0) for i in (3, 2, 0, 1)}
    held["chol"] = chol
    held["left", AMP, 0] = amps[0]
    last = len(HOPS)
    waiting = {slot: [] for slot in range(last + 4)}

    def meet(keys):
        keys = list(dict.fromkeys(keys))
        for key, value in zip(keys, lax.optimization_barrier([held[key] for key in keys])):
            held[key] = value

    def contract(chosen, before, part, kind):
        d_order = jnp.stack([d_tiles[i] for i in chosen])
        return ladder(
            half,
            live[:, d_order].T,
            pick,
            d_order,
            [[held["left", s, piece] for piece in (0, 1, 2, "first", "second")] for s in range(NTV)],
            (held["chol"], held["other", "chol"]),
            [(held["block", s, i], held["other", s, i]) for s in range(1, NTV) for i in chosen],
            held["amp"],
            before,
            part,
            kind,
        )

    for slot in range(last + 1):
        hops = [0, 1] if slot == 0 else [slot + 1] if slot + 1 < last else []
        near_block, far_block, done_block = NEAR.get(slot), FAR.get(slot), FAR_DONE.get(slot)
        now = waiting[slot]
        if slot >= 1:
            now.append(("block", *HOPS[slot - 1]))
        if near_block is not None:
            if near_block != AMP:
                own = held["block", near_block, 0].reshape(a_count, TV, depth)
                held["left", near_block, 0] = own.transpose(1, 0, 2).reshape(row_count, depth)
            now.append(("left", near_block, 0))
        if far_block is not None:
            now += [("left", far_block, flip) for flip in range(3)]
        if done_block is not None:
            now += [("left", done_block, "first"), ("left", done_block, "second")]
        now += [("block", HOPS[u][0] - 1, (HOPS[u][1] + 1) % NTV) for u in hops]
        if slot == 1:
            now.append("chol")
        meet(now)
        for u in hops:
            s, i = HOPS[u]
            held["block", s, i] = lax.ppermute(held["block", s - 1, (i + 1) % NTV], "left", ring)
        if near_block is not None:
            for flip in (1, 2):
                held["left", near_block, flip] = partner(held["left", near_block, 0], "right", NTV, flip)
        if far_block is not None:
            middle = held["left", far_block, 0].shape[0] // 2
            held["left", far_block, "first"] = partner(held["left", far_block, 1][:middle], "right", NTV, 2)
            held["left", far_block, "second"] = partner(held["left", far_block, 2][middle:], "right", NTV, 1)
        if slot == 1:
            held["other", "chol"] = partner(held["chol"], "occ", 2, 1)
            waiting[slot + 1].append(("other", "chol"))
        if slot >= 1:
            unit = HOPS[slot - 1]
            held["other", *unit] = partner(held["block", *unit], "occ", 2, 1)
            waiting[slot + 1].append(("other", *unit))
        if done_block == AMP:
            far = jnp.concatenate([held["left", AMP, "first"], held["left", AMP, "second"]])
            every = [held["left", AMP, flip] for flip in range(3)] + [far]
            held["amp"] = lax.all_gather(jnp.concatenate(every, axis=2), "occ", axis=1, tiled=True)
            waiting[slot + 3].append("amp")
        if slot == last - 1:
            held["sum"] = contract((0, 2), None, (0, NTV), jnp.float32)
            waiting[slot + 1].append("sum")
    early = contract((1, 3), held["sum"], (0, NTV - 1), jnp.bfloat16)
    moved = [shift(early[t], "left", NTV, t + 1) for t in range(NTV - 1)]
    late = contract((1, 3), held["sum"], (NTV - 1, 1), jnp.float32)
    summed = late[0]
    for piece in moved:
        summed = summed + piece.astype(jnp.float32)
    pieces = []
    for flip in range(NTV):
        piece = summed[:, :, flip * columns:(flip + 1) * columns]
        if flip:
            piece = partner(piece.astype(jnp.bfloat16), "right", NTV, flip).astype(jnp.float32)
        pieces.append(piece)
    result = jnp.stack(pieces)[tiles ^ right_index]
    result = result.reshape(NTV, GROUPS, TV // GROUPS, a_count, columns).transpose(0, 3, 2, 1, 4)
    return result.reshape(1, NTV, row_count, columns)


def broadcast(value, axis, source):
    kept = jnp.where(lax.axis_index(axis) == source, value, 0).astype(value.dtype)
    return lax.psum(kept, axis)


def on_device(sizes, chol, amps, listed):
    tile_count = chol.shape[0]
    if sizes == (NTV, NTV, 2) and tile_count == NTV:
        return on_square(chol, amps, listed)
    row_count = chol.shape[1]
    a_local = row_count // TV
    left_index = lax.axis_index("left")
    right_index = lax.axis_index("right")
    first_tile = right_index * tile_count
    full_vectors = lax.all_gather(chol, "left", axis=2, tiled=True)
    collected = []
    for a_tile in range(NTV):
        wanted = a_tile * NTV + left_index
        holder = wanted // tile_count
        holder_slot = wanted % tile_count
        offered = lax.dynamic_index_in_dim(full_vectors, holder_slot, 0, keepdims=False)
        collected.append(broadcast(offered, "right", holder))
    left_rows = jnp.stack(collected)
    own_c = lax.dynamic_index_in_dim(listed, left_index, 1, keepdims=False).reshape(NTV, NTV * NTV)
    live = lax.dynamic_slice_in_dim(own_c, first_tile, tile_count, 1).T.astype(jnp.float32)
    products = jnp.einsum(
        "xrq,tkq->txrk",
        left_rows,
        lax.all_gather(full_vectors, "occ", axis=1, tiled=True),
        preferred_element_type=jnp.float32,
    )
    inner = (products * live[:, :, None, None]).astype(jnp.bfloat16)
    swapped = inner.reshape(tile_count, NTV, a_local, TV, TV, TV).transpose(0, 1, 2, 4, 3, 5)
    swapped = swapped.reshape(tile_count, NTV * a_local * TV, PAIR)
    amp_columns = lax.all_gather(amps, "right", axis=3, tiled=True)
    d_first = first_tile % NTV
    own_amps = lax.dynamic_slice_in_dim(amp_columns[0], d_first, tile_count, 0)
    partial_sum = jnp.einsum(
        "trk,tkn->rn",
        swapped,
        lax.all_gather(own_amps, "occ", axis=1, tiled=True),
        preferred_element_type=jnp.float32,
    )
    partial_sum = partial_sum.reshape(NTV, row_count, NOP)
    owned_a = lax.psum_scatter(partial_sum, "left", scatter_dimension=0, tiled=True)
    b_tile = first_tile // NTV
    placed = lax.dynamic_update_slice_in_dim(
        jnp.zeros((NTV, row_count, NOP), jnp.float32), owned_a, b_tile, 0
    )
    summed = lax.psum_scatter(placed, "right", scatter_dimension=2, tiled=True)
    return summed.reshape(1, NTV, row_count, summed.shape[2])


def solution(mesh):
    placed = (P("right", "occ", "left"), P("left", None, "occ", "right"), P())
    return jax.shard_map(
        functools.partial(on_device, tuple(mesh.shape[axis] for axis in ("left", "right", "occ"))),
        mesh=mesh,
        in_specs=placed,
        out_specs=P("left", None, "occ", "right"),
        check_vma=False,
    )
```

```python
import functools

import jax
import jax.numpy as jnp
from jax import lax
from jax.experimental import pallas as pl
from jax.experimental.pallas import tpu as pltpu
from jax.sharding import PartitionSpec as P

TV = 32
NTV = 4
NOP = 512
PAIR = 1024
GROUPS = 4


def ladder_kernel(steps, count, tile_count, first, half_ref, live_ref, pick_ref, tile_ref, *refs):
    kinds = NTV + 1
    lefts = [refs[s * kinds:(s + 1) * kinds] for s in range(steps)]
    rest = refs[steps * kinds:]
    whole, rest = rest[:2], rest[2:]
    tiles = [rest[2 * n:2 * n + 2] for n in range((steps - 1) * tile_count)]
    rest = rest[2 * (steps - 1) * tile_count:]
    amp_ref = rest[0]
    before_ref = None if first else rest[1]
    out_ref, total_ref, products, ready, left_buf, right_buf, left_sem, right_sem = rest[-8:]
    d_tile, step = pl.program_id(0), pl.program_id(1)
    rows = left_buf.shape[0] // count
    depth = left_buf.shape[1] // steps
    group_rows = rows // GROUPS
    c_part = TV // GROUPS
    a_count = group_rows // c_part
    wide = 2 * GROUPS * TV
    half_blocks = rows // wide
    block_rows = TV // GROUPS * a_count
    slot = d_tile % 2

    def right_copies(i):
        copies = []
        for s in range(steps):
            for side in range(2):
                source = whole[side].at[tile_ref[i]] if s == 0 else tiles[(s - 1) * tile_count + i][side].at[0]
                target = right_buf.at[i % 2, side, :, pl.ds(s * depth, depth)]
                copies.append(pltpu.make_async_copy(source, target, right_sem.at[i % 2, s, side]))
        return copies

    def left_place(t, s, first, size):
        return left_buf.at[pl.ds(t * rows + first, size), pl.ds(s * depth, depth)]

    @pl.when((d_tile == 0) & (step == 0))
    def _():
        for t in range(count):
            for s in range(steps):
                for k in range(NTV - 1):

                    @pl.when(pick_ref[t] == k)
                    def _():
                        pltpu.make_async_copy(lefts[s][k], left_place(t, s, 0, rows), left_sem.at[t, s]).start()

                @pl.when(pick_ref[t] == NTV - 1)
                def _():
                    for part in range(2):
                        target = left_place(t, s, part * (rows // 2), rows // 2)
                        pltpu.make_async_copy(lefts[s][NTV - 1 + part], target, left_sem.at[t, s]).start()
        for copy in right_copies(0):
            copy.start()
        for t in range(count):
            for s in range(steps):
                pltpu.make_async_copy(lefts[s][0], left_place(t, s, 0, rows), left_sem.at[t, s]).wait()

    for i in range(tile_count):

        @pl.when((d_tile == i) & (step == 0))
        def _():
            for copy in right_copies(i):
                copy.wait()
            if i + 1 < tile_count:
                for copy in right_copies(i + 1):
                    copy.start()

    @pl.when(step < GROUPS)
    def _():
        left = jnp.concatenate(
            [
                left_buf[pl.ds(pl.multiple_of(t * rows + step * group_rows, group_rows), group_rows), :]
                for t in range(count)
            ],
            axis=0,
        )
        for half in range(2):
            start = (half_ref[0] if half == 0 else 1 - half_ref[0]) * half_blocks
            for p in range(half_blocks):
                right = jnp.concatenate(
                    [
                        right_buf[
                            slot,
                            half,
                            pl.ds(
                                pl.multiple_of(
                                    p * wide + (g // GROUPS * GROUPS + (g + step) % GROUPS) * TV, TV
                                ),
                                TV,
                            ),
                            :,
                        ]
                        for g in range(2 * GROUPS)
                    ],
                    axis=0,
                )
                products[step, start + p] = lax.dot_general(
                    left, right, (((1,), (1,)), ((), ())), preferred_element_type=jnp.float32
                ).astype(jnp.bfloat16)

    @pl.when(step >= GROUPS)
    def _():
        k = step - GROUPS
        lane_group = lax.broadcasted_iota(jnp.int32, (a_count, wide), 1) // TV % GROUPS
        masks = [lane_group == g for g in range(GROUPS)]
        lanes = GROUPS * TV
        for p in range(2 * half_blocks):
            for t in range(count):
                for c in range(c_part):
                    place = pl.ds(t * group_rows + c * a_count, a_count)
                    mixed = products[k, p, place, :]
                    for g in range(1, GROUPS):
                        mixed = jnp.where(masks[g], products[(k + GROUPS - g) % GROUPS, p, place, :], mixed)
                    for b in range(2):
                        ready[t, 2 * p + b, :, c * lanes:(c + 1) * lanes] = mixed[:, b * lanes:(b + 1) * lanes]
        amp = jnp.concatenate(
            [
                amp_ref[0, pl.ds(pl.multiple_of(((k + GROUPS - g) % GROUPS * c_part + c) * TV, TV), TV), :]
                for c in range(c_part)
                for g in range(GROUPS)
            ],
            axis=0,
        )
        terms = jnp.dot(
            ready[...].reshape(count * block_rows, TV * TV), amp, preferred_element_type=jnp.float32
        ).reshape(count, block_rows, amp.shape[1])
        for t in range(count):
            term = terms[t] * live_ref[d_tile, t].astype(jnp.float32)
            if tile_count == 1:
                out_ref[t, k] = (term if first else before_ref[t, k] + term).astype(out_ref.dtype)
                continue

            @pl.when(d_tile == 0)
            def _():
                total_ref[t, k] = term if first else before_ref[t, k] + term

            @pl.when((d_tile > 0) & (d_tile < tile_count - 1))
            def _():
                total_ref[t, k] += term

            @pl.when(d_tile == tile_count - 1)
            def _():
                out_ref[t, k] = (total_ref[t, k] + term).astype(out_ref.dtype)


def ladder(half, live, pick, tile, lefts, whole, tiles, amp, before, part, kind):
    steps = len(lefts)
    rows, depth = whole[0].shape[1:]
    columns = amp.shape[2]
    a_count = rows // TV
    b_blocks = TV // GROUPS
    wide = 2 * GROUPS * TV
    tile_count = live.shape[0]
    first = before is None
    count = NTV if part is None else NTV // 2
    base = 0 if part is None else part * count
    result = (count, GROUPS, b_blocks * a_count, columns)
    flops = 2 * tile_count * count * rows * 2 * rows * (steps * depth + columns)
    anywhere = pl.BlockSpec(memory_space=pl.ANY)
    copied = [x for step in lefts for x in step] + [*whole] + [x for pair in tiles for x in pair]
    return pl.pallas_call(
        functools.partial(ladder_kernel, steps, count, tile_count, first),
        grid_spec=pltpu.PrefetchScalarGridSpec(
            num_scalar_prefetch=4,
            grid=(tile_count, 2 * GROUPS),
            in_specs=[anywhere] * len(copied)
            + [pl.BlockSpec((1, 2 * rows, columns), lambda i, j, h, v, k, d: (d[i], 0, 0))]
            + [
                pl.BlockSpec(result, lambda i, j, h, v, k, d: (base // count, 0, 0, 0), pipeline_mode=pl.Buffered(1))
            ]
            * (not first),
            out_specs=pl.BlockSpec(result, lambda i, j, h, v, k, d: (0, 0, 0, 0)),
            scratch_shapes=[
                pltpu.VMEM(result, jnp.float32),
                pltpu.VMEM((GROUPS, 2 * rows // wide, count * rows // GROUPS, wide), jnp.bfloat16),
                pltpu.VMEM((count, b_blocks, a_count, TV * TV), jnp.bfloat16),
                pltpu.VMEM((count * rows, steps * depth), jnp.bfloat16),
                pltpu.VMEM((2, 2, rows, steps * depth), jnp.bfloat16),
                pltpu.SemaphoreType.DMA((count, steps)),
                pltpu.SemaphoreType.DMA((2, steps, 2)),
            ],
        ),
        out_shape=jax.ShapeDtypeStruct(result, kind),
        compiler_params=pltpu.CompilerParams(vmem_limit_bytes=60 * 2**20),
        cost_estimate=pl.CostEstimate(flops=flops, bytes_accessed=28 * 2**20, transcendentals=0),
    )(half, live[:, base:base + count], pick[base:base + count], tile, *copied, amp, *([] if first else [before]))


def partner(value, axis, size, flip):
    return lax.ppermute(value, axis, [(i, i ^ flip) for i in range(size)])


def shift(value, axis, size, step):
    return lax.ppermute(value, axis, [(i, (i + step) % size) for i in range(size)])


def ring_order(size):
    return list(range(0, size, 2)) + list(range(size - 1, 0, -2))


HOPS = (
    (1, 2), (1, 1), (1, 0), (2, 1), (2, 0), (3, 0),
    (1, 3), (2, 3), (2, 2), (3, 2), (3, 1), (3, 3),
)
AMP = "amp"
NEAR = {0: 0, 2: AMP, 4: 1, 6: 2, 8: 3}
FAR = {1: 0, 3: AMP, 5: 1, 7: 2, 9: 3}
FAR_DONE = {2: 0, 4: AMP, 6: 1, 8: 2, 10: 3}


def on_square(chol, amps, listed):
    row_count, depth = chol.shape[1:]
    columns = amps.shape[3]
    a_count = row_count // TV
    left_index = lax.axis_index("left")
    right_index = lax.axis_index("right")
    occ_index = lax.axis_index("occ")
    order = ring_order(NTV)
    ring = [(order[p], order[(p + 1) % NTV]) for p in range(NTV)]
    near = [[order[(order.index(level) + i) % NTV] for level in range(NTV)] for i in range(NTV)]

    def at_level(table):
        value = jnp.int32(table[0])
        for level in range(1, NTV):
            value = jnp.where(left_index == level, jnp.int32(table[level]), value)
        return value

    d_tiles = [at_level(table) for table in near]
    tiles = jnp.arange(NTV)
    targets = (left_index + 1 + tiles) % NTV
    pick = (targets ^ right_index).astype(jnp.int32)
    own_c = lax.dynamic_index_in_dim(listed, left_index, 1, keepdims=False)
    live = lax.dynamic_index_in_dim(own_c, right_index, 1, keepdims=False)[targets]
    half = occ_index.reshape(1)

    held = {("block", 0, i): lax.dynamic_slice_in_dim(chol, d_tiles[i], 1, 0) for i in (3, 2, 0, 1)}
    held["chol"] = chol
    held["left", AMP, 0] = amps[0]
    last = len(HOPS)
    waiting = {slot: [] for slot in range(last + 4)}

    def meet(keys):
        keys = list(dict.fromkeys(keys))
        for key, value in zip(keys, lax.optimization_barrier([held[key] for key in keys])):
            held[key] = value

    def contract(chosen, before, part, kind):
        d_order = jnp.stack([d_tiles[i] for i in chosen])
        return ladder(
            half,
            live[:, d_order].T,
            pick,
            d_order,
            [[held["left", s, piece] for piece in (0, 1, 2, "first", "second")] for s in range(NTV)],
            (held["chol"], held["other", "chol"]),
            [(held["block", s, i], held["other", s, i]) for s in range(1, NTV) for i in chosen],
            held["amp"],
            before,
            part,
            kind,
        )

    for slot in range(last + 1):
        hops = [0, 1] if slot == 0 else [slot + 1] if slot + 1 < last else []
        near_block, far_block, done_block = NEAR.get(slot), FAR.get(slot), FAR_DONE.get(slot)
        now = waiting[slot]
        if slot >= 1:
            now.append(("block", *HOPS[slot - 1]))
        if near_block is not None:
            if near_block != AMP:
                own = held["block", near_block, 0].reshape(a_count, TV, depth)
                held["left", near_block, 0] = own.transpose(1, 0, 2).reshape(row_count, depth)
            now.append(("left", near_block, 0))
        if far_block is not None:
            now += [("left", far_block, flip) for flip in range(3)]
        if done_block is not None:
            now += [("left", done_block, "first"), ("left", done_block, "second")]
        now += [("block", HOPS[u][0] - 1, (HOPS[u][1] + 1) % NTV) for u in hops]
        if slot == 1:
            now.append("chol")
        meet(now)
        for u in hops:
            s, i = HOPS[u]
            held["block", s, i] = lax.ppermute(held["block", s - 1, (i + 1) % NTV], "left", ring)
        if near_block is not None:
            for flip in (1, 2):
                held["left", near_block, flip] = partner(held["left", near_block, 0], "right", NTV, flip)
        if far_block is not None:
            middle = held["left", far_block, 0].shape[0] // 2
            held["left", far_block, "first"] = partner(held["left", far_block, 1][:middle], "right", NTV, 2)
            held["left", far_block, "second"] = partner(held["left", far_block, 2][middle:], "right", NTV, 1)
        if slot == 1:
            held["other", "chol"] = partner(held["chol"], "occ", 2, 1)
            waiting[slot + 1].append(("other", "chol"))
        if slot >= 1:
            unit = HOPS[slot - 1]
            held["other", *unit] = partner(held["block", *unit], "occ", 2, 1)
            waiting[slot + 1].append(("other", *unit))
        if done_block == AMP:
            far = jnp.concatenate([held["left", AMP, "first"], held["left", AMP, "second"]])
            every = [held["left", AMP, flip] for flip in range(3)] + [far]
            held["amp"] = lax.all_gather(jnp.concatenate(every, axis=2), "occ", axis=1, tiled=True)
            waiting[slot + 3].append("amp")
        if slot == last - 2:
            held["sum"] = contract((0,), None, None, jnp.float32)
            waiting[slot + 1].append("sum")
    partials = contract((2, 1), held["sum"], None, jnp.float32)
    early = contract((3,), partials, 0, jnp.bfloat16)
    moved = [shift(early[t], "left", NTV, t + 1) for t in range(NTV // 2)]
    late = contract((3,), partials, 1, jnp.float32)
    moved += [
        shift(late[t].astype(jnp.bfloat16), "left", NTV, NTV // 2 + t + 1) for t in range(NTV // 2 - 1)
    ]
    summed = late[NTV // 2 - 1]
    for piece in moved:
        summed = summed + piece.astype(jnp.float32)
    pieces = []
    for flip in range(NTV):
        piece = summed[:, :, flip * columns:(flip + 1) * columns]
        if flip:
            piece = partner(piece.astype(jnp.bfloat16), "right", NTV, flip).astype(jnp.float32)
        pieces.append(piece)
    result = jnp.stack(pieces)[tiles ^ right_index]
    result = result.reshape(NTV, GROUPS, TV // GROUPS, a_count, columns).transpose(0, 3, 2, 1, 4)
    return result.reshape(1, NTV, row_count, columns)


def broadcast(value, axis, source):
    kept = jnp.where(lax.axis_index(axis) == source, value, 0).astype(value.dtype)
    return lax.psum(kept, axis)


def on_device(sizes, chol, amps, listed):
    tile_count = chol.shape[0]
    if sizes == (NTV, NTV, 2) and tile_count == NTV:
        return on_square(chol, amps, listed)
    row_count = chol.shape[1]
    a_local = row_count // TV
    left_index = lax.axis_index("left")
    right_index = lax.axis_index("right")
    first_tile = right_index * tile_count
    full_vectors = lax.all_gather(chol, "left", axis=2, tiled=True)
    collected = []
    for a_tile in range(NTV):
        wanted = a_tile * NTV + left_index
        holder = wanted // tile_count
        holder_slot = wanted % tile_count
        offered = lax.dynamic_index_in_dim(full_vectors, holder_slot, 0, keepdims=False)
        collected.append(broadcast(offered, "right", holder))
    left_rows = jnp.stack(collected)
    own_c = lax.dynamic_index_in_dim(listed, left_index, 1, keepdims=False).reshape(NTV, NTV * NTV)
    live = lax.dynamic_slice_in_dim(own_c, first_tile, tile_count, 1).T.astype(jnp.float32)
    products = jnp.einsum(
        "xrq,tkq->txrk",
        left_rows,
        lax.all_gather(full_vectors, "occ", axis=1, tiled=True),
        preferred_element_type=jnp.float32,
    )
    inner = (products * live[:, :, None, None]).astype(jnp.bfloat16)
    swapped = inner.reshape(tile_count, NTV, a_local, TV, TV, TV).transpose(0, 1, 2, 4, 3, 5)
    swapped = swapped.reshape(tile_count, NTV * a_local * TV, PAIR)
    amp_columns = lax.all_gather(amps, "right", axis=3, tiled=True)
    d_first = first_tile % NTV
    own_amps = lax.dynamic_slice_in_dim(amp_columns[0], d_first, tile_count, 0)
    partial_sum = jnp.einsum(
        "trk,tkn->rn",
        swapped,
        lax.all_gather(own_amps, "occ", axis=1, tiled=True),
        preferred_element_type=jnp.float32,
    )
    partial_sum = partial_sum.reshape(NTV, row_count, NOP)
    owned_a = lax.psum_scatter(partial_sum, "left", scatter_dimension=0, tiled=True)
    b_tile = first_tile // NTV
    placed = lax.dynamic_update_slice_in_dim(
        jnp.zeros((NTV, row_count, NOP), jnp.float32), owned_a, b_tile, 0
    )
    summed = lax.psum_scatter(placed, "right", scatter_dimension=2, tiled=True)
    return summed.reshape(1, NTV, row_count, summed.shape[2])


def solution(mesh):
    placed = (P("right", "occ", "left"), P("left", None, "occ", "right"), P())
    return jax.shard_map(
        functools.partial(on_device, tuple(mesh.shape[axis] for axis in ("left", "right", "occ"))),
        mesh=mesh,
        in_specs=placed,
        out_specs=P("left", None, "occ", "right"),
        check_vma=False,
    )
```

```python
import functools

import jax
import jax.numpy as jnp
from jax import lax
from jax.experimental import pallas as pl
from jax.experimental.pallas import tpu as pltpu
from jax.sharding import PartitionSpec as P

TV = 32
NTV = 4
NOP = 512
PAIR = 1024
GROUPS = 4


def ladder_kernel(steps, count, tile_count, first, half_ref, live_ref, pick_ref, tile_ref, *refs):
    kinds = NTV + 1
    lefts = [refs[s * kinds:(s + 1) * kinds] for s in range(steps)]
    rest = refs[steps * kinds:]
    whole, rest = rest[:2], rest[2:]
    tiles = [rest[2 * n:2 * n + 2] for n in range((steps - 1) * tile_count)]
    rest = rest[2 * (steps - 1) * tile_count:]
    amp_ref = rest[0]
    before_ref = None if first else rest[1]
    out_ref, total_ref, products, ready, left_buf, right_buf, left_sem, right_sem = rest[-8:]
    d_tile, step = pl.program_id(0), pl.program_id(1)
    rows = left_buf.shape[0] // count
    depth = left_buf.shape[1] // steps
    group_rows = rows // GROUPS
    c_part = TV // GROUPS
    a_count = group_rows // c_part
    wide = 2 * GROUPS * TV
    half_blocks = rows // wide
    block_rows = TV // GROUPS * a_count
    slot = d_tile % 2

    def right_copies(i):
        copies = []
        for s in range(steps):
            for side in range(2):
                source = whole[side].at[tile_ref[i]] if s == 0 else tiles[(s - 1) * tile_count + i][side].at[0]
                target = right_buf.at[i % 2, side, :, pl.ds(s * depth, depth)]
                copies.append(pltpu.make_async_copy(source, target, right_sem.at[i % 2, s, side]))
        return copies

    def left_place(t, s, first, size):
        return left_buf.at[pl.ds(t * rows + first, size), pl.ds(s * depth, depth)]

    @pl.when((d_tile == 0) & (step == 0))
    def _():
        for t in range(count):
            for s in range(steps):
                for k in range(NTV - 1):

                    @pl.when(pick_ref[t] == k)
                    def _():
                        pltpu.make_async_copy(lefts[s][k], left_place(t, s, 0, rows), left_sem.at[t, s]).start()

                @pl.when(pick_ref[t] == NTV - 1)
                def _():
                    for part in range(2):
                        target = left_place(t, s, part * (rows // 2), rows // 2)
                        pltpu.make_async_copy(lefts[s][NTV - 1 + part], target, left_sem.at[t, s]).start()
        for copy in right_copies(0):
            copy.start()
        for t in range(count):
            for s in range(steps):
                pltpu.make_async_copy(lefts[s][0], left_place(t, s, 0, rows), left_sem.at[t, s]).wait()

    for i in range(tile_count):

        @pl.when((d_tile == i) & (step == 0))
        def _():
            for copy in right_copies(i):
                copy.wait()
            if i + 1 < tile_count:
                for copy in right_copies(i + 1):
                    copy.start()

    @pl.when(step < GROUPS)
    def _():
        left = jnp.concatenate(
            [
                left_buf[pl.ds(pl.multiple_of(t * rows + step * group_rows, group_rows), group_rows), :]
                for t in range(count)
            ],
            axis=0,
        )
        for half in range(2):
            start = (half_ref[0] if half == 0 else 1 - half_ref[0]) * half_blocks
            for p in range(half_blocks):
                right = jnp.concatenate(
                    [
                        right_buf[
                            slot,
                            half,
                            pl.ds(
                                pl.multiple_of(
                                    p * wide + (g // GROUPS * GROUPS + (g + step) % GROUPS) * TV, TV
                                ),
                                TV,
                            ),
                            :,
                        ]
                        for g in range(2 * GROUPS)
                    ],
                    axis=0,
                )
                products[step, start + p] = lax.dot_general(
                    left, right, (((1,), (1,)), ((), ())), preferred_element_type=jnp.float32
                ).astype(jnp.bfloat16)

    @pl.when(step >= GROUPS)
    def _():
        k = step - GROUPS
        lane_group = lax.broadcasted_iota(jnp.int32, (a_count, wide), 1) // TV % GROUPS
        masks = [lane_group == g for g in range(GROUPS)]
        lanes = GROUPS * TV
        for p in range(2 * half_blocks):
            for t in range(count):
                for c in range(c_part):
                    place = pl.ds(t * group_rows + c * a_count, a_count)
                    mixed = products[k, p, place, :]
                    for g in range(1, GROUPS):
                        mixed = jnp.where(masks[g], products[(k + GROUPS - g) % GROUPS, p, place, :], mixed)
                    for b in range(2):
                        ready[t, 2 * p + b, :, c * lanes:(c + 1) * lanes] = mixed[:, b * lanes:(b + 1) * lanes]
        amp = jnp.concatenate(
            [
                amp_ref[0, pl.ds(pl.multiple_of(((k + GROUPS - g) % GROUPS * c_part + c) * TV, TV), TV), :]
                for c in range(c_part)
                for g in range(GROUPS)
            ],
            axis=0,
        )
        terms = jnp.dot(
            ready[...].reshape(count * block_rows, TV * TV), amp, preferred_element_type=jnp.float32
        ).reshape(count, block_rows, amp.shape[1])
        for t in range(count):
            term = terms[t] * live_ref[d_tile, t].astype(jnp.float32)

            @pl.when(d_tile == 0)
            def _():
                total_ref[t, k] = term if first else before_ref[t, k] + term

            @pl.when((d_tile > 0) & (d_tile < tile_count - 1))
            def _():
                total_ref[t, k] += term

            @pl.when(d_tile == tile_count - 1)
            def _():
                out_ref[t, k] = (total_ref[t, k] + term).astype(out_ref.dtype)


def ladder(half, live, pick, tile, lefts, whole, tiles, amp, before, part, kind):
    steps = len(lefts)
    rows, depth = whole[0].shape[1:]
    columns = amp.shape[2]
    a_count = rows // TV
    b_blocks = TV // GROUPS
    wide = 2 * GROUPS * TV
    tile_count = live.shape[0]
    first = before is None
    count = NTV if first else NTV // 2
    base = part * count
    result = (count, GROUPS, b_blocks * a_count, columns)
    flops = 2 * tile_count * count * rows * 2 * rows * (steps * depth + columns)
    anywhere = pl.BlockSpec(memory_space=pl.ANY)
    copied = [x for step in lefts for x in step] + [*whole] + [x for pair in tiles for x in pair]
    return pl.pallas_call(
        functools.partial(ladder_kernel, steps, count, tile_count, first),
        grid_spec=pltpu.PrefetchScalarGridSpec(
            num_scalar_prefetch=4,
            grid=(tile_count, 2 * GROUPS),
            in_specs=[anywhere] * len(copied)
            + [pl.BlockSpec((1, 2 * rows, columns), lambda i, j, h, v, k, d: (d[i], 0, 0))]
            + [
                pl.BlockSpec(result, lambda i, j, h, v, k, d: (part, 0, 0, 0), pipeline_mode=pl.Buffered(1))
            ]
            * (not first),
            out_specs=pl.BlockSpec(result, lambda i, j, h, v, k, d: (0, 0, 0, 0)),
            scratch_shapes=[
                pltpu.VMEM(result, jnp.float32),
                pltpu.VMEM((GROUPS, 2 * rows // wide, count * rows // GROUPS, wide), jnp.bfloat16),
                pltpu.VMEM((count, b_blocks, a_count, TV * TV), jnp.bfloat16),
                pltpu.VMEM((count * rows, steps * depth), jnp.bfloat16),
                pltpu.VMEM((2, 2, rows, steps * depth), jnp.bfloat16),
                pltpu.SemaphoreType.DMA((count, steps)),
                pltpu.SemaphoreType.DMA((2, steps, 2)),
            ],
        ),
        out_shape=jax.ShapeDtypeStruct(result, kind),
        compiler_params=pltpu.CompilerParams(vmem_limit_bytes=60 * 2**20),
        cost_estimate=pl.CostEstimate(flops=flops, bytes_accessed=28 * 2**20, transcendentals=0),
    )(half, live[:, base:base + count], pick[base:base + count], tile, *copied, amp, *([] if first else [before]))


def partner(value, axis, size, flip):
    return lax.ppermute(value, axis, [(i, i ^ flip) for i in range(size)])


def shift(value, axis, size, step):
    return lax.ppermute(value, axis, [(i, (i + step) % size) for i in range(size)])


def ring_order(size):
    return list(range(0, size, 2)) + list(range(size - 1, 0, -2))


HOPS = (
    (1, 2), (1, 1), (1, 0), (2, 1), (2, 0), (3, 0),
    (1, 3), (2, 3), (2, 2), (3, 2), (3, 1), (3, 3),
)
AMP = "amp"
NEAR = {0: 0, 2: AMP, 4: 1, 6: 2, 8: 3}
FAR = {1: 0, 3: AMP, 5: 1, 7: 2, 9: 3}
FAR_DONE = {2: 0, 4: AMP, 6: 1, 8: 2, 10: 3}


def on_square(chol, amps, listed):
    row_count, depth = chol.shape[1:]
    columns = amps.shape[3]
    a_count = row_count // TV
    left_index = lax.axis_index("left")
    right_index = lax.axis_index("right")
    occ_index = lax.axis_index("occ")
    order = ring_order(NTV)
    ring = [(order[p], order[(p + 1) % NTV]) for p in range(NTV)]
    near = [[order[(order.index(level) + i) % NTV] for level in range(NTV)] for i in range(NTV)]

    def at_level(table):
        value = jnp.int32(table[0])
        for level in range(1, NTV):
            value = jnp.where(left_index == level, jnp.int32(table[level]), value)
        return value

    d_tiles = [at_level(table) for table in near]
    tiles = jnp.arange(NTV)
    away = [NTV // 2] + [i for i in range(1, NTV) if i != NTV // 2] + [0]
    targets = jnp.stack([d_tiles[i] for i in away])

    def around(value, step):
        return lax.ppermute(value, "left", [(order[p], order[(p + step) % NTV]) for p in range(NTV)])

    pick = (targets ^ right_index).astype(jnp.int32)
    own_c = lax.dynamic_index_in_dim(listed, left_index, 1, keepdims=False)
    live = lax.dynamic_index_in_dim(own_c, right_index, 1, keepdims=False)[targets]
    half = occ_index.reshape(1)

    held = {("block", 0, i): lax.dynamic_slice_in_dim(chol, d_tiles[i], 1, 0) for i in (3, 2, 0, 1)}
    held["chol"] = chol
    held["left", AMP, 0] = amps[0]
    last = len(HOPS)
    waiting = {slot: [] for slot in range(last + 4)}

    def meet(keys):
        keys = list(dict.fromkeys(keys))
        for key, value in zip(keys, lax.optimization_barrier([held[key] for key in keys])):
            held[key] = value

    def contract(chosen, before, part, kind):
        d_order = jnp.stack([d_tiles[i] for i in chosen])
        return ladder(
            half,
            live[:, d_order].T,
            pick,
            d_order,
            [[held["left", s, piece] for piece in (0, 1, 2, "first", "second")] for s in range(NTV)],
            (held["chol"], held["other", "chol"]),
            [(held["block", s, i], held["other", s, i]) for s in range(1, NTV) for i in chosen],
            held["amp"],
            before,
            part,
            kind,
        )

    for slot in range(last + 1):
        hops = [0, 1] if slot == 0 else [slot + 1] if slot + 1 < last else []
        near_block, far_block, done_block = NEAR.get(slot), FAR.get(slot), FAR_DONE.get(slot)
        now = waiting[slot]
        if slot >= 1:
            now.append(("block", *HOPS[slot - 1]))
        if near_block is not None:
            if near_block != AMP:
                own = held["block", near_block, 0].reshape(a_count, TV, depth)
                held["left", near_block, 0] = own.transpose(1, 0, 2).reshape(row_count, depth)
            now.append(("left", near_block, 0))
        if far_block is not None:
            now += [("left", far_block, flip) for flip in range(3)]
        if done_block is not None:
            now += [("left", done_block, "first"), ("left", done_block, "second")]
        now += [("block", HOPS[u][0] - 1, (HOPS[u][1] + 1) % NTV) for u in hops]
        if slot == 1:
            now.append("chol")
        meet(now)
        for u in hops:
            s, i = HOPS[u]
            held["block", s, i] = lax.ppermute(held["block", s - 1, (i + 1) % NTV], "left", ring)
        if near_block is not None:
            for flip in (1, 2):
                held["left", near_block, flip] = partner(held["left", near_block, 0], "right", NTV, flip)
        if far_block is not None:
            middle = held["left", far_block, 0].shape[0] // 2
            held["left", far_block, "first"] = partner(held["left", far_block, 1][:middle], "right", NTV, 2)
            held["left", far_block, "second"] = partner(held["left", far_block, 2][middle:], "right", NTV, 1)
        if slot == 1:
            held["other", "chol"] = partner(held["chol"], "occ", 2, 1)
            waiting[slot + 1].append(("other", "chol"))
        if slot >= 1:
            unit = HOPS[slot - 1]
            held["other", *unit] = partner(held["block", *unit], "occ", 2, 1)
            waiting[slot + 1].append(("other", *unit))
        if done_block == AMP:
            far = jnp.concatenate([held["left", AMP, "first"], held["left", AMP, "second"]])
            every = [held["left", AMP, flip] for flip in range(3)] + [far]
            held["amp"] = lax.all_gather(jnp.concatenate(every, axis=2), "occ", axis=1, tiled=True)
            waiting[slot + 3].append("amp")
        if slot == last - 1:
            held["sum"] = contract((0, 2), None, 0, jnp.float32)
            waiting[slot + 1].append("sum")
    early = contract((1, 3), held["sum"], 0, jnp.bfloat16)
    moved = [around(early[t], away[t]) for t in range(NTV // 2)]
    late = contract((1, 3), held["sum"], 1, jnp.float32)
    moved += [around(late[t].astype(jnp.bfloat16), away[NTV // 2 + t]) for t in range(NTV // 2 - 1)]
    summed = late[NTV // 2 - 1]
    for piece in moved:
        summed = summed + piece.astype(jnp.float32)
    pieces = []
    for flip in range(NTV):
        piece = summed[:, :, flip * columns:(flip + 1) * columns]
        if flip:
            piece = partner(piece.astype(jnp.bfloat16), "right", NTV, flip).astype(jnp.float32)
        pieces.append(piece)
    result = jnp.stack(pieces)[tiles ^ right_index]
    result = result.reshape(NTV, GROUPS, TV // GROUPS, a_count, columns).transpose(0, 3, 2, 1, 4)
    return result.reshape(1, NTV, row_count, columns)


def broadcast(value, axis, source):
    kept = jnp.where(lax.axis_index(axis) == source, value, 0).astype(value.dtype)
    return lax.psum(kept, axis)


def on_device(sizes, chol, amps, listed):
    tile_count = chol.shape[0]
    if sizes == (NTV, NTV, 2) and tile_count == NTV:
        return on_square(chol, amps, listed)
    row_count = chol.shape[1]
    a_local = row_count // TV
    left_index = lax.axis_index("left")
    right_index = lax.axis_index("right")
    first_tile = right_index * tile_count
    full_vectors = lax.all_gather(chol, "left", axis=2, tiled=True)
    collected = []
    for a_tile in range(NTV):
        wanted = a_tile * NTV + left_index
        holder = wanted // tile_count
        holder_slot = wanted % tile_count
        offered = lax.dynamic_index_in_dim(full_vectors, holder_slot, 0, keepdims=False)
        collected.append(broadcast(offered, "right", holder))
    left_rows = jnp.stack(collected)
    own_c = lax.dynamic_index_in_dim(listed, left_index, 1, keepdims=False).reshape(NTV, NTV * NTV)
    live = lax.dynamic_slice_in_dim(own_c, first_tile, tile_count, 1).T.astype(jnp.float32)
    products = jnp.einsum(
        "xrq,tkq->txrk",
        left_rows,
        lax.all_gather(full_vectors, "occ", axis=1, tiled=True),
        preferred_element_type=jnp.float32,
    )
    inner = (products * live[:, :, None, None]).astype(jnp.bfloat16)
    swapped = inner.reshape(tile_count, NTV, a_local, TV, TV, TV).transpose(0, 1, 2, 4, 3, 5)
    swapped = swapped.reshape(tile_count, NTV * a_local * TV, PAIR)
    amp_columns = lax.all_gather(amps, "right", axis=3, tiled=True)
    d_first = first_tile % NTV
    own_amps = lax.dynamic_slice_in_dim(amp_columns[0], d_first, tile_count, 0)
    partial_sum = jnp.einsum(
        "trk,tkn->rn",
        swapped,
        lax.all_gather(own_amps, "occ", axis=1, tiled=True),
        preferred_element_type=jnp.float32,
    )
    partial_sum = partial_sum.reshape(NTV, row_count, NOP)
    owned_a = lax.psum_scatter(partial_sum, "left", scatter_dimension=0, tiled=True)
    b_tile = first_tile // NTV
    placed = lax.dynamic_update_slice_in_dim(
        jnp.zeros((NTV, row_count, NOP), jnp.float32), owned_a, b_tile, 0
    )
    summed = lax.psum_scatter(placed, "right", scatter_dimension=2, tiled=True)
    return summed.reshape(1, NTV, row_count, summed.shape[2])


def solution(mesh):
    placed = (P("right", "occ", "left"), P("left", None, "occ", "right"), P())
    return jax.shard_map(
        functools.partial(on_device, tuple(mesh.shape[axis] for axis in ("left", "right", "occ"))),
        mesh=mesh,
        in_specs=placed,
        out_specs=P("left", None, "occ", "right"),
        check_vma=False,
    )
```

```python
import functools

import jax
import jax.numpy as jnp
from jax import lax
from jax.experimental import pallas as pl
from jax.experimental.pallas import tpu as pltpu
from jax.sharding import PartitionSpec as P

TV = 32
NTV = 4
NOP = 512
PAIR = 1024
GROUPS = 4


def ladder_kernel(steps, count, tile_count, first, half_ref, live_ref, pick_ref, tile_ref, *refs):
    kinds = NTV + 1
    lefts = [refs[s * kinds:(s + 1) * kinds] for s in range(steps)]
    rest = refs[steps * kinds:]
    whole, rest = rest[:2], rest[2:]
    tiles = [rest[2 * n:2 * n + 2] for n in range((steps - 1) * tile_count)]
    rest = rest[2 * (steps - 1) * tile_count:]
    amp_ref = rest[0]
    before_ref = None if first else rest[1]
    out_ref, total_ref, products, ready, left_buf, right_buf, left_sem, right_sem = rest[-8:]
    d_tile, step = pl.program_id(0), pl.program_id(1)
    rows = left_buf.shape[0] // count
    depth = left_buf.shape[1] // steps
    group_rows = rows // GROUPS
    c_part = TV // GROUPS
    a_count = group_rows // c_part
    wide = 2 * GROUPS * TV
    half_blocks = rows // wide
    block_rows = TV // GROUPS * a_count
    slot = d_tile % 2

    def right_copies(i):
        copies = []
        for s in range(steps):
            for side in range(2):
                source = whole[side].at[tile_ref[i]] if s == 0 else tiles[(s - 1) * tile_count + i][side].at[0]
                target = right_buf.at[i % 2, side, :, pl.ds(s * depth, depth)]
                copies.append(pltpu.make_async_copy(source, target, right_sem.at[i % 2, s, side]))
        return copies

    def left_place(t, s, first, size):
        return left_buf.at[pl.ds(t * rows + first, size), pl.ds(s * depth, depth)]

    @pl.when((d_tile == 0) & (step == 0))
    def _():
        for t in range(count):
            for s in range(steps):
                for k in range(NTV - 1):

                    @pl.when(pick_ref[t] == k)
                    def _():
                        pltpu.make_async_copy(lefts[s][k], left_place(t, s, 0, rows), left_sem.at[t, s]).start()

                @pl.when(pick_ref[t] == NTV - 1)
                def _():
                    for part in range(2):
                        target = left_place(t, s, part * (rows // 2), rows // 2)
                        pltpu.make_async_copy(lefts[s][NTV - 1 + part], target, left_sem.at[t, s]).start()
        for copy in right_copies(0):
            copy.start()
        for t in range(count):
            for s in range(steps):
                pltpu.make_async_copy(lefts[s][0], left_place(t, s, 0, rows), left_sem.at[t, s]).wait()

    for i in range(tile_count):

        @pl.when((d_tile == i) & (step == 0))
        def _():
            for copy in right_copies(i):
                copy.wait()
            if i + 1 < tile_count:
                for copy in right_copies(i + 1):
                    copy.start()

    @pl.when(step < GROUPS)
    def _():
        left = jnp.concatenate(
            [
                left_buf[pl.ds(pl.multiple_of(t * rows + step * group_rows, group_rows), group_rows), :]
                for t in range(count)
            ],
            axis=0,
        )
        for half in range(2):
            start = (half_ref[0] if half == 0 else 1 - half_ref[0]) * half_blocks
            for p in range(half_blocks):
                right = jnp.concatenate(
                    [
                        right_buf[
                            slot,
                            half,
                            pl.ds(
                                pl.multiple_of(
                                    p * wide + (g // GROUPS * GROUPS + (g + step) % GROUPS) * TV, TV
                                ),
                                TV,
                            ),
                            :,
                        ]
                        for g in range(2 * GROUPS)
                    ],
                    axis=0,
                )
                products[step, start + p] = lax.dot_general(
                    left, right, (((1,), (1,)), ((), ())), preferred_element_type=jnp.float32
                ).astype(jnp.bfloat16)

    @pl.when(step >= GROUPS)
    def _():
        k = step - GROUPS
        lane_group = lax.broadcasted_iota(jnp.int32, (a_count, wide), 1) // TV % GROUPS
        masks = [lane_group == g for g in range(GROUPS)]
        lanes = GROUPS * TV
        for p in range(2 * half_blocks):
            for t in range(count):
                for c in range(c_part):
                    place = pl.ds(t * group_rows + c * a_count, a_count)
                    mixed = products[k, p, place, :]
                    for g in range(1, GROUPS):
                        mixed = jnp.where(masks[g], products[(k + GROUPS - g) % GROUPS, p, place, :], mixed)
                    for b in range(2):
                        ready[t, 2 * p + b, :, c * lanes:(c + 1) * lanes] = mixed[:, b * lanes:(b + 1) * lanes]
        amp = jnp.concatenate(
            [
                amp_ref[0, pl.ds(pl.multiple_of(((k + GROUPS - g) % GROUPS * c_part + c) * TV, TV), TV), :]
                for c in range(c_part)
                for g in range(GROUPS)
            ],
            axis=0,
        )
        terms = jnp.dot(
            ready[...].reshape(count * block_rows, TV * TV), amp, preferred_element_type=jnp.float32
        ).reshape(count, block_rows, amp.shape[1])
        for t in range(count):
            term = terms[t] * live_ref[d_tile, t].astype(jnp.float32)

            @pl.when(d_tile == 0)
            def _():
                total_ref[t, k] = term if first else before_ref[t, k] + term

            @pl.when((d_tile > 0) & (d_tile < tile_count - 1))
            def _():
                total_ref[t, k] += term

            @pl.when(d_tile == tile_count - 1)
            def _():
                out_ref[t, k] = (total_ref[t, k] + term).astype(out_ref.dtype)


def ladder(half, live, pick, tile, lefts, whole, tiles, amp, before, part, kind):
    steps = len(lefts)
    rows, depth = whole[0].shape[1:]
    columns = amp.shape[2]
    a_count = rows // TV
    b_blocks = TV // GROUPS
    wide = 2 * GROUPS * TV
    tile_count = live.shape[0]
    first = before is None
    count = NTV if first else NTV // 2
    base = part * count
    result = (count, GROUPS, b_blocks * a_count, columns)
    flops = 2 * tile_count * count * rows * 2 * rows * (steps * depth + columns)
    anywhere = pl.BlockSpec(memory_space=pl.ANY)
    copied = [x for step in lefts for x in step] + [*whole] + [x for pair in tiles for x in pair]
    return pl.pallas_call(
        functools.partial(ladder_kernel, steps, count, tile_count, first),
        grid_spec=pltpu.PrefetchScalarGridSpec(
            num_scalar_prefetch=4,
            grid=(tile_count, 2 * GROUPS),
            in_specs=[anywhere] * len(copied)
            + [pl.BlockSpec((1, 2 * rows, columns), lambda i, j, h, v, k, d: (d[i], 0, 0))]
            + [
                pl.BlockSpec(result, lambda i, j, h, v, k, d: (part, 0, 0, 0), pipeline_mode=pl.Buffered(1))
            ]
            * (not first),
            out_specs=pl.BlockSpec(result, lambda i, j, h, v, k, d: (0, 0, 0, 0)),
            scratch_shapes=[
                pltpu.VMEM(result, jnp.float32),
                pltpu.VMEM((GROUPS, 2 * rows // wide, count * rows // GROUPS, wide), jnp.bfloat16),
                pltpu.VMEM((count, b_blocks, a_count, TV * TV), jnp.bfloat16),
                pltpu.VMEM((count * rows, steps * depth), jnp.bfloat16),
                pltpu.VMEM((2, 2, rows, steps * depth), jnp.bfloat16),
                pltpu.SemaphoreType.DMA((count, steps)),
                pltpu.SemaphoreType.DMA((2, steps, 2)),
            ],
        ),
        out_shape=jax.ShapeDtypeStruct(result, kind),
        compiler_params=pltpu.CompilerParams(vmem_limit_bytes=60 * 2**20),
        cost_estimate=pl.CostEstimate(flops=flops, bytes_accessed=28 * 2**20, transcendentals=0),
    )(half, live[:, base:base + count], pick[base:base + count], tile, *copied, amp, *([] if first else [before]))


def partner(value, axis, size, flip):
    return lax.ppermute(value, axis, [(i, i ^ flip) for i in range(size)])


def shift(value, axis, size, step):
    return lax.ppermute(value, axis, [(i, (i + step) % size) for i in range(size)])


def ring_order(size):
    return list(range(0, size, 2)) + list(range(size - 1, 0, -2))


HOPS = (
    (1, 2), (1, 1), (1, 0), (2, 1), (2, 0), (3, 0),
    (1, 3), (2, 3), (2, 2), (3, 2), (3, 1), (3, 3),
)
AMP = "amp"
NEAR = {0: 0, 2: AMP, 4: 1, 6: 2, 8: 3}
FAR = {1: 0, 3: AMP, 5: 1, 7: 2, 9: 3}
FAR_DONE = {2: 0, 4: AMP, 6: 1, 8: 2, 10: 3}


def on_square(chol, amps, listed):
    row_count, depth = chol.shape[1:]
    columns = amps.shape[3]
    a_count = row_count // TV
    left_index = lax.axis_index("left")
    right_index = lax.axis_index("right")
    occ_index = lax.axis_index("occ")
    order = ring_order(NTV)
    ring = [(order[p], order[(p + 1) % NTV]) for p in range(NTV)]
    near = [[order[(order.index(level) + i) % NTV] for level in range(NTV)] for i in range(NTV)]

    def at_level(table):
        value = jnp.int32(table[0])
        for level in range(1, NTV):
            value = jnp.where(left_index == level, jnp.int32(table[level]), value)
        return value

    d_tiles = [at_level(table) for table in near]
    tiles = jnp.arange(NTV)
    away = [NTV // 2] + [i for i in range(1, NTV) if i != NTV // 2] + [0]
    targets = jnp.stack([d_tiles[i] for i in away])

    def around(value, step):
        return lax.ppermute(value, "left", [(order[p], order[(p + step) % NTV]) for p in range(NTV)])

    pick = (targets ^ right_index).astype(jnp.int32)
    own_c = lax.dynamic_index_in_dim(listed, left_index, 1, keepdims=False)
    live = lax.dynamic_index_in_dim(own_c, right_index, 1, keepdims=False)[targets]
    half = occ_index.reshape(1)

    held = {("block", 0, i): lax.dynamic_slice_in_dim(chol, d_tiles[i], 1, 0) for i in (3, 2, 0, 1)}
    held["chol"] = chol
    held["left", AMP, 0] = amps[0]
    last = len(HOPS)
    waiting = {slot: [] for slot in range(last + 4)}

    def meet(keys):
        keys = list(dict.fromkeys(keys))
        for key, value in zip(keys, lax.optimization_barrier([held[key] for key in keys])):
            held[key] = value

    def contract(chosen, before, part, kind):
        d_order = jnp.stack([d_tiles[i] for i in chosen])
        return ladder(
            half,
            live[:, d_order].T,
            pick,
            d_order,
            [[held["left", s, piece] for piece in (0, 1, 2, "first", "second")] for s in range(NTV)],
            (held["chol"], held["other", "chol"]),
            [(held["block", s, i], held["other", s, i]) for s in range(1, NTV) for i in chosen],
            held["amp"],
            before,
            part,
            kind,
        )

    for slot in range(last + 1):
        hops = [0, 1] if slot == 0 else [slot + 1] if slot + 1 < last else []
        near_block, far_block, done_block = NEAR.get(slot), FAR.get(slot), FAR_DONE.get(slot)
        now = waiting[slot]
        if slot >= 1:
            now.append(("block", *HOPS[slot - 1]))
        if near_block is not None:
            if near_block != AMP:
                own = held["block", near_block, 0].reshape(a_count, TV, depth)
                held["left", near_block, 0] = own.transpose(1, 0, 2).reshape(row_count, depth)
            now.append(("left", near_block, 0))
        if far_block is not None:
            now += [("left", far_block, flip) for flip in range(3)]
        if done_block is not None:
            now += [("left", done_block, "first"), ("left", done_block, "second")]
        now += [("block", HOPS[u][0] - 1, (HOPS[u][1] + 1) % NTV) for u in hops]
        if slot == 1:
            now.append("chol")
        meet(now)
        for u in hops:
            s, i = HOPS[u]
            held["block", s, i] = lax.ppermute(held["block", s - 1, (i + 1) % NTV], "left", ring)
        if near_block is not None:
            for flip in (1, 2):
                held["left", near_block, flip] = partner(held["left", near_block, 0], "right", NTV, flip)
        if far_block is not None:
            middle = held["left", far_block, 0].shape[0] // 2
            held["left", far_block, "first"] = partner(held["left", far_block, 1][:middle], "right", NTV, 2)
            held["left", far_block, "second"] = partner(held["left", far_block, 2][middle:], "right", NTV, 1)
        if slot == 1:
            held["other", "chol"] = partner(held["chol"], "occ", 2, 1)
            waiting[slot + 1].append(("other", "chol"))
        late_hop = near_block is not None
        for u in [] if slot == 0 or late_hop else [slot - 2, slot - 1] if slot - 1 in NEAR and slot > 1 else [slot - 1]:
            unit = HOPS[u]
            held["other", *unit] = partner(held["block", *unit], "occ", 2, 1)
            waiting[slot + 1].append(("other", *unit))
        if done_block == AMP:
            far = jnp.concatenate([held["left", AMP, "first"], held["left", AMP, "second"]])
            every = [held["left", AMP, flip] for flip in range(3)] + [far]
            held["amp"] = lax.all_gather(jnp.concatenate(every, axis=2), "occ", axis=1, tiled=True)
            waiting[slot + 3].append("amp")
        if slot == last - 1:
            held["sum"] = contract((0, 2), None, 0, jnp.float32)
            waiting[slot + 1].append("sum")
    early = contract((1, 3), held["sum"], 0, jnp.bfloat16)
    moved = [around(early[t], away[t]) for t in range(NTV // 2)]
    late = contract((1, 3), held["sum"], 1, jnp.float32)
    moved += [around(late[t].astype(jnp.bfloat16), away[NTV // 2 + t]) for t in range(NTV // 2 - 1)]
    summed = late[NTV // 2 - 1]
    for piece in moved:
        summed = summed + piece.astype(jnp.float32)
    pieces = []
    for flip in range(NTV):
        piece = summed[:, :, flip * columns:(flip + 1) * columns]
        if flip:
            piece = partner(piece.astype(jnp.bfloat16), "right", NTV, flip).astype(jnp.float32)
        pieces.append(piece)
    result = jnp.stack(pieces)[tiles ^ right_index]
    result = result.reshape(NTV, GROUPS, TV // GROUPS, a_count, columns).transpose(0, 3, 2, 1, 4)
    return result.reshape(1, NTV, row_count, columns)


def broadcast(value, axis, source):
    kept = jnp.where(lax.axis_index(axis) == source, value, 0).astype(value.dtype)
    return lax.psum(kept, axis)


def on_device(sizes, chol, amps, listed):
    tile_count = chol.shape[0]
    if sizes == (NTV, NTV, 2) and tile_count == NTV:
        return on_square(chol, amps, listed)
    row_count = chol.shape[1]
    a_local = row_count // TV
    left_index = lax.axis_index("left")
    right_index = lax.axis_index("right")
    first_tile = right_index * tile_count
    full_vectors = lax.all_gather(chol, "left", axis=2, tiled=True)
    collected = []
    for a_tile in range(NTV):
        wanted = a_tile * NTV + left_index
        holder = wanted // tile_count
        holder_slot = wanted % tile_count
        offered = lax.dynamic_index_in_dim(full_vectors, holder_slot, 0, keepdims=False)
        collected.append(broadcast(offered, "right", holder))
    left_rows = jnp.stack(collected)
    own_c = lax.dynamic_index_in_dim(listed, left_index, 1, keepdims=False).reshape(NTV, NTV * NTV)
    live = lax.dynamic_slice_in_dim(own_c, first_tile, tile_count, 1).T.astype(jnp.float32)
    products = jnp.einsum(
        "xrq,tkq->txrk",
        left_rows,
        lax.all_gather(full_vectors, "occ", axis=1, tiled=True),
        preferred_element_type=jnp.float32,
    )
    inner = (products * live[:, :, None, None]).astype(jnp.bfloat16)
    swapped = inner.reshape(tile_count, NTV, a_local, TV, TV, TV).transpose(0, 1, 2, 4, 3, 5)
    swapped = swapped.reshape(tile_count, NTV * a_local * TV, PAIR)
    amp_columns = lax.all_gather(amps, "right", axis=3, tiled=True)
    d_first = first_tile % NTV
    own_amps = lax.dynamic_slice_in_dim(amp_columns[0], d_first, tile_count, 0)
    partial_sum = jnp.einsum(
        "trk,tkn->rn",
        swapped,
        lax.all_gather(own_amps, "occ", axis=1, tiled=True),
        preferred_element_type=jnp.float32,
    )
    partial_sum = partial_sum.reshape(NTV, row_count, NOP)
    owned_a = lax.psum_scatter(partial_sum, "left", scatter_dimension=0, tiled=True)
    b_tile = first_tile // NTV
    placed = lax.dynamic_update_slice_in_dim(
        jnp.zeros((NTV, row_count, NOP), jnp.float32), owned_a, b_tile, 0
    )
    summed = lax.psum_scatter(placed, "right", scatter_dimension=2, tiled=True)
    return summed.reshape(1, NTV, row_count, summed.shape[2])


def solution(mesh):
    placed = (P("right", "occ", "left"), P("left", None, "occ", "right"), P())
    return jax.shard_map(
        functools.partial(on_device, tuple(mesh.shape[axis] for axis in ("left", "right", "occ"))),
        mesh=mesh,
        in_specs=placed,
        out_specs=P("left", None, "occ", "right"),
        check_vma=False,
    )
```
